32 devices in a mesh: dp: 8 (over y, x, core), tensor: 4 (over z).
Axes of the slice: x: 2, y: 2, z: 4, core: 2. Of those that a mesh axis runs over, the one named last changes fastest.
Arguments:
- tokens: bfloat16 [16384, 768], P(('dp', 'tensor')), may hold values from -6 to 6
- token_ids: int32 [16384], P(('dp', 'tensor')), may hold values from 0 to 50256
- hash_table: int32 [50257], replicated, may hold values from 0 to 15
- ln1_gain: float32 [768], replicated, may hold values from 0.5 to 1.5
- ln1_bias: float32 [768], replicated, may hold values from -1 to 1
- w_qkv: float32 [768, 12, 192], P('dp', 'tensor'), may hold values from -0.21875 to 0.21875
- w_out: float32 [768, 768], P('tensor', 'dp'), may hold values from -1.25 to 1.25
- ln2_gain: float32 [768], replicated, may hold values from 0.5 to 1.5
- ln2_bias: float32 [768], replicated, may hold values from -1 to 1
- expert_in: float32 [16, 768, 3072], P('dp', None, 'tensor'), may hold values from -0.21875 to 0.21875
- expert_out: float32 [16, 3072, 768], P('dp', 'tensor'), may hold values from -0.109375 to 0.109375
- cotangent: bfloat16 [16384, 768], P(('dp', 'tensor')), may hold values from -6 to 6
Outputs:
- out: bfloat16 [16384, 768], P(('dp', 'tensor'))
- grad_tokens: bfloat16 [16384, 768], P(('dp', 'tensor'))
- grad_ln1_gain: float32 [768], replicated
- grad_ln1_bias: float32 [768], replicated
- grad_w_qkv: float32 [768, 12, 192], P('dp', 'tensor')
- grad_w_out: float32 [768, 768], P('tensor', 'dp')
- grad_ln2_gain: float32 [768], replicated
- grad_ln2_bias: float32 [768], replicated
- grad_expert_in: float32 [16, 768, 3072], P('dp', None, 'tensor')
- grad_expert_out: float32 [16, 3072, 768], P('dp', 'tensor')
The draws below stay inside these ranges and needn't reach their ends.
Inputs may be any that keep to these rules, and one draw needn't show every extreme that they name: hash_table gives each token id one expert.
All inputs are finite; a program needn't handle non-finite values.
Results may differ from the reference program's by a relative error of at most 0.018.
Values may be sent and summed in bfloat16 or wider, within the bound.
A program may use at most 192 MiB of HBM per device.

```python
import math
import jax
import jax.numpy as jnp
import numpy as np
from jax import lax

D = 768
HEADS = 12
HD = 64
FF = 3072
VOCAB = 50257
LEN = 1024
TOK_DEV = 512
TOKENS = 16384
EXPERTS = 16
CAP = 64


def with_ends(drawn, key, least, largest):
    longest = drawn.shape.index(max(drawn.shape))
    spots = []
    for shift in (0, 1):
        where = [jax.random.randint(jax.random.fold_in(key, axis), (), 0, length) for axis, length in enumerate(drawn.shape)]
        where[longest] = (where[longest] + shift) % drawn.shape[longest]
        spots.append(tuple(where))
    return drawn.at[spots[0]].set(least).at[spots[1]].set(largest)


def steps_of(own_key, extent, shards, smallest, largest):
    def one(position, blocks):
        steps = jax.random.uniform(jax.random.fold_in(jax.random.fold_in(own_key, 6), position), (blocks,), jnp.float32, smallest / len(shards), largest / len(shards))
        return jnp.repeat(jnp.exp(steps), extent[position] // blocks).reshape((-1,) + (1,) * (len(extent) - position - 1))

    gain = one(*shards[0])
    for cut in shards[1:]:
        gain = gain * one(*cut)
    return gain


def rank_bounds(amount, lean):
    weights = [(1 << 20) // math.isqrt(rank ** lean) + 1 for rank in range(1, amount + 1)]
    spread = 1 + sum(weights) // (1 << 30)
    return np.cumsum(np.array([max(1, weight // spread) for weight in weights]))


def ranked(key, extent, amount, slope):
    table = rank_bounds(amount, slope)
    ticket = jax.random.randint(jax.random.fold_in(key, 1), extent, 0, int(table[amount - 1]))
    rank = jnp.searchsorted(jnp.asarray(table, jnp.int32), ticket, side="right")
    return jax.random.permutation(jax.random.fold_in(key, 2), amount)[rank].astype(jnp.int32)


def centred(rng, dims, spread, limit, split=(), kind=jnp.bfloat16):
    drawn = spread * jax.random.normal(rng, dims, jnp.float32)
    if split:
        drawn = drawn * steps_of(rng, dims, split, -0.22, 0.18)
    return jnp.clip(drawn, -limit, limit).astype(kind)


def setup_inputs(seed: int = 0) -> dict:
    splits = jax.random.split(jax.random.key(seed), 13)
    tokens = centred(splits[0], (TOKENS, D), 1.0, 6.0, ((0, 32),))
    token_ids = with_ends(ranked(splits[1], (TOKENS,), VOCAB, 2), jax.random.fold_in(splits[1], 3), 0, VOCAB - 1).astype(jnp.int32)
    hash_table = with_ends(jax.random.randint(splits[2], (VOCAB,), 0, EXPERTS), jax.random.fold_in(splits[2], 1), 0, EXPERTS - 1).astype(jnp.int32)
    ln1_gain = jnp.clip(1.0 + 0.1 * jax.random.normal(splits[3], (D,), jnp.float32), 0.5, 1.5)
    ln1_bias = centred(splits[4], (D,), 0.2, 1.0, (), jnp.float32)
    w_qkv = centred(splits[5], (D, HEADS, 3 * HD), D ** -0.5, 0.21875, ((0, 8), (1, 4)), jnp.float32)
    w_out = centred(splits[6], (D, D), (D // 32) ** -0.5, 1.25, ((0, 4), (1, 8)), jnp.float32)
    ln2_gain = jnp.clip(1.0 + 0.1 * jax.random.normal(splits[7], (D,), jnp.float32), 0.5, 1.5)
    ln2_bias = centred(splits[8], (D,), 0.2, 1.0, (), jnp.float32)
    expert_in = centred(splits[9], (EXPERTS, D, FF), D ** -0.5, 0.21875, ((0, 8), (2, 4)), jnp.float32)
    expert_out = centred(splits[10], (EXPERTS, FF, D), FF ** -0.5, 0.109375, ((0, 8), (1, 4)), jnp.float32)
    cotangent = centred(splits[11], (TOKENS, D), 1.0, 6.0, ((0, 32),))
    return {"tokens": tokens, "token_ids": token_ids, "hash_table": hash_table, "ln1_gain": ln1_gain, "ln1_bias": ln1_bias, "w_qkv": w_qkv, "w_out": w_out, "ln2_gain": ln2_gain, "ln2_bias": ln2_bias, "expert_in": expert_in, "expert_out": expert_out, "cotangent": cotangent}


@jax.custom_vjp
def low(v):
    return lax.optimization_barrier(v.astype(jnp.bfloat16)).astype(jnp.float32)

@jax.custom_vjp
def low_back(v):
    return v

def low_keep(v):
    return (low(v), None)

def low_pass(kept, grad):
    return (grad,)

def back_keep(v):
    return (v, None)

def back_low(kept, grad):
    return (low(grad),)
low.defvjp(low_keep, low_pass)
low_back.defvjp(back_keep, back_low)
FULL_PRECISION = lax.Precision.HIGHEST
EPSILON = 1e-05

def normalize(values, norm_gain, norm_shift):
    center = lax.optimization_barrier(jnp.mean(values, axis=-1, keepdims=True))
    centered = values - center
    inv_scale = lax.rsqrt(lax.optimization_barrier(jnp.mean(centered * centered, axis=-1, keepdims=True)) + EPSILON)
    return centered * inv_scale * norm_gain + norm_shift

def attend(seq_block):
    query_rows = seq_block[:, :, 0]
    key_rows = seq_block[:, :, 1]
    value_rows = seq_block[:, :, 2]
    scores = jnp.einsum('qhd,khd->hqk', query_rows, key_rows, precision=FULL_PRECISION) * 0.125
    scores = low_back(scores)
    positions = jnp.arange(LEN, dtype=jnp.int32)
    causal = positions[:, None] >= positions[None, :]
    scores = jnp.where(causal[None], scores, -1e+30)
    row_max = lax.optimization_barrier(jnp.max(scores, axis=-1, keepdims=True))
    exp_scores = jnp.exp(scores - row_max)
    probabilities = exp_scores / lax.optimization_barrier(jnp.sum(exp_scores, axis=-1, keepdims=True))
    return jnp.einsum('hqk,khd->qhd', low(probabilities), value_rows, precision=FULL_PRECISION)

def expert(inputs):
    buffer, weight_in, weight_out = inputs
    hidden = low_back(jnp.dot(buffer, weight_in, precision=FULL_PRECISION))
    activated = low(jax.nn.gelu(hidden, approximate=True))
    return low_back(low(jnp.dot(activated, weight_out, precision=FULL_PRECISION)))

def reference(tokens, token_ids, hash_table, ln1_gain, ln1_bias, w_qkv, w_out, ln2_gain, ln2_bias, expert_in, expert_out, cotangent):
    block_count = TOKENS // TOK_DEV
    slot_total = EXPERTS * block_count * CAP
    expert_of = jnp.take(hash_table, token_ids).astype(jnp.int32)
    one_hot = (expert_of[:, None] == jnp.arange(EXPERTS, dtype=jnp.int32)[None, :]).astype(jnp.int32)
    one_hot = one_hot.reshape(block_count, TOK_DEV, EXPERTS)
    running = jnp.cumsum(one_hot, axis=1).astype(jnp.int32)
    slot_rank = lax.optimization_barrier(jnp.sum((running - 1) * one_hot, axis=2)).astype(jnp.int32).reshape(TOKENS)
    kept_rows = slot_rank < CAP
    block_of = (jnp.arange(TOKENS, dtype=jnp.int32) // TOK_DEV).astype(jnp.int32)
    target = jnp.where(kept_rows, (expert_of * block_count + block_of) * CAP + slot_rank, slot_total).astype(jnp.int32)
    source_row = jnp.minimum(target, slot_total - 1).astype(jnp.int32)

    def forward(residual, gain_one, bias_one, qkv_weight, out_weight, gain_two, bias_two, weight_in, weight_out):
        first_norm = low(normalize(residual, gain_one, bias_one))
        projected = jnp.dot(first_norm, low(qkv_weight).reshape(D, HEADS * 3 * HD), precision=FULL_PRECISION)
        projected = low_back(low(projected)).reshape(TOKENS // LEN, LEN, HEADS, 3, HD)
        mixed_heads = lax.map(jax.checkpoint(attend), projected).reshape(TOKENS, D)
        mixed_heads = low_back(low(mixed_heads))
        middle = residual + low_back(jnp.dot(mixed_heads, low(out_weight), precision=FULL_PRECISION))
        second_norm = low_back(low(normalize(middle, gain_two, bias_two)))
        buffer = jnp.zeros((slot_total, D), jnp.float32).at[target].set(second_norm, mode='drop')
        buffer = buffer.reshape(EXPERTS, block_count * CAP, D)
        results = lax.map(jax.checkpoint(expert), (buffer, low(weight_in), low(weight_out)))
        results = results.reshape(slot_total, D)
        picked = jnp.take(results, source_row, axis=0)
        return middle + jnp.where(kept_rows[:, None], picked, 0.0)
    residual = tokens.astype(jnp.float32)
    output, pull = jax.vjp(forward, residual, ln1_gain, ln1_bias, w_qkv, w_out, ln2_gain, ln2_bias, expert_in, expert_out)
    grads = pull(cotangent.astype(jnp.float32))
    return (output.astype(jnp.bfloat16), grads[0].astype(jnp.bfloat16), grads[1], grads[2], grads[3], grads[4], grads[5], grads[6], grads[7], grads[8])
```

```python
import jax
import jax.numpy as jnp
from jax import lax
from jax.sharding import PartitionSpec as P

LEN = 1024


EPSILON = 1e-05
SCORE_SCALE = 0.125
MASKED = -1e30


def normalize(values, norm_gain, norm_shift):
    center = jnp.mean(values, axis=-1, keepdims=True)
    centered = values - center
    inv_scale = lax.rsqrt(jnp.mean(centered * centered, axis=-1, keepdims=True) + EPSILON)
    unit_rows = centered * inv_scale
    return (unit_rows * norm_gain + norm_shift, unit_rows, inv_scale)


def norm_back(grad_rows, unit_rows, inv_scale, norm_gain):
    scaled = grad_rows * norm_gain
    mean_plain = jnp.mean(scaled, axis=-1, keepdims=True)
    mean_unit = jnp.mean(scaled * unit_rows, axis=-1, keepdims=True)
    return inv_scale * (scaled - mean_plain - unit_rows * mean_unit)


def smooth(values):
    return jax.nn.gelu(values, approximate=True)


def causal_scores(query_rows, key_rows):
    length = query_rows.shape[0]
    scores = (
        jnp.einsum("qhd,khd->hqk", query_rows, key_rows, preferred_element_type=jnp.float32)
        * SCORE_SCALE
    )
    causal = lax.broadcasted_iota(jnp.int32, (length, length), 0) >= lax.broadcasted_iota(
        jnp.int32, (length, length), 1
    )
    return jnp.where(causal[None], scores, MASKED)


def attend(seq_block):
    scores = causal_scores(seq_block[:, :, 0], seq_block[:, :, 1])
    row_max = jnp.max(scores, axis=-1, keepdims=True)
    exp_scores = jnp.exp(scores - row_max)
    denominator = jnp.sum(exp_scores, axis=-1, keepdims=True)
    probabilities = (exp_scores / denominator).astype(jnp.bfloat16)
    mixed_heads = jnp.einsum(
        "hqk,khd->qhd", probabilities, seq_block[:, :, 2], preferred_element_type=jnp.float32
    )
    return (mixed_heads.astype(jnp.bfloat16), (row_max + jnp.log(denominator))[:, :, 0])


def attend_back(inputs):
    seq_block, mixed_grad, log_total = inputs
    query_rows = seq_block[:, :, 0]
    key_rows = seq_block[:, :, 1]
    value_rows = seq_block[:, :, 2]
    probabilities = jnp.exp(causal_scores(query_rows, key_rows) - log_total[:, :, None])
    prob_grad = jnp.einsum(
        "qhd,khd->hqk", mixed_grad, value_rows, preferred_element_type=jnp.float32
    )
    row_inner = jnp.sum(probabilities * prob_grad, axis=-1, keepdims=True)
    score_grad = (probabilities * (prob_grad - row_inner)).astype(jnp.bfloat16)
    value_grad = jnp.einsum(
        "hqk,qhd->khd",
        probabilities.astype(jnp.bfloat16),
        mixed_grad,
        preferred_element_type=jnp.float32,
    )
    query_grad = (
        jnp.einsum("hqk,khd->qhd", score_grad, key_rows, preferred_element_type=jnp.float32)
        * SCORE_SCALE
    )
    key_grad = (
        jnp.einsum("hqk,qhd->khd", score_grad, query_rows, preferred_element_type=jnp.float32)
        * SCORE_SCALE
    )
    return jnp.stack([query_grad, key_grad, value_grad], axis=2).astype(jnp.bfloat16)


def expert_back(shaped, hidden, activated, grad_rows, weight_out):
    act_grad = jnp.einsum(
        "secd,efd->secf", grad_rows, weight_out, preferred_element_type=jnp.float32
    )
    out_wgrad = jnp.einsum(
        "secf,secd->efd", activated, grad_rows, preferred_element_type=jnp.float32
    )
    unused, pull = jax.vjp(smooth, hidden)
    hidden_grad = pull(act_grad)[0].astype(jnp.bfloat16)
    in_wgrad = jnp.einsum("secd,secf->edf", shaped, hidden_grad, preferred_element_type=jnp.float32)
    return (hidden_grad, in_wgrad, out_wgrad)


def on_device(
    tokens,
    token_ids,
    hash_table,
    ln1_gain,
    ln1_bias,
    w_qkv,
    w_out,
    ln2_gain,
    ln2_bias,
    expert_in,
    expert_out,
    cotangent,
):
    row_count = tokens.shape[0]
    model_width = tokens.shape[1]
    local_experts = expert_in.shape[0]
    dp_count = lax.axis_size("dp")
    qkv_weight, out_weight = (
        lax.all_gather(w_qkv.astype(jnp.bfloat16), "dp", axis=0, tiled=True),
        lax.all_gather(w_out.astype(jnp.bfloat16), "dp", axis=1, tiled=True),
    )
    qkv_flat = qkv_weight.reshape(model_width, -1)
    heads_here = qkv_weight.shape[1]
    head_dim = qkv_weight.shape[2] // 3
    residual = tokens.astype(jnp.float32)
    first_norm, unit_one, scale_one = normalize(residual, ln1_gain, ln1_bias)
    first_all = lax.all_gather(first_norm.astype(jnp.bfloat16), "tensor", axis=0, tiled=True)
    group_rows = first_all.shape[0]
    projected = jnp.dot(first_all, qkv_flat, preferred_element_type=jnp.float32).astype(
        jnp.bfloat16
    )
    seq_blocks = projected.reshape(group_rows // LEN, LEN, heads_here, 3, head_dim)
    mixed_heads, log_total = lax.map(attend, seq_blocks)
    mixed_flat = mixed_heads.reshape(group_rows, heads_here * head_dim)
    attention = lax.psum_scatter(
        jnp.dot(mixed_flat, out_weight, preferred_element_type=jnp.float32).astype(jnp.bfloat16),
        "tensor",
        scatter_dimension=0,
        tiled=True,
    ).astype(jnp.float32)
    middle = residual + attention
    second_norm, unit_two, scale_two = normalize(middle, ln2_gain, ln2_bias)
    experts_total = dp_count * local_experts
    capacity = 2 * row_count // experts_total
    slot_count = experts_total * capacity
    expert_of = jnp.take(hash_table, token_ids)
    one_hot = (expert_of[:, None] == jnp.arange(experts_total, dtype=jnp.int32)[None, :]).astype(
        jnp.int32
    )
    before = (
        lax.broadcasted_iota(jnp.int32, (row_count, row_count), 0)
        > lax.broadcasted_iota(jnp.int32, (row_count, row_count), 1)
    ).astype(jnp.bfloat16)
    earlier = jnp.dot(before, one_hot.astype(jnp.bfloat16), preferred_element_type=jnp.float32)
    slot_rank = jnp.sum(earlier.astype(jnp.int32) * one_hot, axis=1)
    kept_rows = slot_rank < capacity
    target = jnp.where(kept_rows, expert_of * capacity + slot_rank, slot_count)
    source_row = jnp.minimum(target, slot_count - 1)

    def dispatch_rows(values):
        return (
            jnp.zeros((slot_count, model_width), jnp.bfloat16).at[target].set(values, mode="drop")
        )

    def collect_rows(values):
        return jnp.where(
            kept_rows[:, None], jnp.take(values, source_row, axis=0).astype(jnp.float32), 0.0
        )

    out_grad = cotangent.astype(jnp.float32)
    received = lax.all_to_all(
        dispatch_rows(second_norm.astype(jnp.bfloat16)),
        "dp",
        split_axis=0,
        concat_axis=0,
        tiled=True,
    )
    grad_sent = lax.all_to_all(
        dispatch_rows(cotangent), "dp", split_axis=0, concat_axis=0, tiled=True
    )
    weight_in, weight_out = (
        lax.all_gather(expert_in.astype(jnp.bfloat16), "tensor", axis=2, tiled=True),
        lax.all_gather(expert_out.astype(jnp.bfloat16), "tensor", axis=1, tiled=True),
    )
    shaped = received.reshape(dp_count, local_experts, capacity, model_width)
    hidden = jnp.einsum("secd,edf->secf", shaped, weight_in, preferred_element_type=jnp.float32)
    activated = smooth(hidden).astype(jnp.bfloat16)
    expert_result = jnp.einsum(
        "secf,efd->secd", activated, weight_out, preferred_element_type=jnp.float32
    )
    expert_result = expert_result.astype(jnp.bfloat16).reshape(slot_count, model_width)
    grad_rows = grad_sent.reshape(dp_count, local_experts, capacity, model_width)
    hidden_grad, in_wgrad, out_wgrad = expert_back(shaped, hidden, activated, grad_rows, weight_out)
    row_grad = jnp.einsum(
        "secf,edf->secd", hidden_grad, weight_in, preferred_element_type=jnp.float32
    )
    row_grad = row_grad.astype(jnp.bfloat16).reshape(slot_count, model_width)
    grad_expert_in, grad_expert_out = (
        lax.psum_scatter(
            in_wgrad.astype(jnp.bfloat16), "tensor", scatter_dimension=2, tiled=True
        ).astype(jnp.float32),
        lax.psum_scatter(
            out_wgrad.astype(jnp.bfloat16), "tensor", scatter_dimension=1, tiled=True
        ).astype(jnp.float32),
    )
    returned = lax.all_to_all(expert_result, "dp", split_axis=0, concat_axis=0, tiled=True)
    mixed_out = middle + collect_rows(returned)
    row_back = lax.all_to_all(row_grad, "dp", split_axis=0, concat_axis=0, tiled=True)
    second_grad = collect_rows(row_back)
    gain_two_grad = jnp.sum(second_grad * unit_two, axis=0)
    bias_two_grad = jnp.sum(second_grad, axis=0)
    middle_grad = out_grad + norm_back(second_grad, unit_two, scale_two, ln2_gain)
    middle_all = lax.all_gather(middle_grad.astype(jnp.bfloat16), "tensor", axis=0, tiled=True)
    out_wgrad_local = jnp.einsum(
        "tk,td->kd", mixed_flat, middle_all, preferred_element_type=jnp.float32
    )
    mixed_grad = jnp.einsum(
        "td,kd->tk", middle_all, out_weight, preferred_element_type=jnp.float32
    ).astype(jnp.bfloat16)
    mixed_grad = mixed_grad.reshape(group_rows // LEN, LEN, heads_here, head_dim)
    qkv_grad = lax.map(attend_back, (seq_blocks, mixed_grad, log_total)).reshape(group_rows, -1)
    qkv_wgrad = jnp.einsum(
        "td,tk->dk", first_all, qkv_grad, preferred_element_type=jnp.float32
    ).reshape(qkv_weight.shape)
    first_grad = lax.psum_scatter(
        jnp.einsum("tk,dk->td", qkv_grad, qkv_flat, preferred_element_type=jnp.float32).astype(
            jnp.bfloat16
        ),
        "tensor",
        scatter_dimension=0,
        tiled=True,
    ).astype(jnp.float32)
    gain_one_grad = jnp.sum(first_grad * unit_one, axis=0)
    bias_one_grad = jnp.sum(first_grad, axis=0)
    input_grad = middle_grad + norm_back(first_grad, unit_one, scale_one, ln1_gain)
    qkv_total, out_total = (
        lax.psum_scatter(
            qkv_wgrad.astype(jnp.bfloat16), "dp", scatter_dimension=0, tiled=True
        ).astype(jnp.float32),
        lax.psum_scatter(
            out_wgrad_local.astype(jnp.bfloat16), "dp", scatter_dimension=1, tiled=True
        ).astype(jnp.float32),
    )
    norm_sums = lax.psum(
        (gain_one_grad, bias_one_grad, gain_two_grad, bias_two_grad), ("dp", "tensor")
    )
    return (
        mixed_out.astype(jnp.bfloat16),
        input_grad.astype(jnp.bfloat16),
        norm_sums[0],
        norm_sums[1],
        qkv_total,
        out_total,
        norm_sums[2],
        norm_sums[3],
        grad_expert_in,
        grad_expert_out,
    )


def solution(mesh):
    placed = (
        P(("dp", "tensor"), None),
        P(("dp", "tensor")),
        P(),
        P(),
        P(),
        P("dp", "tensor", None),
        P("tensor", "dp"),
        P(),
        P(),
        P("dp", None, "tensor"),
        P("dp", "tensor", None),
        P(("dp", "tensor"), None),
    )
    return jax.shard_map(
        on_device,
        mesh=mesh,
        in_specs=placed,
        out_specs=(
            P(("dp", "tensor"), None),
            P(("dp", "tensor"), None),
            P(),
            P(),
            P("dp", "tensor", None),
            P("tensor", "dp"),
            P(),
            P(),
            P("dp", None, "tensor"),
            P("dp", "tensor", None),
        ),
        check_vma=False,
    )
```

```python
import jax
import jax.numpy as jnp
from jax import lax
from jax.sharding import PartitionSpec as P

LEN = 1024


EPSILON = 1e-05
SCORE_SCALE = 0.125
MASKED = -1e30


def normalize(values, norm_gain, norm_shift):
    center = jnp.mean(values, axis=-1, keepdims=True)
    centered = values - center
    inv_scale = lax.rsqrt(jnp.mean(centered * centered, axis=-1, keepdims=True) + EPSILON)
    unit_rows = centered * inv_scale
    return (unit_rows * norm_gain + norm_shift, unit_rows, inv_scale)


def norm_back(grad_rows, unit_rows, inv_scale, norm_gain):
    scaled = grad_rows * norm_gain
    mean_plain = jnp.mean(scaled, axis=-1, keepdims=True)
    mean_unit = jnp.mean(scaled * unit_rows, axis=-1, keepdims=True)
    return inv_scale * (scaled - mean_plain - unit_rows * mean_unit)


def smooth(values):
    return jax.nn.gelu(values, approximate=True)


def causal_scores(query_rows, key_rows):
    length = query_rows.shape[0]
    scores = (
        jnp.einsum("qhd,khd->hqk", query_rows, key_rows, preferred_element_type=jnp.float32)
        * SCORE_SCALE
    )
    causal = lax.broadcasted_iota(jnp.int32, (length, length), 0) >= lax.broadcasted_iota(
        jnp.int32, (length, length), 1
    )
    return jnp.where(causal[None], scores, MASKED)


def attend(seq_block):
    scores = causal_scores(seq_block[:, :, 0], seq_block[:, :, 1])
    row_max = jnp.max(scores, axis=-1, keepdims=True)
    exp_scores = jnp.exp(scores - row_max)
    denominator = jnp.sum(exp_scores, axis=-1, keepdims=True)
    probabilities = (exp_scores / denominator).astype(jnp.bfloat16)
    mixed_heads = jnp.einsum(
        "hqk,khd->qhd", probabilities, seq_block[:, :, 2], preferred_element_type=jnp.float32
    )
    return (mixed_heads.astype(jnp.bfloat16), (row_max + jnp.log(denominator))[:, :, 0])


def attend_back(seq_block, mixed_grad, log_total):
    query_rows = seq_block[:, :, 0]
    key_rows = seq_block[:, :, 1]
    value_rows = seq_block[:, :, 2]
    probabilities = jnp.exp(causal_scores(query_rows, key_rows) - log_total[:, :, None])
    prob_grad = jnp.einsum(
        "qhd,khd->hqk", mixed_grad, value_rows, preferred_element_type=jnp.float32
    )
    row_inner = jnp.sum(probabilities * prob_grad, axis=-1, keepdims=True)
    score_grad = (probabilities * (prob_grad - row_inner)).astype(jnp.bfloat16)
    value_grad = jnp.einsum(
        "hqk,qhd->khd",
        probabilities.astype(jnp.bfloat16),
        mixed_grad,
        preferred_element_type=jnp.float32,
    )
    query_grad = (
        jnp.einsum("hqk,khd->qhd", score_grad, key_rows, preferred_element_type=jnp.float32)
        * SCORE_SCALE
    )
    key_grad = (
        jnp.einsum("hqk,qhd->khd", score_grad, query_rows, preferred_element_type=jnp.float32)
        * SCORE_SCALE
    )
    return jnp.stack([query_grad, key_grad, value_grad], axis=2).astype(jnp.bfloat16)


def product(spec, left, right):
    return jnp.einsum(spec, left, right, preferred_element_type=jnp.float32)


def on_device(
    tokens,
    token_ids,
    hash_table,
    ln1_gain,
    ln1_bias,
    w_qkv,
    w_out,
    ln2_gain,
    ln2_bias,
    expert_in,
    expert_out,
    cotangent,
):
    low = jnp.bfloat16
    row_count, model_width = tokens.shape
    local_experts = expert_in.shape[0]
    dp_count = lax.axis_size("dp")
    line = lax.axis_size("tensor")
    shares = LEN // row_count
    place = lax.axis_index("tensor")
    part = place % shares
    swap = [(t, t ^ 1) for t in range(line)]
    hop = [(t, t ^ 2) for t in range(line)]
    head_dim = w_qkv.shape[2] // 3
    heads_shard = w_qkv.shape[1]

    def swapped(values):
        return lax.ppermute(values, "tensor", swap)

    def joined(own, other):
        both = jnp.stack([own, other])
        return jnp.where(part == 0, both, both[::-1]).reshape((-1,) + own.shape[1:])

    def halves(both):
        pair = both.reshape((shares, -1) + both.shape[1:])
        return (
            lax.dynamic_index_in_dim(pair, part, 0, False),
            lax.dynamic_index_in_dim(pair, 1 - part, 0, False),
        )

    experts_total = dp_count * local_experts
    capacity = 2 * row_count // experts_total
    slot_count = experts_total * capacity
    expert_of = jnp.take(hash_table, token_ids)
    one_hot = (expert_of[:, None] == jnp.arange(experts_total, dtype=jnp.int32)[None, :]).astype(
        jnp.int32
    )
    before = (
        lax.broadcasted_iota(jnp.int32, (row_count, row_count), 0)
        > lax.broadcasted_iota(jnp.int32, (row_count, row_count), 1)
    ).astype(low)
    earlier = jnp.dot(before, one_hot.astype(low), preferred_element_type=jnp.float32)
    slot_rank = jnp.sum(earlier.astype(jnp.int32) * one_hot, axis=1)
    target = jnp.where(slot_rank < capacity, expert_of * capacity + slot_rank, slot_count)
    targets = lax.all_gather(target, "tensor", axis=0)
    route = (targets[:, None, :] == jnp.arange(slot_count, dtype=jnp.int32)[None, :, None]).astype(
        low
    )

    def dispatch(values):
        rows = lax.all_gather(values, "tensor", axis=0)
        slots = product("bsr,brd->bsd", route, rows).astype(low)
        slots = slots.reshape(line, dp_count, local_experts, capacity, model_width)
        slots = slots.transpose(1, 2, 0, 3, 4)
        slots = slots.reshape(dp_count, local_experts, line * capacity, model_width)
        return lax.all_to_all(slots, "dp", split_axis=0, concat_axis=0, tiled=True)

    def collect(values):
        back = lax.all_to_all(values, "dp", split_axis=0, concat_axis=0, tiled=True)
        back = back.reshape(dp_count, local_experts, line, capacity, model_width)
        back = back.transpose(2, 0, 1, 3, 4).reshape(line, slot_count, model_width)
        rows = product("bsr,bsd->brd", route, back).astype(low)
        rows = rows.reshape(line * row_count, model_width)
        return lax.psum_scatter(rows, "tensor", scatter_dimension=0, tiled=True).astype(
            jnp.float32
        )

    qkv_own = w_qkv.astype(low)
    qkv_pair = jnp.stack([qkv_own, lax.ppermute(qkv_own, "tensor", hop)], axis=1)
    qkv_flat = lax.all_gather(qkv_pair, "dp", axis=0, tiled=True).reshape(model_width, -1)
    out_rows = lax.all_gather(w_out.astype(low), "tensor", axis=0)
    out_weight = lax.all_gather(out_rows, "dp", axis=2, tiled=True)

    def picked(shards):
        own = lax.dynamic_index_in_dim(shards, place, 0, False)
        far = lax.dynamic_index_in_dim(shards, place ^ 2, 0, False)
        return jnp.concatenate([own, far])

    def picked_other(shards):
        own = lax.dynamic_index_in_dim(shards, place ^ 1, 0, False)
        far = lax.dynamic_index_in_dim(shards, place ^ 3, 0, False)
        return jnp.concatenate([own, far])

    out_mine = picked(out_weight)
    out_other = picked_other(out_weight)

    residual = tokens.astype(jnp.float32)
    first_norm, unit_one, scale_one = normalize(residual, ln1_gain, ln1_bias)
    first_low = first_norm.astype(low)
    first_all = joined(first_low, swapped(first_low))
    projected = jnp.dot(first_all, qkv_flat, preferred_element_type=jnp.float32).astype(low)
    heads_here = 2 * heads_shard
    seq_block = projected.reshape(LEN, heads_here, 3, head_dim)
    mixed_heads, log_total = attend(seq_block)
    mixed_own, mixed_sent = halves(mixed_heads.reshape(LEN, heads_here * head_dim))
    mixed_other = swapped(mixed_sent)
    attention = product("tk,kd->td", mixed_own, out_mine) + product(
        "tk,kd->td", mixed_other, out_other
    )
    middle = residual + attention
    second_norm, unit_two, scale_two = normalize(middle, ln2_gain, ln2_bias)

    out_grad = cotangent.astype(jnp.float32)
    grad_rows = dispatch(cotangent)
    shaped = dispatch(second_norm.astype(low))
    weight_in = expert_in.astype(low)
    weight_out = expert_out.astype(low)
    hidden = product("secd,edf->secf", shaped, weight_in)
    activated, pull = jax.vjp(smooth, hidden)
    activated = activated.astype(low)
    expert_result = product("secf,efd->secd", activated, weight_out).astype(low)
    act_grad = product("secd,efd->secf", grad_rows, weight_out)
    hidden_grad = pull(act_grad)[0].astype(low)
    row_grad = product("secf,edf->secd", hidden_grad, weight_in).astype(low)
    grad_expert_out = product("secf,secd->efd", activated, grad_rows)
    grad_expert_in = product("secd,secf->edf", shaped, hidden_grad)

    second_grad = collect(row_grad)
    mixed_out = middle + collect(expert_result)
    gain_two_grad = jnp.sum(second_grad * unit_two, axis=0)
    bias_two_grad = jnp.sum(second_grad, axis=0)
    middle_grad = out_grad + norm_back(second_grad, unit_two, scale_two, ln2_gain)
    middle_low = middle_grad.astype(low)
    grad_mine = product("td,kd->tk", middle_low, out_mine).astype(low)
    grad_sent = product("td,kd->tk", middle_low, out_other).astype(low)
    mixed_grad = joined(grad_mine, swapped(grad_sent)).reshape(LEN, heads_here, head_dim)
    wgrad_mine = product("tk,td->kd", mixed_own, middle_low).reshape(2, -1, model_width)
    wgrad_other = product("tk,td->kd", mixed_other, middle_low).reshape(2, -1, model_width)
    out_wgrad = jnp.stack([wgrad_mine[0], wgrad_other[0], wgrad_mine[1], wgrad_other[1]])
    out_part = lax.psum_scatter(out_wgrad.astype(low), "dp", scatter_dimension=2, tiled=True)
    out_total = out_part[0].astype(jnp.float32)
    for i in range(1, line):
        sent = lax.ppermute(out_part[i], "tensor", [(t, t ^ i) for t in range(line)])
        out_total = out_total + sent.astype(jnp.float32)

    qkv_grad = attend_back(seq_block, mixed_grad, log_total).reshape(LEN, -1)
    qkv_wgrad = product("td,tk->dk", first_all, qkv_grad).astype(low)
    qkv_part = lax.psum_scatter(qkv_wgrad, "dp", scatter_dimension=0, tiled=True)
    qkv_part = qkv_part.reshape((-1, 2) + w_qkv.shape[1:])
    qkv_total = qkv_part[:, 0].astype(jnp.float32) + lax.ppermute(
        qkv_part[:, 1], "tensor", hop
    ).astype(jnp.float32)
    first_own, first_sent = halves(product("tk,dk->td", qkv_grad, qkv_flat))
    first_grad = first_own + swapped(first_sent.astype(low)).astype(jnp.float32)
    gain_one_grad = jnp.sum(first_grad * unit_one, axis=0)
    bias_one_grad = jnp.sum(first_grad, axis=0)
    input_grad = middle_grad + norm_back(first_grad, unit_one, scale_one, ln1_gain)
    norm_sums = lax.psum(
        (gain_one_grad, bias_one_grad, gain_two_grad, bias_two_grad), ("dp", "tensor")
    )
    return (
        mixed_out.astype(low),
        input_grad.astype(low),
        norm_sums[0],
        norm_sums[1],
        qkv_total,
        out_total,
        norm_sums[2],
        norm_sums[3],
        grad_expert_in,
        grad_expert_out,
    )


def solution(mesh):
    rows = P(("dp", "tensor"), None)
    weights = (P("dp", "tensor", None), P("tensor", "dp"))
    experts = (P("dp", None, "tensor"), P("dp", "tensor", None))
    return jax.shard_map(
        on_device,
        mesh=mesh,
        in_specs=(rows, P(("dp", "tensor")), P(), P(), P(), *weights, P(), P(), *experts, rows),
        out_specs=(rows, rows, P(), P(), *weights, P(), P(), *experts),
        check_vma=False,
    )
```

```python
import functools

import jax
import jax.numpy as jnp
from jax import lax
from jax.experimental import pallas as pl
from jax.experimental.pallas import tpu as pltpu
from jax.sharding import PartitionSpec as P

LEN = 1024


EPSILON = 1e-05
SCORE_SCALE = 0.125
MASKED = -1e30
MESH = pl.DeviceIdType.MESH


def normalize(values, norm_gain, norm_shift):
    center = jnp.mean(values, axis=-1, keepdims=True)
    centered = values - center
    inv_scale = lax.rsqrt(jnp.mean(centered * centered, axis=-1, keepdims=True) + EPSILON)
    unit_rows = centered * inv_scale
    return (unit_rows * norm_gain + norm_shift, unit_rows, inv_scale)


def norm_back(grad_rows, unit_rows, inv_scale, norm_gain):
    scaled = grad_rows * norm_gain
    mean_plain = jnp.mean(scaled, axis=-1, keepdims=True)
    mean_unit = jnp.mean(scaled * unit_rows, axis=-1, keepdims=True)
    return inv_scale * (scaled - mean_plain - unit_rows * mean_unit)


def smooth(values):
    return jax.nn.gelu(values, approximate=True)


def lanes_of(values, mask):
    return jnp.where(mask, values, 0.0).astype(jnp.bfloat16)


def dot_rows(left, right):
    return lax.dot_general(left, right, (((1,), (1,)), ((), ())), preferred_element_type=jnp.float32)


def dot_columns(left, right):
    return lax.dot_general(left, right, (((0,), (0,)), ((), ())), preferred_element_type=jnp.float32)


def dot_plain(left, right):
    return jnp.dot(left, right, preferred_element_type=jnp.float32)


def masked_scores(query, key, first):
    scores = dot_rows(query, key)
    rows, columns = scores.shape
    row = lax.broadcasted_iota(jnp.int32, (rows, rows), 0)
    column = lax.broadcasted_iota(jnp.int32, (rows, rows), 1)
    edge = jnp.where(row >= column, scores[:, first:], MASKED)
    return edge if first == 0 else jnp.concatenate([scores[:, :first], edge], axis=1)


def attend_back_kernel(head_dim, block, q_ref, k_ref, v_ref, log_ref, grad_ref, dq_ref, dk_sum, dv_sum):
    length, width = q_ref.shape
    lane = lax.broadcasted_iota(jnp.int32, (block, width), 1)
    for first in reversed(range(0, length, block)):
        rows = pl.ds(first, block)
        seen = pl.ds(0, first + block)
        lanes_seen = lax.broadcasted_iota(jnp.int32, (first + block, width), 1)
        wide_query = q_ref[rows, :].astype(jnp.float32) * SCORE_SCALE
        key, value, grad = k_ref[seen, :], v_ref[seen, :], grad_ref[rows, :]
        query, wide_grad = wide_query.astype(jnp.bfloat16), grad.astype(jnp.float32)
        dq = jnp.zeros((block, width), jnp.float32)
        dk = jnp.zeros((first + block, width), jnp.float32)
        dv = jnp.zeros((first + block, width), jnp.float32)
        for head in range(width // head_dim):
            mine = lane // head_dim == head
            there = lanes_seen // head_dim == head
            scores = masked_scores(lanes_of(wide_query, mine), key, first)
            log_total = log_ref[rows, pl.ds(head * head_dim, 1)]
            probs = jnp.exp(scores - log_total)
            prob_grad = dot_rows(lanes_of(wide_grad, mine), value)
            inner = jnp.sum(probs * prob_grad, axis=-1, keepdims=True)
            score_grad = (probs * (prob_grad - inner)).astype(jnp.bfloat16)
            dq = jnp.where(mine, dot_plain(score_grad, key), dq)
            dk = jnp.where(there, dot_columns(score_grad, query), dk)
            dv = jnp.where(there, dot_columns(probs.astype(jnp.bfloat16), grad), dv)
        dq_ref[rows, :] = dq * SCORE_SCALE
        if first + block == length:
            dk_sum[...] = dk
            dv_sum[...] = dv
        else:
            dk_sum[seen, :] += dk
            dv_sum[seen, :] += dv


PAIR = 128
BLOCK = 256


def attend_back(projected, log_total, mixed_grad, head_dim):
    length, columns = projected.shape
    wide = columns // 3
    pairs = wide // PAIR

    def kind(which):
        return pl.BlockSpec((length, PAIR), lambda p: (0, which * pairs + p))

    return pl.pallas_call(
        functools.partial(attend_back_kernel, head_dim, BLOCK),
        grid=(pairs,),
        in_specs=[kind(0), kind(1), kind(2), kind(0), kind(0)],
        out_specs=[pl.BlockSpec((length, PAIR), lambda p: (0, p))] * 3,
        out_shape=[jax.ShapeDtypeStruct((length, wide), jnp.float32)] * 3,
        compiler_params=pltpu.CompilerParams(vmem_limit_bytes=32 << 20),
        cost_estimate=pl.CostEstimate(
            flops=40 * length * length * wide // 5,
            bytes_accessed=18 * length * wide,
            transcendentals=length * length * wide // head_dim,
        ),
        name="attend_back",
    )(projected, projected, projected, log_total, mixed_grad)


def block_order(place):
    half = place // 2
    return (place, 1 + 4 * half - place, 2 - half, 3 - 3 * half)


def greet(dp_count, line):
    me, place = lax.axis_index("dp"), lax.axis_index("tensor")
    barrier = pltpu.get_barrier_semaphore()

    def plane(i, carry):
        pl.semaphore_signal(
            barrier, 1, device_id={"dp": lax.rem(me + i, dp_count)}, device_id_type=MESH
        )
        return carry

    lax.fori_loop(1, dp_count, plane, 0)
    for i in range(1, line):
        pl.semaphore_signal(
            barrier, 1, device_id={"tensor": lax.rem(place + i, line)}, device_id_type=MESH
        )
    pl.semaphore_wait(barrier, dp_count + line - 2)


class Line:
    def __init__(self, own, held, send_sem, recv_sem):
        self.own, self.held, self.send_sem, self.recv_sem = own, held, send_sem, recv_sem
        self.place = lax.axis_index("tensor")
        self.order = block_order(self.place)
        self.last = held.shape[0] - 1

    def copy(self, source, block, index, to):
        return pltpu.make_async_remote_copy(
            src_ref=source,
            dst_ref=self.held.at[block],
            send_sem=self.send_sem.at[index],
            recv_sem=self.recv_sem.at[block],
            device_id={"tensor": to},
            device_id_type=MESH,
        )

    def left(self):
        return self.copy(self.own, self.place, 0, self.place - 1)

    def right(self):
        return self.copy(self.own, self.place, self.last + 1, self.place + 1)

    def onward(self, step):
        block = self.order[step]
        up = self.copy(self.held.at[block], block, step, self.place + 1)
        down = self.copy(self.held.at[block], block, step, self.place - 1)
        return (
            (jnp.logical_and(block < self.place, self.place < self.last), up),
            (jnp.logical_and(block > self.place, self.place > 0), down),
        )

    def start(self):
        pl.when(self.place > 0)(lambda: self.left().start())
        pl.when(self.place < self.last)(lambda: self.right().start())

    def take(self, step):
        block = self.order[step]
        self.copy(self.held.at[block], block, step, block).wait_recv()
        for needed, copy in self.onward(step):
            pl.when(needed)(copy.start)

    def finish(self):
        pl.when(self.place > 0)(lambda: self.left().wait_send())
        pl.when(self.place < self.last)(lambda: self.right().wait_send())
        for step in range(1, self.last + 1):
            for needed, copy in self.onward(step):
                pl.when(needed)(copy.wait_send)


def slot_matrix(target_ref, block, first, count):
    target = target_ref[block, 0:1, :]
    slot = lax.broadcasted_iota(jnp.int32, (count, target.shape[1]), 0) + first
    return jnp.where(slot == target, 1.0, 0.0).astype(jnp.bfloat16)


class Plane:
    def __init__(self, piece, place_of, send_sem, recv_sem, local_sem, dp_count):
        self.piece, self.place_of = piece, place_of
        self.send_sem, self.recv_sem, self.local_sem = send_sem, recv_sem, local_sem
        self.me, self.dp_count = lax.axis_index("dp"), dp_count

    def copy(self, step, i):
        to = lax.rem(self.me + i, self.dp_count)
        return pltpu.make_async_remote_copy(
            src_ref=self.piece(step, to),
            dst_ref=self.place_of(step, self.me),
            send_sem=self.send_sem.at[step, i],
            recv_sem=self.recv_sem.at[step, i],
            device_id={"dp": to},
            device_id_type=MESH,
        )

    def own(self, step):
        return pltpu.make_async_copy(
            self.piece(step, self.me), self.place_of(step, self.me), self.local_sem.at[step]
        )

    def start(self, step):
        def one(i, carry):
            self.copy(step, i).start()
            return carry

        lax.fori_loop(1, self.dp_count, one, 0)
        self.own(step).start()

    def wait_recv(self, step):
        def one(i, carry):
            here = lax.rem(self.me + self.dp_count - i, self.dp_count)
            pltpu.make_async_remote_copy(
                src_ref=self.piece(step, self.me),
                dst_ref=self.place_of(step, here),
                send_sem=self.send_sem.at[step, i],
                recv_sem=self.recv_sem.at[step, i],
                device_id={"dp": here},
                device_id_type=MESH,
            ).wait_recv()
            return carry

        lax.fori_loop(1, self.dp_count, one, 0)
        self.own(step).wait()

    def wait_send(self, step):
        def one(i, carry):
            self.copy(step, i).wait_send()
            return carry

        lax.fori_loop(1, self.dp_count, one, 0)


def dispatch_block(rows, target_ref, block, slots, step, per):
    groups = slots.shape[1]
    chunk = 256 // per

    def one(i, carry):
        chosen = slot_matrix(target_ref, block, i * 256, 256)
        values = dot_plain(chosen, rows[...]).astype(jnp.bfloat16)
        slots[step, pl.ds(i * chunk, chunk)] = values.reshape((chunk, per) + values.shape[1:])
        return carry

    lax.fori_loop(0, groups // chunk, one, 0)


def collect_block(slots, target_ref, block, step, per):
    groups = slots.shape[1]
    chunk = 256 // per
    total = None
    for i in range(groups // chunk):
        chosen = slot_matrix(target_ref, block, i * 256, 256)
        values = slots[step, pl.ds(i * chunk, chunk)]
        term = dot_columns(chosen, values.reshape((256,) + values.shape[2:]))
        total = term if total is None else total + term
    return total


GELU_SCALE = 0.7978845608028654
GELU_CUBE = 0.044715


def expert_kernel(
    dp_count,
    rows_ref,
    target_ref,
    grads_ref,
    w_in_ref,
    w_out_ref,
    back_ref,
    result_ref,
    d_in_ref,
    d_out_ref,
    held,
    slots,
    arrived,
    grads,
    active,
    hidden_grad,
    sent_back,
    returned,
    far,
    line_send,
    line_recv,
    send_sem,
    recv_sem,
    back_send,
    back_recv,
    local_sem,
    back_local,
    grad_sem,
    far_send,
    far_recv,
    out_sem,
):
    line = held.shape[0]
    experts, _, _, per, width = arrived.shape
    place, me = lax.axis_index("tensor"), lax.axis_index("dp")
    order = block_order(place)
    rows_of = dp_count * per
    greet(dp_count, line)
    along = Line(rows_ref, held, line_send, line_recv)
    along.start()
    out_plane = Plane(
        lambda step, to: slots.at[step, pl.ds(to * experts, experts)],
        lambda step, at: arrived.at[:, step, at],
        send_sem,
        recv_sem,
        local_sem,
        dp_count,
    )
    back_plane = Plane(
        lambda step, to: sent_back.at[:, step, to],
        lambda step, at: returned.at[step, pl.ds(at * experts, experts)],
        back_send,
        back_recv,
        back_local,
        dp_count,
    )

    def grad_copy(step):
        return pltpu.make_async_copy(
            grads_ref.at[:, step], grads.at[:, step % 2], grad_sem.at[step]
        )

    def dispatch(step):
        if step:
            along.take(step)
        source = rows_ref if step == 0 else held.at[order[step]]
        dispatch_block(source, target_ref, order[step], slots, step, per)
        out_plane.start(step)

    half = dp_count // 2

    def forward(step):
        grad_copy(step).wait()
        for expert in range(experts):

            def one(i, carry):
                part = pl.ds(i * half, half)
                x = arrived[expert, step, part].reshape(half * per, width)
                g = grads[expert, step % 2, part].reshape(half * per, width)
                hidden = dot_plain(x, w_in_ref[expert])
                inner = GELU_SCALE * (hidden + GELU_CUBE * hidden * hidden * hidden)
                bend = jnp.tanh(inner)
                gate = 0.5 * (1.0 + bend)
                active[expert, part] = (
                    (hidden * gate).astype(jnp.bfloat16).reshape(half, per, -1)
                )
                slope = gate + 0.5 * hidden * (1.0 - bend * bend) * (
                    GELU_SCALE * (1.0 + 3.0 * GELU_CUBE * hidden * hidden)
                )
                change = (dot_rows(g, w_out_ref[expert]) * slope).astype(jnp.bfloat16)
                hidden_grad[expert, part] = change.reshape(half, per, -1)
                row_grad = dot_rows(change, w_in_ref[expert]).astype(jnp.bfloat16)
                sent_back[expert, step, part] = row_grad.reshape(half, per, width)
                return carry

            lax.fori_loop(0, 2, one, 0)
        back_plane.start(step)

    def result_copy(step, expert):
        return pltpu.make_async_copy(
            slots.at[step, pl.ds(expert * dp_count, dp_count)],
            result_ref.at[expert, order[step]],
            out_sem.at[step, expert],
        )

    def later(step):
        out_plane.wait_send(step)
        for expert in range(experts):
            a = active[expert].reshape(rows_of, -1)
            result = dot_plain(a, w_out_ref[expert]).astype(jnp.bfloat16)
            slots[step, pl.ds(expert * dp_count, dp_count)] = result.reshape(
                dp_count, per, width
            )
            result_copy(step, expert).start()
            g = grads[expert, step % 2].reshape(rows_of, width)
            x = arrived[expert, step].reshape(rows_of, width)
            change = hidden_grad[expert].reshape(rows_of, -1)
            if step == 0:
                d_out_ref[expert] = dot_columns(a, g)
                d_in_ref[expert] = dot_columns(x, change)
            else:
                d_out_ref[expert] += dot_columns(a, g)
                d_in_ref[expert] += dot_columns(x, change)

    mine = lax.rem(place, 2)
    mate = order[1]
    rows_half = rows_ref.shape[0] // 2
    kept = pl.ds(mine * rows_half, rows_half)
    passed = pl.ds((1 - mine) * rows_half, rows_half)

    def mate_copy():
        return pltpu.make_async_remote_copy(
            src_ref=held.at[1],
            dst_ref=far.at[0],
            send_sem=far_send.at[0],
            recv_sem=far_recv.at[0],
            device_id={"tensor": mate},
            device_id_type=MESH,
        )

    def half_copy(step):
        return pltpu.make_async_remote_copy(
            src_ref=held.at[step, passed],
            dst_ref=far.at[step, passed],
            send_sem=far_send.at[step - 1],
            recv_sem=far_recv.at[step - 1],
            device_id={"tensor": mate},
            device_id_type=MESH,
        )

    def owner_copy(step, part, at):
        return pltpu.make_async_remote_copy(
            src_ref=held.at[step, part],
            dst_ref=far.at[1, part],
            send_sem=far_send.at[step + 1],
            recv_sem=far_recv.at[3 + at],
            device_id={"tensor": order[step]},
            device_id_type=MESH,
        )

    grad_copy(0).start()
    grad_copy(1).start()
    dispatch(0)
    for step in range(line):
        if step + 1 < line:
            dispatch(step + 1)
        out_plane.wait_recv(step)
        forward(step)
        later(step)
        if step + 2 < line:
            grad_copy(step + 2).start()
    along.finish()
    back_plane.wait_recv(0)
    back_ref[...] = collect_block(returned, target_ref, order[0], 0, per)
    for step in range(1, line):
        back_plane.wait_recv(step)
        held[step] = collect_block(returned, target_ref, order[step], step, per).astype(
            jnp.bfloat16
        )
        if step == 1:
            mate_copy().start()
            continue
        half_copy(step).start()
        pltpu.make_async_remote_copy(
            src_ref=held.at[step, kept],
            dst_ref=far.at[step, kept],
            send_sem=far_send.at[step - 1],
            recv_sem=far_recv.at[step - 1],
            device_id={"tensor": mate},
            device_id_type=MESH,
        ).wait_recv()
        held[step, kept] = (
            held[step, kept].astype(jnp.float32) + far[step, kept].astype(jnp.float32)
        ).astype(jnp.bfloat16)
        owner_copy(step, kept, mine).start()
    mate_copy().wait()
    owner_copy(2, pl.ds(0, rows_half), 0).wait_recv()
    owner_copy(2, pl.ds(rows_half, rows_half), 1).wait_recv()
    back_ref[...] += far[0].astype(jnp.float32) + far[1].astype(jnp.float32)
    for step in range(line):
        back_plane.wait_send(step)
        for expert in range(experts):
            result_copy(step, expert).wait()
    for step in (2, 3):
        half_copy(step).wait_send()
        owner_copy(step, kept, mine).wait_send()


def run_experts(rows, targets, grads, w_in, w_out, dp_count, line):
    experts, _, _, per, width = grads.shape
    units = w_in.shape[2]
    low, dma = jnp.bfloat16, pltpu.SemaphoreType.DMA
    whole, far = pl.BlockSpec(memory_space=pltpu.VMEM), pl.BlockSpec(memory_space=pl.ANY)
    groups = dp_count * experts
    return pl.pallas_call(
        functools.partial(expert_kernel, dp_count),
        in_specs=[whole, whole, far, whole, whole],
        out_specs=[whole, far, whole, whole],
        out_shape=[
            jax.ShapeDtypeStruct(rows.shape, jnp.float32),
            jax.ShapeDtypeStruct(grads.shape, low),
            jax.ShapeDtypeStruct((experts, width, units), jnp.float32),
            jax.ShapeDtypeStruct((experts, units, width), jnp.float32),
        ],
        scratch_shapes=[
            pltpu.VMEM((line,) + rows.shape, low),
            pltpu.VMEM((line, groups, per, width), low),
            pltpu.VMEM(grads.shape, low),
            pltpu.VMEM((experts, 2, dp_count, per, width), low),
            pltpu.VMEM((experts, dp_count, per, units), low),
            pltpu.VMEM((experts, dp_count, per, units), low),
            pltpu.VMEM(grads.shape, low),
            pltpu.VMEM((line, groups, per, width), low),
            pltpu.VMEM((line,) + rows.shape, low),
            dma((line + 1,)),
            dma((line,)),
            dma((line, dp_count)),
            dma((line, dp_count)),
            dma((line, dp_count)),
            dma((line, dp_count)),
            dma((line,)),
            dma((line,)),
            dma((line,)),
            dma((line + 1,)),
            dma((line + 1,)),
            dma((line, experts)),
        ],
        compiler_params=pltpu.CompilerParams(
            collective_id=0, has_side_effects=True, vmem_limit_bytes=61 << 20
        ),
        cost_estimate=pl.CostEstimate(
            flops=12 * experts * line * dp_count * per * width * units,
            bytes_accessed=8 * grads.size,
            transcendentals=grads.size,
        ),
        name="experts",
    )(rows, targets, grads, w_in, w_out)


def norm_stats(values):
    center = jnp.mean(values, axis=-1, keepdims=True)
    centered = values - center
    inv_scale = lax.rsqrt(jnp.mean(centered * centered, axis=-1, keepdims=True) + EPSILON)
    return centered * inv_scale, inv_scale


def attend_pair(proj_ref, mixed_ref, log_ref, pair, head_dim):
    length = proj_ref.shape[0]
    wide = proj_ref.shape[1] // 3
    here = pl.ds(pair * PAIR, PAIR)
    lane = lax.broadcasted_iota(jnp.int32, (BLOCK, PAIR), 1)
    for first in range(0, length, BLOCK):
        rows, seen = pl.ds(first, BLOCK), pl.ds(0, first + BLOCK)
        wide_query = proj_ref[rows, here].astype(jnp.float32) * SCORE_SCALE
        key = proj_ref[seen, pl.ds(wide + pair * PAIR, PAIR)]
        value = proj_ref[seen, pl.ds(2 * wide + pair * PAIR, PAIR)]
        mixed = jnp.zeros((BLOCK, PAIR), jnp.float32)
        logs = jnp.zeros((BLOCK, PAIR), jnp.float32)
        for head in range(PAIR // head_dim):
            mine = lane // head_dim == head
            scores = masked_scores(lanes_of(wide_query, mine), key, first)
            top = jnp.max(scores, axis=-1, keepdims=True)
            powers = jnp.exp(scores - top)
            total = jnp.sum(powers, axis=-1, keepdims=True)
            probs = (powers * (1.0 / total)).astype(jnp.bfloat16)
            mixed = jnp.where(mine, dot_plain(probs, value), mixed)
            logs = jnp.where(mine, top + jnp.log(total), logs)
        mixed_ref[rows, here] = mixed.astype(jnp.bfloat16)
        log_ref[rows, here] = logs


def send(source, there, send_sem, recv_sem, **to):
    return pltpu.make_async_remote_copy(
        src_ref=source,
        dst_ref=there,
        send_sem=send_sem,
        recv_sem=recv_sem,
        device_id=to,
        device_id_type=MESH,
    )


class Share:
    def __init__(self, held, sems, dp_count):
        self.held, self.steps = held, dp_count // 2
        self.sems, self.dp_count = sems, dp_count
        self.me = lax.axis_index("dp")
        self.other = self.me + 1 - 2 * lax.rem(self.me, 2)

    def block(self, of, i):
        return lax.rem(of + self.dp_count - 2 * i, self.dp_count)

    def across(self, i):
        to = lax.rem(self.me + 2 * i, self.dp_count)
        mine = self.held.at[self.me]
        return send(mine, mine, self.sems.at[0, i], self.sems.at[1, i], dp=to)

    def within(self, i):
        piece = self.held.at[self.block(self.me, i)]
        return send(piece, piece, self.sems.at[2, i], self.sems.at[3, i], dp=self.other)

    def start(self):
        for i in range(1, self.steps):
            self.across(i).start()
        self.within(0).start()

    def relay(self):
        for i in range(1, self.steps):
            at = self.block(self.me, i)
            piece = self.held.at[at]
            send(piece, piece, self.sems.at[0, i], self.sems.at[1, i], dp=at).wait_recv()
            self.within(i).start()

    def finish(self):
        for i in range(self.steps):
            piece = self.held.at[self.block(self.other, i)]
            send(piece, piece, self.sems.at[2, i], self.sems.at[3, i], dp=self.other).wait_recv()

    def drain(self):
        for i in range(self.steps):
            if i:
                self.across(i).wait_send()
            self.within(i).wait_send()


def front_kernel(
    dp_count,
    head_dim,
    tokens_ref,
    cot_ref,
    own_target_ref,
    qkv_a_ref,
    qkv_b_ref,
    out_a_ref,
    out_b_ref,
    gains_ref,
    grads_ref,
    target_ref,
    wq_ref,
    wo_ref,
    first_ref,
    proj_ref,
    log_ref,
    mixed_ref,
    middle_ref,
    second_ref,
    held,
    slots,
    hop,
    out_parts,
    mixed_all,
    line_send,
    line_recv,
    send_sem,
    recv_sem,
    local_sem,
    target_send,
    target_recv,
    near_send,
    near_recv,
    mix_send,
    mix_recv,
    q_sems,
    o_sems,
):
    line = held.shape[0]
    experts, _, _, per, _ = grads_ref.shape
    rows = tokens_ref.shape[0]
    me, place = lax.axis_index("dp"), lax.axis_index("tensor")
    order = block_order(place)
    mate, across, last = order[1], lax.rem(place + 2, line), line - 1 - place
    part = lax.rem(place, 2)
    wide = proj_ref.shape[1] // 3
    greet(dp_count, line)

    near = [
        send(qkv_b_ref, hop, near_send.at[0], near_recv.at[0], tensor=across),
        send(out_a_ref, out_parts.at[1], near_send.at[1], near_recv.at[1], tensor=mate),
        send(out_b_ref, out_parts.at[0], near_send.at[2], near_recv.at[2], tensor=across),
        send(out_b_ref, out_parts.at[2], near_send.at[3], near_recv.at[3], tensor=last),
    ]
    for copy in near:
        copy.start()
    target_ref[place] = own_target_ref[...]

    def target_copy(i, at, to):
        return send(
            target_ref.at[at], target_ref.at[at], target_send.at[i], target_recv.at[i], tensor=to
        )

    for i in range(1, line):
        target_copy(i, place, lax.rem(place + i, line)).start()

    def first_rows(i, carry):
        values = tokens_ref[pl.ds(i * 128, 128), :].astype(jnp.float32)
        unit, _ = norm_stats(values)
        unit = unit * gains_ref[0:1, :] + gains_ref[1:2, :]
        first_ref[part, pl.ds(i * 128, 128), :] = unit.astype(jnp.bfloat16)
        return carry

    lax.fori_loop(0, rows // 128, first_rows, 0)
    first_copy = send(
        first_ref.at[part], first_ref.at[part], near_send.at[4], near_recv.at[4], tensor=mate
    )
    first_copy.start()
    along = Line(cot_ref, held, line_send, line_recv)
    along.start()
    near[0].wait_recv()
    for kind in range(3):
        base = kind * wide
        wq_ref[me, :, base : base + PAIR] = qkv_a_ref[:, base : base + PAIR]
        wq_ref[me, :, base + PAIR : base + wide] = (
            qkv_a_ref[:, base + PAIR : base + wide].astype(jnp.float32)
            + hop[kind].astype(jnp.float32)
        ).astype(jnp.bfloat16)
    share_q = Share(wq_ref, q_sems, dp_count)
    share_q.start()
    for copy in near[1:]:
        copy.wait_recv()
    for group, (a, b) in enumerate(((out_a_ref[...], 0), (out_parts[1], 2))):
        base = group * wide
        a = a.astype(jnp.float32)
        b = out_parts[b].astype(jnp.float32)
        wo_ref[me, :, base : base + PAIR] = a[:, :PAIR].astype(jnp.bfloat16)
        wo_ref[me, :, base + PAIR : base + 2 * PAIR] = (a[:, PAIR:] + b[:, :PAIR]).astype(
            jnp.bfloat16
        )
        wo_ref[me, :, base + 2 * PAIR : base + wide] = b[:, PAIR:].astype(jnp.bfloat16)
    share_o = Share(wo_ref, o_sems, dp_count)
    share_o.start()
    share_q.relay()

    plane = Plane(
        lambda step, to: slots.at[step, pl.ds(to * experts, experts)],
        lambda step, at: grads_ref.at[:, step, at],
        send_sem,
        recv_sem,
        local_sem,
        dp_count,
    )

    def dispatch(step):
        if step:
            along.take(step)
        source = cot_ref if step == 0 else held.at[order[step]]
        dispatch_block(source, target_ref, order[step], slots, step, per)
        plane.start(step)

    dispatch(0)
    share_o.relay()
    share_q.finish()
    send(
        first_ref.at[1 - part], first_ref.at[1 - part], near_send.at[4], near_recv.at[4], tensor=mate
    ).wait_recv()

    def project(i, carry):
        values = first_ref[i // 2, pl.ds(lax.rem(i, 2) * (rows // 2), rows // 2), :]
        weights = wq_ref[...].reshape(-1, 3 * wide)
        proj_ref[pl.ds(i * (rows // 2), rows // 2), :] = dot_plain(values, weights).astype(
            jnp.bfloat16
        )
        return carry

    lax.fori_loop(0, 4, project, 0)
    for i in range(1, line):
        target_copy(i, lax.rem(place + line - i, line), lax.rem(place + line - i, line)).wait_recv()

    def mix_copy(pair):
        here = pl.ds(pair * PAIR, PAIR)
        return send(
            mixed_all.at[pl.ds((1 - part) * rows, rows), here],
            mixed_ref.at[1, :, here],
            mix_send.at[pair],
            mix_recv.at[pair],
            tensor=mate,
        )

    for pair in range(wide // PAIR):
        dispatch(pair + 1)
        attend_pair(proj_ref, mixed_all, log_ref, pair, head_dim)
        mix_copy(pair).start()
    mixed_ref[0] = mixed_all[pl.ds(part * rows, rows), :]
    share_o.finish()
    for pair in range(wide // PAIR):
        mix_copy(pair).wait_recv()

    def finish_rows(i, carry):
        here = pl.ds(i * 128, 128)
        total = tokens_ref[here, :].astype(jnp.float32)
        total += dot_rows(mixed_ref[0, here, :], wo_ref[:, :, :wide].reshape(-1, wide)) + dot_rows(
            mixed_ref[1, here, :], wo_ref[:, :, wide:].reshape(-1, wide)
        )
        middle_ref[here, :] = total
        unit, _ = norm_stats(total)
        second_ref[here, :] = (unit * gains_ref[2:3, :] + gains_ref[3:4, :]).astype(jnp.bfloat16)
        return carry

    lax.fori_loop(0, rows // 128, finish_rows, 0)
    along.finish()
    share_q.drain()
    share_o.drain()
    for copy in near:
        copy.wait_send()
    first_copy.wait_send()
    for i in range(1, line):
        target_copy(i, place, lax.rem(place + i, line)).wait_send()
    for pair in range(wide // PAIR):
        mix_copy(pair).wait_send()
    for step in range(line):
        plane.wait_recv(step)
        plane.wait_send(step)


def run_front(tokens, cotangent, target, weights, gains, sizes):
    dp_count, line, experts, per, head_dim = sizes
    rows, width = tokens.shape
    qkv_a, qkv_b, out_a, out_b = weights
    share, columns = qkv_a.shape
    wide = columns // 3
    low, dma = jnp.bfloat16, pltpu.SemaphoreType.DMA
    whole, far = pl.BlockSpec(memory_space=pltpu.VMEM), pl.BlockSpec(memory_space=pl.ANY)
    shape = jax.ShapeDtypeStruct
    return pl.pallas_call(
        functools.partial(front_kernel, dp_count, head_dim),
        in_specs=[whole] * 8,
        out_specs=[far] + [whole] * 9,
        out_shape=[
            shape((experts, line, dp_count, per, width), low),
            shape((line,) + target.shape, jnp.int32),
            shape((dp_count, share, columns), low),
            shape((dp_count, share, 2 * wide), low),
            shape((2, rows, width), low),
            shape((2 * rows, columns), low),
            shape((2 * rows, wide), jnp.float32),
            shape((2, rows, wide), low),
            shape((rows, width), jnp.float32),
            shape((rows, width), low),
        ],
        scratch_shapes=[
            pltpu.VMEM((line, rows, width), low),
            pltpu.VMEM((line, dp_count * experts, per, width), low),
            pltpu.VMEM(qkv_b.shape, low),
            pltpu.VMEM((3,) + out_b.shape, low),
            pltpu.VMEM((2 * rows, wide), low),
            dma((line + 1,)),
            dma((line,)),
            dma((line, dp_count)),
            dma((line, dp_count)),
            dma((line,)),
            dma((line,)),
            dma((line,)),
            dma((5,)),
            dma((5,)),
            dma((wide // PAIR,)),
            dma((wide // PAIR,)),
            dma((4, dp_count // 2)),
            dma((4, dp_count // 2)),
        ],
        compiler_params=pltpu.CompilerParams(
            collective_id=1, has_side_effects=True, vmem_limit_bytes=56 << 20
        ),
        name="front",
    )(tokens, cotangent, target, *weights, gains)


def product(spec, left, right):
    return jnp.einsum(spec, left, right, preferred_element_type=jnp.float32)


def on_device(
    tokens,
    token_ids,
    hash_table,
    ln1_gain,
    ln1_bias,
    w_qkv,
    w_out,
    ln2_gain,
    ln2_bias,
    expert_in,
    expert_out,
    cotangent,
):
    low = jnp.bfloat16
    row_count, model_width = tokens.shape
    local_experts = expert_in.shape[0]
    dp_count = lax.axis_size("dp")
    line = lax.axis_size("tensor")
    shares = LEN // row_count
    place = lax.axis_index("tensor")
    part = place % shares
    swap = [(t, t ^ 1) for t in range(line)]
    hop = [(t, t ^ 2) for t in range(line)]
    head_dim = w_qkv.shape[2] // 3
    heads_shard = w_qkv.shape[1]

    def swapped(values):
        return lax.ppermute(values, "tensor", swap)

    def joined(own, other):
        both = jnp.stack([own, other])
        return jnp.where(part == 0, both, both[::-1]).reshape((-1,) + own.shape[1:])

    def halves(both):
        pair = both.reshape((shares, -1) + both.shape[1:])
        return (
            lax.dynamic_index_in_dim(pair, part, 0, False),
            lax.dynamic_index_in_dim(pair, 1 - part, 0, False),
        )

    experts_total = dp_count * local_experts
    capacity = 2 * row_count // experts_total
    slot_count = experts_total * capacity
    expert_of = jnp.take(hash_table, token_ids)
    one_hot = (expert_of[:, None] == jnp.arange(experts_total, dtype=jnp.int32)[None, :]).astype(
        jnp.int32
    )
    before = (
        lax.broadcasted_iota(jnp.int32, (row_count, row_count), 0)
        > lax.broadcasted_iota(jnp.int32, (row_count, row_count), 1)
    ).astype(low)
    earlier = jnp.dot(before, one_hot.astype(low), preferred_element_type=jnp.float32)
    slot_rank = jnp.sum(earlier.astype(jnp.int32) * one_hot, axis=1)
    target = jnp.where(slot_rank < capacity, expert_of * capacity + slot_rank, slot_count)
    own_target = jnp.broadcast_to(target[None, :], (8, row_count))

    share = w_qkv.shape[0]
    wide = 2 * heads_shard * head_dim
    by_kind = w_qkv.astype(low).reshape(share, heads_shard, 3, head_dim).transpose(0, 2, 1, 3)
    qkv_a = jnp.pad(by_kind.reshape(share, 3, -1), ((0, 0), (0, 0), (0, wide // 2)))
    qkv_b = jnp.concatenate([by_kind[:, :, -1:], by_kind[:, :, :-1]], axis=2).reshape(share, 3, -1)
    qkv_b = jnp.pad(qkv_b, ((0, 0), (0, 0), (head_dim, 0))).transpose(1, 0, 2)
    out_rows = w_out.astype(low).T
    out_a = jnp.pad(out_rows, ((0, 0), (0, head_dim)))
    out_b = jnp.concatenate([out_rows[:, -head_dim:], out_rows[:, :-head_dim]], axis=1)
    out_b = jnp.pad(out_b, ((0, 0), (head_dim, 0)))
    gains = jnp.stack([ln1_gain, ln1_bias, ln2_gain, ln2_bias])
    sizes = (dp_count, line, local_experts, capacity, head_dim)
    (
        grad_rows,
        targets,
        qkv_weight,
        out_weight,
        first_all,
        projected,
        log_total,
        mixed_pair,
        middle,
        second_low,
    ) = run_front(
        tokens,
        cotangent,
        own_target,
        (qkv_a.reshape(share, -1), qkv_b, out_a, out_b),
        jnp.pad(gains, ((0, 4), (0, 0))),
        sizes,
    )
    qkv_flat = qkv_weight.reshape(model_width, -1)
    out_weight = out_weight.reshape(model_width, -1)
    first_all = first_all.reshape(LEN, model_width)
    residual = tokens.astype(jnp.float32)
    _, unit_one, scale_one = normalize(residual, ln1_gain, ln1_bias)
    _, unit_two, scale_two = normalize(middle, ln2_gain, ln2_bias)

    out_grad = cotangent.astype(jnp.float32)
    second_grad, result, grad_expert_in, grad_expert_out = run_experts(
        second_low,
        targets,
        grad_rows,
        expert_in.astype(low),
        expert_out.astype(low),
        dp_count,
        line,
    )
    gain_two_grad = jnp.sum(second_grad * unit_two, axis=0)
    bias_two_grad = jnp.sum(second_grad, axis=0)
    middle_grad = out_grad + norm_back(second_grad, unit_two, scale_two, ln2_gain)
    middle_low = middle_grad.astype(low)
    mixed_both = product("td,dk->tk", middle_low, out_weight).astype(low)
    mixed_grad = joined(mixed_both[:, :wide], swapped(mixed_both[:, wide:]))
    result, mixed_grad = lax.optimization_barrier((result, mixed_grad))
    result = lax.all_to_all(result.transpose(2, 0, 1, 3, 4), "dp", split_axis=0, concat_axis=0)
    result = result.transpose(2, 0, 1, 3, 4).reshape(line, slot_count, model_width)
    chosen = (
        jnp.arange(slot_count, dtype=jnp.int32)[None, :, None] == targets[:, :1, :]
    ).astype(low)
    rows = product("bsr,bsd->brd", chosen, result).astype(low)
    rows = rows.reshape(line * row_count, model_width)
    rows = lax.psum_scatter(rows, "tensor", scatter_dimension=0, tiled=True)
    mixed_out = middle + rows.astype(jnp.float32)
    out_wgrad = product("td,ptk->dpk", middle_low, mixed_pair).reshape(model_width, -1).astype(low)
    out_part = lax.psum_scatter(out_wgrad, "dp", scatter_dimension=0, tiled=True)
    half = wide // 2

    def swap_last(values):
        return jnp.concatenate([values[:, head_dim:], values[:, :head_dim]], axis=1)

    pieces = (
        out_part[:, :half],
        out_part[:, wide : wide + half],
        swap_last(out_part[:, half:wide]),
        swap_last(out_part[:, wide + half :]),
    )
    out_total = pieces[0].astype(jnp.float32)
    for i in range(1, line):
        sent = lax.ppermute(pieces[i], "tensor", [(t, t ^ i) for t in range(line)])
        out_total = out_total + sent.astype(jnp.float32)
    out_total = out_total.T

    qkv_grad = jnp.concatenate(attend_back(projected, log_total, mixed_grad, head_dim), axis=1).astype(low)
    qkv_wgrad = product("td,tk->dk", first_all, qkv_grad).astype(low)
    qkv_part = lax.psum_scatter(qkv_wgrad, "dp", scatter_dimension=0, tiled=True)
    qkv_part = qkv_part.reshape(share, 3, wide)
    qkv_far = qkv_part[:, :, half:]
    qkv_far = jnp.concatenate([qkv_far[:, :, head_dim:], qkv_far[:, :, :head_dim]], axis=2)
    qkv_far = lax.ppermute(qkv_far, "tensor", hop)
    qkv_total = qkv_part[:, :, :half].astype(jnp.float32) + qkv_far.astype(jnp.float32)
    qkv_total = qkv_total.reshape(share, 3, heads_shard, head_dim).transpose(0, 2, 1, 3)
    qkv_total = qkv_total.reshape(w_qkv.shape)
    first_own, first_sent = halves(product("tk,dk->td", qkv_grad, qkv_flat))
    first_grad = first_own + swapped(first_sent.astype(low)).astype(jnp.float32)
    gain_one_grad = jnp.sum(first_grad * unit_one, axis=0)
    bias_one_grad = jnp.sum(first_grad, axis=0)
    input_grad = middle_grad + norm_back(first_grad, unit_one, scale_one, ln1_gain)
    norm_sums = lax.psum(
        (gain_one_grad, bias_one_grad, gain_two_grad, bias_two_grad), ("dp", "tensor")
    )
    return (
        mixed_out.astype(low),
        input_grad.astype(low),
        norm_sums[0],
        norm_sums[1],
        qkv_total,
        out_total,
        norm_sums[2],
        norm_sums[3],
        grad_expert_in,
        grad_expert_out,
    )


def solution(mesh):
    rows = P(("dp", "tensor"), None)
    weights = (P("dp", "tensor", None), P("tensor", "dp"))
    experts = (P("dp", None, "tensor"), P("dp", "tensor", None))
    return jax.shard_map(
        on_device,
        mesh=mesh,
        in_specs=(rows, P(("dp", "tensor")), P(), P(), P(), *weights, P(), P(), *experts, rows),
        out_specs=(rows, rows, P(), P(), *weights, P(), P(), *experts),
        check_vma=False,
    )
```

```python
import functools

import jax
import jax.numpy as jnp
from jax import lax
from jax.experimental import pallas as pl
from jax.experimental.pallas import tpu as pltpu
from jax.sharding import PartitionSpec as P

LEN = 1024


EPSILON = 1e-05
SCORE_SCALE = 0.125
MASKED = -1e30
MESH = pl.DeviceIdType.MESH


def lanes_of(values, mask):
    return jnp.where(mask, values, 0.0).astype(jnp.bfloat16)


def dot_rows(left, right):
    return lax.dot_general(left, right, (((1,), (1,)), ((), ())), preferred_element_type=jnp.float32)


def dot_columns(left, right):
    return lax.dot_general(left, right, (((0,), (0,)), ((), ())), preferred_element_type=jnp.float32)


def dot_plain(left, right):
    return jnp.dot(left, right, preferred_element_type=jnp.float32)


def masked_scores(query, key, first):
    scores = dot_rows(query, key)
    rows, columns = scores.shape
    row = lax.broadcasted_iota(jnp.int32, (rows, rows), 0)
    column = lax.broadcasted_iota(jnp.int32, (rows, rows), 1)
    edge = jnp.where(row >= column, scores[:, first:], MASKED)
    return edge if first == 0 else jnp.concatenate([scores[:, :first], edge], axis=1)


PAIR = 128
BLOCK = 256


def block_order(place):
    half = place // 2
    return (place, 1 + 4 * half - place, 2 - half, 3 - 3 * half)


def greet(dp_count, line):
    me, place = lax.axis_index("dp"), lax.axis_index("tensor")
    barrier = pltpu.get_barrier_semaphore()

    def plane(i, carry):
        pl.semaphore_signal(
            barrier, 1, device_id={"dp": lax.rem(me + i, dp_count)}, device_id_type=MESH
        )
        return carry

    lax.fori_loop(1, dp_count, plane, 0)
    for i in range(1, line):
        pl.semaphore_signal(
            barrier, 1, device_id={"tensor": lax.rem(place + i, line)}, device_id_type=MESH
        )
    pl.semaphore_wait(barrier, dp_count + line - 2)


class Line:
    def __init__(self, own, held, send_sem, recv_sem):
        self.own, self.held, self.send_sem, self.recv_sem = own, held, send_sem, recv_sem
        self.place = lax.axis_index("tensor")
        self.order = block_order(self.place)
        self.last = held.shape[0] - 1

    def copy(self, source, block, index, to):
        return pltpu.make_async_remote_copy(
            src_ref=source,
            dst_ref=self.held.at[block],
            send_sem=self.send_sem.at[index],
            recv_sem=self.recv_sem.at[block],
            device_id={"tensor": to},
            device_id_type=MESH,
        )

    def left(self):
        return self.copy(self.own, self.place, 0, self.place - 1)

    def right(self):
        return self.copy(self.own, self.place, self.last + 1, self.place + 1)

    def onward(self, step):
        block = self.order[step]
        up = self.copy(self.held.at[block], block, step, self.place + 1)
        down = self.copy(self.held.at[block], block, step, self.place - 1)
        return (
            (jnp.logical_and(block < self.place, self.place < self.last), up),
            (jnp.logical_and(block > self.place, self.place > 0), down),
        )

    def start(self):
        pl.when(self.place > 0)(lambda: self.left().start())
        pl.when(self.place < self.last)(lambda: self.right().start())

    def take(self, step):
        block = self.order[step]
        self.copy(self.held.at[block], block, step, block).wait_recv()
        for needed, copy in self.onward(step):
            pl.when(needed)(copy.start)

    def finish(self):
        pl.when(self.place > 0)(lambda: self.left().wait_send())
        pl.when(self.place < self.last)(lambda: self.right().wait_send())
        for step in range(1, self.last + 1):
            for needed, copy in self.onward(step):
                pl.when(needed)(copy.wait_send)


def slot_matrix(target_ref, block, first, count):
    target = target_ref[block, 0:1, :]
    slot = lax.broadcasted_iota(jnp.int32, (count, target.shape[1]), 0) + first
    return jnp.where(slot == target, 1.0, 0.0).astype(jnp.bfloat16)


class Plane:
    def __init__(self, piece, place_of, send_sem, recv_sem, local_sem, dp_count):
        self.piece, self.place_of = piece, place_of
        self.send_sem, self.recv_sem, self.local_sem = send_sem, recv_sem, local_sem
        self.me, self.dp_count = lax.axis_index("dp"), dp_count

    def copy(self, step, i):
        to = lax.rem(self.me + i, self.dp_count)
        return pltpu.make_async_remote_copy(
            src_ref=self.piece(step, to),
            dst_ref=self.place_of(step, self.me),
            send_sem=self.send_sem.at[step, i],
            recv_sem=self.recv_sem.at[step, i],
            device_id={"dp": to},
            device_id_type=MESH,
        )

    def own(self, step):
        return pltpu.make_async_copy(
            self.piece(step, self.me), self.place_of(step, self.me), self.local_sem.at[step]
        )

    def start(self, step):
        def one(i, carry):
            self.copy(step, i).start()
            return carry

        lax.fori_loop(1, self.dp_count, one, 0)
        self.own(step).start()

    def wait_recv(self, step):
        def one(i, carry):
            here = lax.rem(self.me + self.dp_count - i, self.dp_count)
            pltpu.make_async_remote_copy(
                src_ref=self.piece(step, self.me),
                dst_ref=self.place_of(step, here),
                send_sem=self.send_sem.at[step, i],
                recv_sem=self.recv_sem.at[step, i],
                device_id={"dp": here},
                device_id_type=MESH,
            ).wait_recv()
            return carry

        lax.fori_loop(1, self.dp_count, one, 0)
        self.own(step).wait()

    def wait_send(self, step):
        def one(i, carry):
            self.copy(step, i).wait_send()
            return carry

        lax.fori_loop(1, self.dp_count, one, 0)


def dispatch_block(rows, target_ref, block, slots, step, per):
    groups = slots.shape[1]
    chunk = 256 // per

    def one(i, carry):
        chosen = slot_matrix(target_ref, block, i * 256, 256)
        values = dot_plain(chosen, rows[...]).astype(jnp.bfloat16)
        slots[step, pl.ds(i * chunk, chunk)] = values.reshape((chunk, per) + values.shape[1:])
        return carry

    lax.fori_loop(0, groups // chunk, one, 0)


def collect_block(slots, target_ref, block, step, per):
    groups = slots.shape[1]
    chunk = 256 // per
    total = None
    for i in range(groups // chunk):
        chosen = slot_matrix(target_ref, block, i * 256, 256)
        values = slots[step, pl.ds(i * chunk, chunk)]
        term = dot_columns(chosen, values.reshape((256,) + values.shape[2:]))
        total = term if total is None else total + term
    return total


def send(source, there, send_sem, recv_sem, **to):
    return pltpu.make_async_remote_copy(
        src_ref=source,
        dst_ref=there,
        send_sem=send_sem,
        recv_sem=recv_sem,
        device_id=to,
        device_id_type=MESH,
    )


class Return:
    def __init__(self, plane, returned, target_ref, stage, far, far_send, far_recv, per):
        self.plane, self.returned, self.target_ref = plane, returned, target_ref
        self.stage, self.far, self.per = stage, far, per
        self.far_send, self.far_recv = far_send, far_recv
        self.place = lax.axis_index("tensor")
        self.order = block_order(self.place)
        self.mine = lax.rem(self.place, 2)
        self.half = stage.shape[1] // 2
        self.kept = pl.ds(self.mine * self.half, self.half)
        self.passed = pl.ds((1 - self.mine) * self.half, self.half)

    def mate_copy(self):
        return send(
            self.stage.at[1],
            self.far.at[0],
            self.far_send.at[0],
            self.far_recv.at[0],
            tensor=self.order[1],
        )

    def half_copy(self, step, part):
        return send(
            self.stage.at[step, part],
            self.far.at[step, part],
            self.far_send.at[step - 1],
            self.far_recv.at[step - 1],
            tensor=self.order[1],
        )

    def owner_copy(self, step, part, at):
        return send(
            self.stage.at[step, part],
            self.far.at[1, part],
            self.far_send.at[step + 1],
            self.far_recv.at[3 + at],
            tensor=self.order[step],
        )

    def collect(self, step):
        return collect_block(self.returned, self.target_ref, self.order[step], step, self.per)

    def step(self, step):
        self.plane.wait_recv(step)
        self.stage[step] = self.collect(step).astype(jnp.bfloat16)
        if step == 1:
            self.mate_copy().start()
            return
        self.half_copy(step, self.passed).start()
        self.half_copy(step, self.kept).wait_recv()
        self.stage[step, self.kept] = (
            self.stage[step, self.kept].astype(jnp.float32)
            + self.far[step, self.kept].astype(jnp.float32)
        ).astype(jnp.bfloat16)
        self.owner_copy(step, self.kept, self.mine).start()

    def wait(self):
        self.mate_copy().wait()
        self.owner_copy(2, pl.ds(0, self.half), 0).wait_recv()
        self.owner_copy(2, pl.ds(self.half, self.half), 1).wait_recv()

    def drain(self):
        for step in range(4):
            self.plane.wait_send(step)
        for step in (2, 3):
            self.half_copy(step, self.passed).wait_send()
            self.owner_copy(step, self.kept, self.mine).wait_send()


GELU_SCALE = 0.7978845608028654
GELU_CUBE = 0.044715


def expert_kernel(
    dp_count,
    rows_ref,
    target_ref,
    grads_ref,
    w_in_ref,
    w_out_ref,
    back_ref,
    result_ref,
    d_in_ref,
    d_out_ref,
    held,
    slots,
    arrived,
    grads,
    active,
    hidden_grad,
    sent_back,
    returned,
    far,
    line_send,
    line_recv,
    send_sem,
    recv_sem,
    back_send,
    back_recv,
    local_sem,
    back_local,
    grad_sem,
    far_send,
    far_recv,
    out_sem,
):
    line = held.shape[0]
    experts, _, _, per, width = arrived.shape
    place, me = lax.axis_index("tensor"), lax.axis_index("dp")
    order = block_order(place)
    rows_of = dp_count * per
    greet(dp_count, line)
    along = Line(rows_ref, held, line_send, line_recv)
    along.start()
    out_plane = Plane(
        lambda step, to: slots.at[step, pl.ds(to * experts, experts)],
        lambda step, at: arrived.at[:, step, at],
        send_sem,
        recv_sem,
        local_sem,
        dp_count,
    )
    back_plane = Plane(
        lambda step, to: sent_back.at[:, step, to],
        lambda step, at: returned.at[step, pl.ds(at * experts, experts)],
        back_send,
        back_recv,
        back_local,
        dp_count,
    )

    def grad_copy(step):
        return pltpu.make_async_copy(
            grads_ref.at[:, step], grads.at[:, step % 2], grad_sem.at[step]
        )

    def dispatch(step):
        if step:
            along.take(step)
        source = rows_ref if step == 0 else held.at[order[step]]
        dispatch_block(source, target_ref, order[step], slots, step, per)
        out_plane.start(step)

    half = dp_count // 2

    def forward(step):
        grad_copy(step).wait()
        for expert in range(experts):

            def one(i, carry):
                part = pl.ds(i * half, half)
                x = arrived[expert, step, part].reshape(half * per, width)
                g = grads[expert, step % 2, part].reshape(half * per, width)
                hidden = dot_plain(x, w_in_ref[expert])
                inner = GELU_SCALE * (hidden + GELU_CUBE * hidden * hidden * hidden)
                bend = jnp.tanh(inner)
                gate = 0.5 * (1.0 + bend)
                active[expert, part] = (
                    (hidden * gate).astype(jnp.bfloat16).reshape(half, per, -1)
                )
                slope = gate + 0.5 * hidden * (1.0 - bend * bend) * (
                    GELU_SCALE * (1.0 + 3.0 * GELU_CUBE * hidden * hidden)
                )
                change = (dot_rows(g, w_out_ref[expert]) * slope).astype(jnp.bfloat16)
                hidden_grad[expert, part] = change.reshape(half, per, -1)
                row_grad = dot_rows(change, w_in_ref[expert]).astype(jnp.bfloat16)
                sent_back[expert, step, part] = row_grad.reshape(half, per, width)
                return carry

            lax.fori_loop(0, 2, one, 0)
        back_plane.start(step)

    def result_copy(step, expert):
        return pltpu.make_async_copy(
            slots.at[step, pl.ds(expert * dp_count, dp_count)],
            result_ref.at[expert, order[step]],
            out_sem.at[step, expert],
        )

    def later(step):
        out_plane.wait_send(step)
        for expert in range(experts):
            a = active[expert].reshape(rows_of, -1)
            result = dot_plain(a, w_out_ref[expert]).astype(jnp.bfloat16)
            slots[step, pl.ds(expert * dp_count, dp_count)] = result.reshape(
                dp_count, per, width
            )
            result_copy(step, expert).start()
            g = grads[expert, step % 2].reshape(rows_of, width)
            x = arrived[expert, step].reshape(rows_of, width)
            change = hidden_grad[expert].reshape(rows_of, -1)
            if step == 0:
                d_out_ref[expert] = dot_columns(a, g)
                d_in_ref[expert] = dot_columns(x, change)
            else:
                d_out_ref[expert] += dot_columns(a, g)
                d_in_ref[expert] += dot_columns(x, change)

    home = Return(back_plane, returned, target_ref, held, far, far_send, far_recv, per)
    grad_copy(0).start()
    grad_copy(1).start()
    dispatch(0)
    for step in range(line):
        if step + 1 < line:
            dispatch(step + 1)
        out_plane.wait_recv(step)
        forward(step)
        later(step)
        if step + 2 < line:
            grad_copy(step + 2).start()
    along.finish()
    back_plane.wait_recv(0)
    back_ref[...] = home.collect(0)
    for step in range(1, line):
        home.step(step)
    home.wait()
    back_ref[...] += far[0].astype(jnp.float32) + far[1].astype(jnp.float32)
    home.drain()
    for step in range(line):
        for expert in range(experts):
            result_copy(step, expert).wait()


def run_experts(rows, targets, grads, w_in, w_out, dp_count, line):
    experts, _, _, per, width = grads.shape
    units = w_in.shape[2]
    low, dma = jnp.bfloat16, pltpu.SemaphoreType.DMA
    whole, far = pl.BlockSpec(memory_space=pltpu.VMEM), pl.BlockSpec(memory_space=pl.ANY)
    groups = dp_count * experts
    return pl.pallas_call(
        functools.partial(expert_kernel, dp_count),
        in_specs=[whole, whole, far, whole, whole],
        out_specs=[whole, far, whole, whole],
        out_shape=[
            jax.ShapeDtypeStruct(rows.shape, jnp.float32),
            jax.ShapeDtypeStruct(grads.shape, low),
            jax.ShapeDtypeStruct((experts, width, units), jnp.float32),
            jax.ShapeDtypeStruct((experts, units, width), jnp.float32),
        ],
        scratch_shapes=[
            pltpu.VMEM((line,) + rows.shape, low),
            pltpu.VMEM((line, groups, per, width), low),
            pltpu.VMEM(grads.shape, low),
            pltpu.VMEM((experts, 2, dp_count, per, width), low),
            pltpu.VMEM((experts, dp_count, per, units), low),
            pltpu.VMEM((experts, dp_count, per, units), low),
            pltpu.VMEM(grads.shape, low),
            pltpu.VMEM((line, groups, per, width), low),
            pltpu.VMEM((line,) + rows.shape, low),
            dma((line + 1,)),
            dma((line,)),
            dma((line, dp_count)),
            dma((line, dp_count)),
            dma((line, dp_count)),
            dma((line, dp_count)),
            dma((line,)),
            dma((line,)),
            dma((line,)),
            dma((line + 1,)),
            dma((line + 1,)),
            dma((line, experts)),
        ],
        compiler_params=pltpu.CompilerParams(
            collective_id=0, has_side_effects=True, vmem_limit_bytes=61 << 20
        ),
        cost_estimate=pl.CostEstimate(
            flops=12 * experts * line * dp_count * per * width * units,
            bytes_accessed=8 * grads.size,
            transcendentals=grads.size,
        ),
        name="experts",
    )(rows, targets, grads, w_in, w_out)


def norm_stats(values):
    center = jnp.mean(values, axis=-1, keepdims=True)
    centered = values - center
    inv_scale = lax.rsqrt(jnp.mean(centered * centered, axis=-1, keepdims=True) + EPSILON)
    return centered * inv_scale, inv_scale


def attend_pair(proj_ref, mixed_ref, log_ref, pair, head_dim):
    length = proj_ref.shape[0]
    wide = proj_ref.shape[1] // 3
    here = pl.ds(pair * PAIR, PAIR)
    lane = lax.broadcasted_iota(jnp.int32, (BLOCK, PAIR), 1)
    for first in range(0, length, BLOCK):
        rows, seen = pl.ds(first, BLOCK), pl.ds(0, first + BLOCK)
        wide_query = proj_ref[rows, here].astype(jnp.float32) * SCORE_SCALE
        key = proj_ref[seen, pl.ds(wide + pair * PAIR, PAIR)]
        value = proj_ref[seen, pl.ds(2 * wide + pair * PAIR, PAIR)]
        mixed = jnp.zeros((BLOCK, PAIR), jnp.float32)
        logs = jnp.zeros((BLOCK, PAIR), jnp.float32)
        for head in range(PAIR // head_dim):
            mine = lane // head_dim == head
            scores = masked_scores(lanes_of(wide_query, mine), key, first)
            top = jnp.max(scores, axis=-1, keepdims=True)
            powers = jnp.exp(scores - top)
            total = jnp.sum(powers, axis=-1, keepdims=True)
            probs = (powers * (1.0 / total)).astype(jnp.bfloat16)
            mixed = jnp.where(mine, dot_plain(probs, value), mixed)
            logs = jnp.where(mine, top + jnp.log(total), logs)
        mixed_ref[rows, here] = mixed.astype(jnp.bfloat16)
        log_ref[rows, here] = logs


class Share:
    def __init__(self, held, sems, dp_count):
        self.held, self.steps = held, dp_count // 2
        self.sems, self.dp_count = sems, dp_count
        self.me = lax.axis_index("dp")
        self.other = self.me + 1 - 2 * lax.rem(self.me, 2)

    def block(self, of, i):
        return lax.rem(of + self.dp_count - 2 * i, self.dp_count)

    def across(self, i):
        to = lax.rem(self.me + 2 * i, self.dp_count)
        mine = self.held.at[self.me]
        return send(mine, mine, self.sems.at[0, i], self.sems.at[1, i], dp=to)

    def within(self, i):
        piece = self.held.at[self.block(self.me, i)]
        return send(piece, piece, self.sems.at[2, i], self.sems.at[3, i], dp=self.other)

    def start(self):
        for i in range(1, self.steps):
            self.across(i).start()
        self.within(0).start()

    def relay(self):
        for i in range(1, self.steps):
            at = self.block(self.me, i)
            piece = self.held.at[at]
            send(piece, piece, self.sems.at[0, i], self.sems.at[1, i], dp=at).wait_recv()
            self.within(i).start()

    def finish(self):
        for i in range(self.steps):
            piece = self.held.at[self.block(self.other, i)]
            send(piece, piece, self.sems.at[2, i], self.sems.at[3, i], dp=self.other).wait_recv()

    def drain(self):
        for i in range(self.steps):
            if i:
                self.across(i).wait_send()
            self.within(i).wait_send()


def front_kernel(
    dp_count,
    head_dim,
    tokens_ref,
    cot_ref,
    own_target_ref,
    qkv_a_ref,
    qkv_b_ref,
    out_a_ref,
    out_b_ref,
    gains_ref,
    grads_ref,
    target_ref,
    wq_ref,
    wo_ref,
    first_ref,
    proj_ref,
    log_ref,
    mixed_ref,
    middle_ref,
    second_ref,
    held,
    slots,
    hop,
    out_parts,
    mixed_all,
    line_send,
    line_recv,
    send_sem,
    recv_sem,
    local_sem,
    target_send,
    target_recv,
    near_send,
    near_recv,
    mix_send,
    mix_recv,
    q_sems,
    o_sems,
):
    line = held.shape[0]
    experts, _, _, per, _ = grads_ref.shape
    rows = tokens_ref.shape[0]
    me, place = lax.axis_index("dp"), lax.axis_index("tensor")
    order = block_order(place)
    mate, across, last = order[1], lax.rem(place + 2, line), line - 1 - place
    part = lax.rem(place, 2)
    wide = proj_ref.shape[1] // 3
    greet(dp_count, line)

    near = [
        send(qkv_b_ref, hop, near_send.at[0], near_recv.at[0], tensor=across),
        send(out_a_ref, out_parts.at[1], near_send.at[1], near_recv.at[1], tensor=mate),
        send(out_b_ref, out_parts.at[0], near_send.at[2], near_recv.at[2], tensor=across),
        send(out_b_ref, out_parts.at[2], near_send.at[3], near_recv.at[3], tensor=last),
    ]
    for copy in near:
        copy.start()
    target_ref[place] = own_target_ref[...]

    def target_copy(i, at, to):
        return send(
            target_ref.at[at], target_ref.at[at], target_send.at[i], target_recv.at[i], tensor=to
        )

    for i in range(1, line):
        target_copy(i, place, lax.rem(place + i, line)).start()

    def first_rows(i, carry):
        values = tokens_ref[pl.ds(i * 128, 128), :].astype(jnp.float32)
        unit, _ = norm_stats(values)
        unit = unit * gains_ref[0:1, :] + gains_ref[1:2, :]
        first_ref[part, pl.ds(i * 128, 128), :] = unit.astype(jnp.bfloat16)
        return carry

    lax.fori_loop(0, rows // 128, first_rows, 0)
    first_copy = send(
        first_ref.at[part], first_ref.at[part], near_send.at[4], near_recv.at[4], tensor=mate
    )
    first_copy.start()
    along = Line(cot_ref, held, line_send, line_recv)
    along.start()
    near[0].wait_recv()
    for kind in range(3):
        base = kind * wide
        wq_ref[me, :, base : base + PAIR] = qkv_a_ref[:, base : base + PAIR]
        wq_ref[me, :, base + PAIR : base + wide] = (
            qkv_a_ref[:, base + PAIR : base + wide].astype(jnp.float32)
            + hop[kind].astype(jnp.float32)
        ).astype(jnp.bfloat16)
    share_q = Share(wq_ref, q_sems, dp_count)
    share_q.start()
    for copy in near[1:]:
        copy.wait_recv()
    for group, (a, b) in enumerate(((out_a_ref[...], 0), (out_parts[1], 2))):
        base = group * wide
        a = a.astype(jnp.float32)
        b = out_parts[b].astype(jnp.float32)
        wo_ref[me, :, base : base + PAIR] = a[:, :PAIR].astype(jnp.bfloat16)
        wo_ref[me, :, base + PAIR : base + 2 * PAIR] = (a[:, PAIR:] + b[:, :PAIR]).astype(
            jnp.bfloat16
        )
        wo_ref[me, :, base + 2 * PAIR : base + wide] = b[:, PAIR:].astype(jnp.bfloat16)
    share_o = Share(wo_ref, o_sems, dp_count)
    share_o.start()
    share_q.relay()

    plane = Plane(
        lambda step, to: slots.at[step, pl.ds(to * experts, experts)],
        lambda step, at: grads_ref.at[:, step, at],
        send_sem,
        recv_sem,
        local_sem,
        dp_count,
    )

    def dispatch(step):
        if step:
            along.take(step)
        source = cot_ref if step == 0 else held.at[order[step]]
        dispatch_block(source, target_ref, order[step], slots, step, per)
        plane.start(step)

    dispatch(0)
    share_o.relay()
    share_q.finish()
    send(
        first_ref.at[1 - part], first_ref.at[1 - part], near_send.at[4], near_recv.at[4], tensor=mate
    ).wait_recv()

    def project(i, carry):
        values = first_ref[i // 2, pl.ds(lax.rem(i, 2) * (rows // 2), rows // 2), :]
        weights = wq_ref[...].reshape(-1, 3 * wide)
        proj_ref[pl.ds(i * (rows // 2), rows // 2), :] = dot_plain(values, weights).astype(
            jnp.bfloat16
        )
        return carry

    lax.fori_loop(0, 4, project, 0)
    for i in range(1, line):
        target_copy(i, lax.rem(place + line - i, line), lax.rem(place + line - i, line)).wait_recv()

    def mix_copy(pair):
        here = pl.ds(pair * PAIR, PAIR)
        return send(
            mixed_all.at[pl.ds((1 - part) * rows, rows), here],
            mixed_ref.at[1, :, here],
            mix_send.at[pair],
            mix_recv.at[pair],
            tensor=mate,
        )

    for pair in range(wide // PAIR):
        dispatch(pair + 1)
        attend_pair(proj_ref, mixed_all, log_ref, pair, head_dim)
        mix_copy(pair).start()
    mixed_ref[0] = mixed_all[pl.ds(part * rows, rows), :]
    share_o.finish()
    for pair in range(wide // PAIR):
        mix_copy(pair).wait_recv()

    def finish_rows(i, carry):
        here = pl.ds(i * 128, 128)
        total = tokens_ref[here, :].astype(jnp.float32)
        total += dot_rows(mixed_ref[0, here, :], wo_ref[:, :, :wide].reshape(-1, wide)) + dot_rows(
            mixed_ref[1, here, :], wo_ref[:, :, wide:].reshape(-1, wide)
        )
        middle_ref[here, :] = total
        unit, _ = norm_stats(total)
        second_ref[here, :] = (unit * gains_ref[2:3, :] + gains_ref[3:4, :]).astype(jnp.bfloat16)
        return carry

    lax.fori_loop(0, rows // 128, finish_rows, 0)
    along.finish()
    share_q.drain()
    share_o.drain()
    for copy in near:
        copy.wait_send()
    first_copy.wait_send()
    for i in range(1, line):
        target_copy(i, place, lax.rem(place + i, line)).wait_send()
    for pair in range(wide // PAIR):
        mix_copy(pair).wait_send()
    for step in range(line):
        plane.wait_recv(step)
        plane.wait_send(step)


def run_front(tokens, cotangent, target, weights, gains, sizes):
    dp_count, line, experts, per, head_dim = sizes
    rows, width = tokens.shape
    qkv_a, qkv_b, out_a, out_b = weights
    share, columns = qkv_a.shape
    wide = columns // 3
    low, dma = jnp.bfloat16, pltpu.SemaphoreType.DMA
    whole, far = pl.BlockSpec(memory_space=pltpu.VMEM), pl.BlockSpec(memory_space=pl.ANY)
    shape = jax.ShapeDtypeStruct
    return pl.pallas_call(
        functools.partial(front_kernel, dp_count, head_dim),
        in_specs=[whole] * 8,
        out_specs=[far] + [whole] * 9,
        out_shape=[
            shape((experts, line, dp_count, per, width), low),
            shape((line,) + target.shape, jnp.int32),
            shape((dp_count, share, columns), low),
            shape((dp_count, share, 2 * wide), low),
            shape((2, rows, width), low),
            shape((2 * rows, columns), low),
            shape((2 * rows, wide), jnp.float32),
            shape((2, rows, wide), low),
            shape((rows, width), jnp.float32),
            shape((rows, width), low),
        ],
        scratch_shapes=[
            pltpu.VMEM((line, rows, width), low),
            pltpu.VMEM((line, dp_count * experts, per, width), low),
            pltpu.VMEM(qkv_b.shape, low),
            pltpu.VMEM((3,) + out_b.shape, low),
            pltpu.VMEM((2 * rows, wide), low),
            dma((line + 1,)),
            dma((line,)),
            dma((line, dp_count)),
            dma((line, dp_count)),
            dma((line,)),
            dma((line,)),
            dma((line,)),
            dma((5,)),
            dma((5,)),
            dma((wide // PAIR,)),
            dma((wide // PAIR,)),
            dma((4, dp_count // 2)),
            dma((4, dp_count // 2)),
        ],
        compiler_params=pltpu.CompilerParams(
            collective_id=1, has_side_effects=True, vmem_limit_bytes=56 << 20
        ),
        name="front",
    )(tokens, cotangent, target, *weights, gains)


def attend_back_pair(proj_ref, log_ref, grad_ref, out_ref, dk_sum, dv_sum, pair, head_dim):
    length, wide = proj_ref.shape[0], proj_ref.shape[1] // 3
    here = pl.ds(pair * PAIR, PAIR)
    key_at, value_at = pl.ds(wide + pair * PAIR, PAIR), pl.ds(2 * wide + pair * PAIR, PAIR)
    lane = lax.broadcasted_iota(jnp.int32, (BLOCK, PAIR), 1)
    for first in reversed(range(0, length, BLOCK)):
        rows, seen = pl.ds(first, BLOCK), pl.ds(0, first + BLOCK)
        lanes_seen = lax.broadcasted_iota(jnp.int32, (first + BLOCK, PAIR), 1)
        wide_query = proj_ref[rows, here].astype(jnp.float32) * SCORE_SCALE
        key, value, grad = proj_ref[seen, key_at], proj_ref[seen, value_at], grad_ref[rows, here]
        query, wide_grad = wide_query.astype(jnp.bfloat16), grad.astype(jnp.float32)
        dq = jnp.zeros((BLOCK, PAIR), jnp.float32)
        dk = jnp.zeros((first + BLOCK, PAIR), jnp.float32)
        dv = jnp.zeros((first + BLOCK, PAIR), jnp.float32)
        for head in range(PAIR // head_dim):
            mine = lane // head_dim == head
            there = lanes_seen // head_dim == head
            scores = masked_scores(lanes_of(wide_query, mine), key, first)
            log_total = log_ref[rows, pl.ds(pair * PAIR + head * head_dim, 1)]
            probs = jnp.exp(scores - log_total)
            prob_grad = dot_rows(lanes_of(wide_grad, mine), value)
            inner = jnp.sum(probs * prob_grad, axis=-1, keepdims=True)
            score_grad = (probs * (prob_grad - inner)).astype(jnp.bfloat16)
            dq = jnp.where(mine, dot_plain(score_grad, key), dq)
            dk = jnp.where(there, dot_columns(score_grad, query), dk)
            dv = jnp.where(there, dot_columns(probs.astype(jnp.bfloat16), grad), dv)
        out_ref[rows, here] = (dq * SCORE_SCALE).astype(jnp.bfloat16)
        if first + BLOCK == length:
            dk_sum[...] = dk
            dv_sum[...] = dv
        else:
            dk_sum[seen, :] += dk
            dv_sum[seen, :] += dv
    out_ref[:, key_at] = dk_sum[...].astype(jnp.bfloat16)
    out_ref[:, value_at] = dv_sum[...].astype(jnp.bfloat16)


class Pieces:
    def __init__(self, source, held, sems, dp_count):
        self.source, self.held, self.sems, self.dp_count = source, held, sems, dp_count
        self.me = lax.axis_index("dp")

    def copy(self, i, to):
        return send(
            self.source.at[to],
            self.held.at[self.me],
            self.sems.at[0, i],
            self.sems.at[1, i],
            dp=to,
        )

    def start(self):
        def one(i, carry):
            self.copy(i, lax.rem(self.me + i, self.dp_count)).start()
            return carry

        lax.fori_loop(1, self.dp_count, one, 0)

    def total(self, sum_ref):
        sum_ref[...] = self.source[self.me].astype(jnp.float32)

        def one(i, carry):
            at = lax.rem(self.me + self.dp_count - i, self.dp_count)
            send(
                self.source.at[self.me],
                self.held.at[at],
                self.sems.at[0, i],
                self.sems.at[1, i],
                dp=at,
            ).wait_recv()
            sum_ref[...] += self.held[at].astype(jnp.float32)
            return carry

        lax.fori_loop(1, self.dp_count, one, 0)

    def drain(self):
        def one(i, carry):
            self.copy(i, lax.rem(self.me + i, self.dp_count)).wait_send()
            return carry

        lax.fori_loop(1, self.dp_count, one, 0)


def norm_back_rows(grad, values, gain):
    unit, inv_scale = norm_stats(values)
    scaled = grad * gain
    mean_plain = jnp.mean(scaled, axis=-1, keepdims=True)
    mean_unit = jnp.mean(scaled * unit, axis=-1, keepdims=True)
    change = inv_scale * (scaled - mean_plain - unit * mean_unit)
    return (
        change,
        jnp.sum(grad * unit, axis=0, keepdims=True),
        jnp.sum(grad, axis=0, keepdims=True),
    )


def back_kernel(
    dp_count,
    head_dim,
    back_ref,
    cot_ref,
    tokens_ref,
    middle_ref,
    gains_ref,
    target_ref,
    wq_ref,
    wo_ref,
    first_ref,
    proj_ref,
    log_ref,
    mixed_ref,
    result_ref,
    out_ref,
    grad_tokens_ref,
    sums_ref,
    d_qkv_ref,
    d_out_ref,
    returned,
    stage,
    far,
    middle_grad,
    middle_low,
    mixed_grad,
    mixed_sent,
    qkv_grad,
    dk_sum,
    dv_sum,
    out_pieces,
    out_held,
    out_sum,
    out_sent,
    out_near,
    qkv_pieces,
    qkv_held,
    qkv_sum,
    qkv_sent,
    qkv_near,
    first_sent,
    first_near,
    line_sums,
    plane_sums,
    send_sem,
    recv_sem,
    local_sem,
    far_send,
    far_recv,
    near_send,
    near_recv,
    out_sems,
    qkv_sems,
    line_send,
    line_recv,
    plane_send,
    plane_recv,
):
    rows, width = tokens_ref.shape
    experts, line, _, per, _ = result_ref.shape
    wide = proj_ref.shape[1] // 3
    share = wq_ref.shape[1]
    me, place = lax.axis_index("dp"), lax.axis_index("tensor")
    order = block_order(place)
    mate, across, last = order[1], lax.rem(place + 2, line), line - 1 - place
    part = lax.rem(place, 2)
    greet(dp_count, line)
    plane = Plane(
        lambda step, to: result_ref.at[:, order[step], to],
        lambda step, at: returned.at[step, pl.ds(at * experts, experts)],
        send_sem,
        recv_sem,
        local_sem,
        dp_count,
    )
    for step in range(line):
        plane.start(step)
    results = Return(plane, returned, target_ref, stage, far, far_send, far_recv, per)
    sums_ref[...] = jnp.zeros_like(sums_ref)

    def second_rows(i, carry):
        here = pl.ds(i * 128, 128)
        change, gain_sum, bias_sum = norm_back_rows(
            back_ref[here, :], middle_ref[here, :], gains_ref[2:3, :]
        )
        change = cot_ref[here, :].astype(jnp.float32) + change
        middle_grad[here, :] = change
        middle_low[here, :] = change.astype(jnp.bfloat16)
        sums_ref[2:3, :] += gain_sum
        sums_ref[3:4, :] += bias_sum
        return carry

    lax.fori_loop(0, rows // 128, second_rows, 0)
    mixed_sent[...] = dot_plain(
        middle_low[...], wo_ref[:, :, wide:].reshape(width, wide)
    ).astype(jnp.bfloat16)
    mixed_copy = send(
        mixed_sent,
        mixed_grad.at[pl.ds(part * rows, rows)],
        near_send.at[0],
        near_recv.at[0],
        tensor=mate,
    )
    mixed_copy.start()
    mixed_grad[pl.ds(part * rows, rows), :] = dot_plain(
        middle_low[...], wo_ref[:, :, :wide].reshape(width, wide)
    ).astype(jnp.bfloat16)
    for group in range(2):
        product_ = dot_columns(middle_low[...], mixed_ref[group]).astype(jnp.bfloat16)
        out_pieces[:, :, group * wide : (group + 1) * wide] = product_.reshape(
            dp_count, share, wide
        )
    outs = Pieces(out_pieces, out_held, out_sems, dp_count)
    outs.start()
    send(
        mixed_sent,
        mixed_grad.at[pl.ds((1 - part) * rows, rows)],
        near_send.at[0],
        near_recv.at[0],
        tensor=mate,
    ).wait_recv()
    for pair in range(wide // PAIR):
        attend_back_pair(
            proj_ref, log_ref, mixed_grad, qkv_grad, dk_sum, dv_sum, pair, head_dim
        )
    first_sent[...] = dot_rows(
        qkv_grad[pl.ds((1 - part) * rows, rows), :], wq_ref[...].reshape(width, 3 * wide)
    ).astype(jnp.bfloat16)
    first_copy = send(first_sent, first_near, near_send.at[1], near_recv.at[1], tensor=mate)
    first_copy.start()
    middle_rows = width // 2
    for half in range(2):
        total = dot_columns(
            first_ref[0, :, half * middle_rows : (half + 1) * middle_rows], qkv_grad[:rows, :]
        )
        total += dot_columns(
            first_ref[1, :, half * middle_rows : (half + 1) * middle_rows], qkv_grad[rows:, :]
        )
        qkv_pieces[pl.ds(half * dp_count // 2, dp_count // 2)] = total.astype(
            jnp.bfloat16
        ).reshape(dp_count // 2, share, 3 * wide)
    qkvs = Pieces(qkv_pieces, qkv_held, qkv_sems, dp_count)
    qkvs.start()

    outs.total(out_sum)
    for i, base in enumerate((wide, PAIR, wide + PAIR)):
        out_sent[i] = out_sum[:, base : base + 2 * PAIR].astype(jnp.bfloat16)
    out_copies = [
        send(out_sent.at[i], out_near.at[i], near_send.at[3 + i], near_recv.at[3 + i], tensor=to)
        for i, to in enumerate((mate, across, last))
    ]
    for copy in out_copies:
        copy.start()

    def first_rows(i, carry):
        here = pl.ds(i * 128, 128)
        grad = dot_rows(
            qkv_grad[pl.ds(part * rows + i * 128, 128), :], wq_ref[...].reshape(width, 3 * wide)
        )
        grad += first_near[here, :].astype(jnp.float32)
        change, gain_sum, bias_sum = norm_back_rows(
            grad, tokens_ref[here, :].astype(jnp.float32), gains_ref[0:1, :]
        )
        grad_tokens_ref[here, :] = (middle_grad[here, :] + change).astype(jnp.bfloat16)
        sums_ref[0:1, :] += gain_sum
        sums_ref[1:2, :] += bias_sum
        return carry

    first_copy.wait_recv()
    lax.fori_loop(0, rows // 128, first_rows, 0)
    line_sums[place] = sums_ref[...]

    def line_copy(i, at, to):
        return send(line_sums.at[at], line_sums.at[at], line_send.at[i], line_recv.at[i], tensor=to)

    for i in range(1, line):
        line_copy(i, place, lax.rem(place + i, line)).start()
    plane.wait_recv(0)
    middle_grad[...] = middle_ref[...] + results.collect(0)
    results.step(1)
    for i in range(1, line):
        at = lax.rem(place + line - i, line)
        line_copy(i, at, at).wait_recv()
    plane_sums[me] = (line_sums[0] + line_sums[1]) + (line_sums[2] + line_sums[3])

    def plane_copy(i, at, to):
        return send(
            plane_sums.at[at], plane_sums.at[at], plane_send.at[i], plane_recv.at[i], dp=to
        )

    def plane_start(i, carry):
        plane_copy(i, me, lax.rem(me + i, dp_count)).start()
        return carry

    lax.fori_loop(1, dp_count, plane_start, 0)
    results.step(2)
    qkvs.total(qkv_sum)
    for kind in range(3):
        base = kind * wide + PAIR
        qkv_sent[kind] = qkv_sum[:, base : base + 2 * PAIR].astype(jnp.bfloat16)
    qkv_copy = send(qkv_sent, qkv_near, near_send.at[2], near_recv.at[2], tensor=across)
    qkv_copy.start()
    results.step(3)

    def plane_wait(i, carry):
        at = lax.rem(me + dp_count - i, dp_count)
        plane_copy(i, at, at).wait_recv()
        return carry

    lax.fori_loop(1, dp_count, plane_wait, 0)
    sums_ref[...] = plane_sums[0]

    def plane_add(i, carry):
        sums_ref[...] += plane_sums[i]
        return carry

    lax.fori_loop(1, dp_count, plane_add, 0)
    for copy in out_copies:
        copy.wait_recv()
    arrived = [out_near[i].astype(jnp.float32) for i in range(3)]
    d_out_ref[:, :PAIR] = (
        out_sum[:, :PAIR] + arrived[0][:, :PAIR] + arrived[1][:, PAIR:] + arrived[2][:, PAIR:]
    )
    turned = pltpu.roll(arrived[1][:, :PAIR] + arrived[2][:, :PAIR], head_dim, 1)
    d_out_ref[:, PAIR:] = out_sum[:, PAIR : 2 * PAIR] + arrived[0][:, PAIR:] + turned
    qkv_copy.wait_recv()
    for kind in range(3):
        base, at = kind * wide, kind * 2 * PAIR
        come = qkv_near[kind].astype(jnp.float32)
        d_qkv_ref[:, at : at + PAIR] = qkv_sum[:, base : base + PAIR] + come[:, PAIR:]
        d_qkv_ref[:, at + PAIR : at + 2 * PAIR] = qkv_sum[
            :, base + PAIR : base + 2 * PAIR
        ] + pltpu.roll(come[:, :PAIR], head_dim, 1)
    results.wait()
    out_ref[...] = (
        middle_grad[...] + far[0].astype(jnp.float32) + far[1].astype(jnp.float32)
    ).astype(jnp.bfloat16)
    results.drain()
    outs.drain()
    qkvs.drain()
    mixed_copy.wait_send()
    first_copy.wait_send()
    qkv_copy.wait_send()
    for copy in out_copies:
        copy.wait_send()
    for i in range(1, line):
        line_copy(i, place, lax.rem(place + i, line)).wait_send()

    def plane_drain(i, carry):
        plane_copy(i, me, lax.rem(me + i, dp_count)).wait_send()
        return carry

    lax.fori_loop(1, dp_count, plane_drain, 0)


def run_back(dp_count, head_dim, *args):
    tokens, wq, proj, result = args[2], args[6], args[9], args[12]
    rows, width = tokens.shape
    experts, line, _, per, _ = result.shape
    share = wq.shape[1]
    wide = proj.shape[1] // 3
    low, wider, dma = jnp.bfloat16, jnp.float32, pltpu.SemaphoreType.DMA
    whole, far = pl.BlockSpec(memory_space=pltpu.VMEM), pl.BlockSpec(memory_space=pl.ANY)
    shape, vmem = jax.ShapeDtypeStruct, pltpu.VMEM
    return pl.pallas_call(
        functools.partial(back_kernel, dp_count, head_dim),
        in_specs=[whole] * 12 + [far],
        out_specs=[whole] * 5,
        out_shape=[
            shape((rows, width), low),
            shape((rows, width), low),
            shape((8, width), wider),
            shape((share, 6 * PAIR), wider),
            shape((share, 2 * PAIR), wider),
        ],
        scratch_shapes=[
            vmem((line, dp_count * experts, per, width), low),
            vmem((line, rows, width), low),
            vmem((line, rows, width), low),
            vmem((rows, width), wider),
            vmem((rows, width), low),
            vmem((2 * rows, wide), low),
            vmem((rows, wide), low),
            vmem((2 * rows, 3 * wide), low),
            vmem((2 * rows, PAIR), wider),
            vmem((2 * rows, PAIR), wider),
            vmem((dp_count, share, 2 * wide), low),
            vmem((dp_count, share, 2 * wide), low),
            vmem((share, 2 * wide), wider),
            vmem((3, share, 2 * PAIR), low),
            vmem((3, share, 2 * PAIR), low),
            vmem((dp_count, share, 3 * wide), low),
            vmem((dp_count, share, 3 * wide), low),
            vmem((share, 3 * wide), wider),
            vmem((3, share, 2 * PAIR), low),
            vmem((3, share, 2 * PAIR), low),
            vmem((rows, width), low),
            vmem((rows, width), low),
            vmem((line, 8, width), wider),
            vmem((dp_count, 8, width), wider),
            dma((line, dp_count)),
            dma((line, dp_count)),
            dma((line,)),
            dma((line + 1,)),
            dma((line + 1,)),
            dma((6,)),
            dma((6,)),
            dma((2, dp_count)),
            dma((2, dp_count)),
            dma((line,)),
            dma((line,)),
            dma((dp_count,)),
            dma((dp_count,)),
        ],
        compiler_params=pltpu.CompilerParams(
            collective_id=2, has_side_effects=True, vmem_limit_bytes=58 << 20
        ),
        name="back",
    )(*args)


def on_device(
    tokens,
    token_ids,
    hash_table,
    ln1_gain,
    ln1_bias,
    w_qkv,
    w_out,
    ln2_gain,
    ln2_bias,
    expert_in,
    expert_out,
    cotangent,
):
    low = jnp.bfloat16
    row_count, model_width = tokens.shape
    local_experts = expert_in.shape[0]
    dp_count = lax.axis_size("dp")
    line = lax.axis_size("tensor")
    head_dim = w_qkv.shape[2] // 3
    heads_shard = w_qkv.shape[1]

    experts_total = dp_count * local_experts
    capacity = 2 * row_count // experts_total
    slot_count = experts_total * capacity
    expert_of = jnp.take(hash_table, token_ids)
    one_hot = (expert_of[:, None] == jnp.arange(experts_total, dtype=jnp.int32)[None, :]).astype(
        jnp.int32
    )
    before = (
        lax.broadcasted_iota(jnp.int32, (row_count, row_count), 0)
        > lax.broadcasted_iota(jnp.int32, (row_count, row_count), 1)
    ).astype(low)
    earlier = jnp.dot(before, one_hot.astype(low), preferred_element_type=jnp.float32)
    slot_rank = jnp.sum(earlier.astype(jnp.int32) * one_hot, axis=1)
    target = jnp.where(slot_rank < capacity, expert_of * capacity + slot_rank, slot_count)
    own_target = jnp.broadcast_to(target[None, :], (8, row_count))

    share = w_qkv.shape[0]
    wide = 2 * heads_shard * head_dim
    by_kind = w_qkv.astype(low).reshape(share, heads_shard, 3, head_dim).transpose(0, 2, 1, 3)
    qkv_a = jnp.pad(by_kind.reshape(share, 3, -1), ((0, 0), (0, 0), (0, wide // 2)))
    qkv_b = jnp.concatenate([by_kind[:, :, -1:], by_kind[:, :, :-1]], axis=2).reshape(share, 3, -1)
    qkv_b = jnp.pad(qkv_b, ((0, 0), (0, 0), (head_dim, 0))).transpose(1, 0, 2)
    out_rows = w_out.astype(low).T
    out_a = jnp.pad(out_rows, ((0, 0), (0, head_dim)))
    out_b = jnp.concatenate([out_rows[:, -head_dim:], out_rows[:, :-head_dim]], axis=1)
    out_b = jnp.pad(out_b, ((0, 0), (head_dim, 0)))
    gains = jnp.pad(jnp.stack([ln1_gain, ln1_bias, ln2_gain, ln2_bias]), ((0, 4), (0, 0)))
    sizes = (dp_count, line, local_experts, capacity, head_dim)
    (
        grad_rows,
        targets,
        qkv_weight,
        out_weight,
        first_all,
        projected,
        log_total,
        mixed_pair,
        middle,
        second_low,
    ) = run_front(
        tokens,
        cotangent,
        own_target,
        (qkv_a.reshape(share, -1), qkv_b, out_a, out_b),
        gains,
        sizes,
    )
    second_grad, result, grad_expert_in, grad_expert_out = run_experts(
        second_low,
        targets,
        grad_rows,
        expert_in.astype(low),
        expert_out.astype(low),
        dp_count,
        line,
    )
    out, grad_tokens, sums, grad_qkv, grad_out = run_back(
        dp_count,
        head_dim,
        second_grad,
        cotangent,
        tokens,
        middle,
        gains,
        targets,
        qkv_weight,
        out_weight,
        first_all,
        projected,
        log_total,
        mixed_pair,
        result,
    )
    half = wide // 2
    grad_qkv = grad_qkv.reshape(share, 3, -1)[:, :, :half]
    grad_qkv = grad_qkv.reshape(share, 3, heads_shard, head_dim).transpose(0, 2, 1, 3)
    return (
        out,
        grad_tokens,
        sums[0],
        sums[1],
        grad_qkv.reshape(w_qkv.shape),
        grad_out[:, :half].T,
        sums[2],
        sums[3],
        grad_expert_in,
        grad_expert_out,
    )


def solution(mesh):
    rows = P(("dp", "tensor"), None)
    weights = (P("dp", "tensor", None), P("tensor", "dp"))
    experts = (P("dp", None, "tensor"), P("dp", "tensor", None))
    return jax.shard_map(
        on_device,
        mesh=mesh,
        in_specs=(rows, P(("dp", "tensor")), P(), P(), P(), *weights, P(), P(), *experts, rows),
        out_specs=(rows, rows, P(), P(), *weights, P(), P(), *experts),
        check_vma=False,
    )
```

```python
import functools

import jax
import jax.numpy as jnp
from jax import lax
from jax.experimental import pallas as pl
from jax.experimental.pallas import tpu as pltpu
from jax.sharding import PartitionSpec as P

LEN = 1024


EPSILON = 1e-05
SCORE_SCALE = 0.125
MASKED = -1e30
MESH = pl.DeviceIdType.MESH


def lanes_of(values, mask):
    return jnp.where(mask, values, 0.0).astype(jnp.bfloat16)


def dot_rows(left, right):
    return lax.dot_general(left, right, (((1,), (1,)), ((), ())), preferred_element_type=jnp.float32)


def dot_columns(left, right):
    return lax.dot_general(left, right, (((0,), (0,)), ((), ())), preferred_element_type=jnp.float32)


def dot_plain(left, right):
    return jnp.dot(left, right, preferred_element_type=jnp.float32)


def masked_scores(query, key, first):
    scores = dot_rows(query, key)
    rows, columns = scores.shape
    row = lax.broadcasted_iota(jnp.int32, (rows, rows), 0)
    column = lax.broadcasted_iota(jnp.int32, (rows, rows), 1)
    edge = jnp.where(row >= column, scores[:, first:], MASKED)
    return edge if first == 0 else jnp.concatenate([scores[:, :first], edge], axis=1)


PAIR = 128
BLOCK = 256


def block_order(place):
    half = place // 2
    return (place, 1 + 4 * half - place, 2 - half, 3 - 3 * half)


def greet(dp_count, line):
    me, place = lax.axis_index("dp"), lax.axis_index("tensor")
    barrier = pltpu.get_barrier_semaphore()

    def plane(i, carry):
        pl.semaphore_signal(
            barrier, 1, device_id={"dp": lax.rem(me + i, dp_count)}, device_id_type=MESH
        )
        return carry

    lax.fori_loop(1, dp_count, plane, 0)
    for i in range(1, line):
        pl.semaphore_signal(
            barrier, 1, device_id={"tensor": lax.rem(place + i, line)}, device_id_type=MESH
        )
    pl.semaphore_wait(barrier, dp_count + line - 2)


class Line:
    def __init__(self, own, held, send_sem, recv_sem):
        self.own, self.held, self.send_sem, self.recv_sem = own, held, send_sem, recv_sem
        self.place = lax.axis_index("tensor")
        self.order = block_order(self.place)
        self.last = held.shape[0] - 1

    def copy(self, source, block, index, to):
        return pltpu.make_async_remote_copy(
            src_ref=source,
            dst_ref=self.held.at[block],
            send_sem=self.send_sem.at[index],
            recv_sem=self.recv_sem.at[block],
            device_id={"tensor": to},
            device_id_type=MESH,
        )

    def left(self):
        return self.copy(self.own, self.place, 0, self.place - 1)

    def right(self):
        return self.copy(self.own, self.place, self.last + 1, self.place + 1)

    def onward(self, step):
        block = self.order[step]
        up = self.copy(self.held.at[block], block, step, self.place + 1)
        down = self.copy(self.held.at[block], block, step, self.place - 1)
        return (
            (jnp.logical_and(block < self.place, self.place < self.last), up),
            (jnp.logical_and(block > self.place, self.place > 0), down),
        )

    def start(self):
        pl.when(self.place > 0)(lambda: self.left().start())
        pl.when(self.place < self.last)(lambda: self.right().start())

    def take(self, step):
        block = self.order[step]
        self.copy(self.held.at[block], block, step, block).wait_recv()
        for needed, copy in self.onward(step):
            pl.when(needed)(copy.start)

    def finish(self):
        pl.when(self.place > 0)(lambda: self.left().wait_send())
        pl.when(self.place < self.last)(lambda: self.right().wait_send())
        for step in range(1, self.last + 1):
            for needed, copy in self.onward(step):
                pl.when(needed)(copy.wait_send)


def slot_matrix(target_ref, block, first, count):
    target = target_ref[block, 0:1, :]
    slot = lax.broadcasted_iota(jnp.int32, (count, target.shape[1]), 0) + first
    return jnp.where(slot == target, 1.0, 0.0).astype(jnp.bfloat16)


class Plane:
    def __init__(self, piece, place_of, send_sem, recv_sem, local_sem, dp_count):
        self.piece, self.place_of = piece, place_of
        self.send_sem, self.recv_sem, self.local_sem = send_sem, recv_sem, local_sem
        self.me, self.dp_count = lax.axis_index("dp"), dp_count

    def copy(self, step, i):
        to = lax.rem(self.me + i, self.dp_count)
        return pltpu.make_async_remote_copy(
            src_ref=self.piece(step, to),
            dst_ref=self.place_of(step, self.me),
            send_sem=self.send_sem.at[step, i],
            recv_sem=self.recv_sem.at[step, i],
            device_id={"dp": to},
            device_id_type=MESH,
        )

    def own(self, step):
        return pltpu.make_async_copy(
            self.piece(step, self.me), self.place_of(step, self.me), self.local_sem.at[step]
        )

    def start(self, step):
        def one(i, carry):
            self.copy(step, i).start()
            return carry

        lax.fori_loop(1, self.dp_count, one, 0)
        self.own(step).start()

    def wait_recv(self, step):
        def one(i, carry):
            here = lax.rem(self.me + self.dp_count - i, self.dp_count)
            pltpu.make_async_remote_copy(
                src_ref=self.piece(step, self.me),
                dst_ref=self.place_of(step, here),
                send_sem=self.send_sem.at[step, i],
                recv_sem=self.recv_sem.at[step, i],
                device_id={"dp": here},
                device_id_type=MESH,
            ).wait_recv()
            return carry

        lax.fori_loop(1, self.dp_count, one, 0)
        self.own(step).wait()

    def wait_send(self, step):
        def one(i, carry):
            self.copy(step, i).wait_send()
            return carry

        lax.fori_loop(1, self.dp_count, one, 0)


def dispatch_block(rows, target_ref, block, slots, step, per):
    groups = slots.shape[1]
    chunk = 256 // per

    def one(i, carry):
        chosen = slot_matrix(target_ref, block, i * 256, 256)
        values = dot_plain(chosen, rows[...]).astype(jnp.bfloat16)
        slots[step, pl.ds(i * chunk, chunk)] = values.reshape((chunk, per) + values.shape[1:])
        return carry

    lax.fori_loop(0, groups // chunk, one, 0)


def collect_block(slots, target_ref, block, step, per):
    groups = slots.shape[1]
    chunk = 256 // per
    total = None
    for i in range(groups // chunk):
        chosen = slot_matrix(target_ref, block, i * 256, 256)
        values = slots[step, pl.ds(i * chunk, chunk)]
        term = dot_columns(chosen, values.reshape((256,) + values.shape[2:]))
        total = term if total is None else total + term
    return total


def send(source, there, send_sem, recv_sem, **to):
    return pltpu.make_async_remote_copy(
        src_ref=source,
        dst_ref=there,
        send_sem=send_sem,
        recv_sem=recv_sem,
        device_id=to,
        device_id_type=MESH,
    )


class Return:
    def __init__(self, plane, returned, target_ref, stage, far, far_send, far_recv, per):
        self.plane, self.returned, self.target_ref = plane, returned, target_ref
        self.stage, self.far, self.per = stage, far, per
        self.far_send, self.far_recv = far_send, far_recv
        self.place = lax.axis_index("tensor")
        self.order = block_order(self.place)
        self.mine = lax.rem(self.place, 2)
        self.half = stage.shape[1] // 2
        self.kept = pl.ds(self.mine * self.half, self.half)
        self.passed = pl.ds((1 - self.mine) * self.half, self.half)

    def mate_copy(self):
        return send(
            self.stage.at[1],
            self.far.at[0],
            self.far_send.at[0],
            self.far_recv.at[0],
            tensor=self.order[1],
        )

    def half_copy(self, step, part):
        return send(
            self.stage.at[step, part],
            self.far.at[step, part],
            self.far_send.at[step - 1],
            self.far_recv.at[step - 1],
            tensor=self.order[1],
        )

    def owner_copy(self, step, part, at):
        return send(
            self.stage.at[step, part],
            self.far.at[1, part],
            self.far_send.at[step + 1],
            self.far_recv.at[3 + at],
            tensor=self.order[step],
        )

    def collect(self, step):
        return collect_block(self.returned, self.target_ref, self.order[step], step, self.per)

    def begin(self, step, then=None):
        self.plane.wait_recv(step)
        if then is not None:
            self.plane.start(then)
        self.stage[step] = self.collect(step).astype(jnp.bfloat16)
        if step == 1:
            self.mate_copy().start()
        else:
            self.half_copy(step, self.passed).start()

    def end(self, step):
        self.half_copy(step, self.kept).wait_recv()
        self.stage[step, self.kept] = (
            self.stage[step, self.kept].astype(jnp.float32)
            + self.far[step, self.kept].astype(jnp.float32)
        ).astype(jnp.bfloat16)
        self.owner_copy(step, self.kept, self.mine).start()

    def wait(self):
        self.mate_copy().wait()
        self.owner_copy(2, pl.ds(0, self.half), 0).wait_recv()
        self.owner_copy(2, pl.ds(self.half, self.half), 1).wait_recv()

    def drain(self):
        for step in range(4):
            self.plane.wait_send(step)
        for step in (2, 3):
            self.half_copy(step, self.passed).wait_send()
            self.owner_copy(step, self.kept, self.mine).wait_send()


GELU_SCALE = 0.7978845608028654
GELU_CUBE = 0.044715


def expert_kernel(
    dp_count,
    rows_ref,
    target_ref,
    grads_ref,
    wide_in_ref,
    wide_out_ref,
    back_ref,
    result_ref,
    d_in_ref,
    d_out_ref,
    held,
    slots,
    arrived,
    grads,
    active,
    hidden_grad,
    sent_back,
    returned,
    far,
    w_in_ref,
    w_out_ref,
    loaded,
    line_send,
    line_recv,
    send_sem,
    recv_sem,
    back_send,
    back_recv,
    local_sem,
    back_local,
    grad_sem,
    far_send,
    far_recv,
    out_sem,
    load_sem,
):
    line = held.shape[0]
    experts, _, _, per, width = arrived.shape
    place, me = lax.axis_index("tensor"), lax.axis_index("dp")
    order = block_order(place)
    rows_of = dp_count * per
    greet(dp_count, line)
    along = Line(rows_ref, held, line_send, line_recv)
    along.start()
    out_plane = Plane(
        lambda step, to: slots.at[step, pl.ds(to * experts, experts)],
        lambda step, at: arrived.at[:, step, at],
        send_sem,
        recv_sem,
        local_sem,
        dp_count,
    )
    back_plane = Plane(
        lambda step, to: sent_back.at[:, step, to],
        lambda step, at: returned.at[step, pl.ds(at * experts, experts)],
        back_send,
        back_recv,
        back_local,
        dp_count,
    )

    def grad_copy(step):
        return pltpu.make_async_copy(
            grads_ref.at[:, step], grads.at[:, step % 2], grad_sem.at[step]
        )

    def dispatch(step):
        if step:
            along.take(step)
        source = rows_ref if step == 0 else held.at[order[step]]
        dispatch_block(source, target_ref, order[step], slots, step, per)
        out_plane.start(step)

    half = dp_count // 2

    def forward(step):
        grad_copy(step).wait()
        for expert in range(experts):

            def one(i, carry):
                part = pl.ds(i * half, half)
                x = arrived[expert, step, part].reshape(half * per, width)
                g = grads[expert, step % 2, part].reshape(half * per, width)
                hidden = dot_plain(x, w_in_ref[expert])
                inner = GELU_SCALE * (hidden + GELU_CUBE * hidden * hidden * hidden)
                bend = jnp.tanh(inner)
                gate = 0.5 * (1.0 + bend)
                active[expert, part] = (
                    (hidden * gate).astype(jnp.bfloat16).reshape(half, per, -1)
                )
                slope = gate + 0.5 * hidden * (1.0 - bend * bend) * (
                    GELU_SCALE * (1.0 + 3.0 * GELU_CUBE * hidden * hidden)
                )
                change = (dot_rows(g, w_out_ref[expert]) * slope).astype(jnp.bfloat16)
                hidden_grad[expert, part] = change.reshape(half, per, -1)
                row_grad = dot_rows(change, w_in_ref[expert]).astype(jnp.bfloat16)
                sent_back[expert, step, part] = row_grad.reshape(half, per, width)
                return carry

            lax.fori_loop(0, 2, one, 0)
        if step > 1:
            back_plane.start(step)

    def result_copy(step, expert):
        return pltpu.make_async_copy(
            slots.at[step, pl.ds(expert * dp_count, dp_count)],
            result_ref.at[expert, order[step]],
            out_sem.at[step, expert],
        )

    def later(step):
        out_plane.wait_send(step)
        for expert in range(experts):
            a = active[expert].reshape(rows_of, -1)
            result = dot_plain(a, w_out_ref[expert]).astype(jnp.bfloat16)
            slots[step, pl.ds(expert * dp_count, dp_count)] = result.reshape(
                dp_count, per, width
            )
            result_copy(step, expert).start()
            g = grads[expert, step % 2].reshape(rows_of, width)
            x = arrived[expert, step].reshape(rows_of, width)
            change = hidden_grad[expert].reshape(rows_of, -1)
            if step == 0:
                d_out_ref[expert] = dot_columns(a, g)
                d_in_ref[expert] = dot_columns(x, change)
            else:
                d_out_ref[expert] += dot_columns(a, g)
                d_in_ref[expert] += dot_columns(x, change)

    home = Return(back_plane, returned, target_ref, held, far, far_send, far_recv, per)
    chunk = loaded.shape[1]
    loads = [
        (wide, narrow, expert, i * chunk)
        for wide, narrow in ((wide_in_ref, w_in_ref), (wide_out_ref, w_out_ref))
        for expert in range(experts)
        for i in range(narrow.shape[1] // chunk)
    ]

    def load(i):
        wide, _, expert, first = loads[i]
        return pltpu.make_async_copy(
            wide.at[expert, pl.ds(first, chunk)], loaded.at[i % 2], load_sem.at[i % 2]
        )

    load(0).start()
    grad_copy(0).start()
    grad_copy(1).start()
    dispatch(0)
    for i, (_, narrow, expert, first) in enumerate(loads):
        if i + 1 < len(loads):
            load(i + 1).start()
        load(i).wait()
        narrow[expert, pl.ds(first, chunk), :] = loaded[i % 2].astype(jnp.bfloat16)
    for step in range(line):
        if step + 1 < line:
            dispatch(step + 1)
        out_plane.wait_recv(step)
        forward(step)
        later(step)
        if step + 2 < line:
            grad_copy(step + 2).start()
    along.finish()
    home.begin(2, 1)
    home.end(2)
    home.begin(3, 0)
    home.end(3)
    home.begin(1)
    back_plane.wait_recv(0)
    back_ref[...] = home.collect(0)
    home.wait()
    back_ref[...] += far[0].astype(jnp.float32) + far[1].astype(jnp.float32)
    home.drain()
    for step in range(line):
        for expert in range(experts):
            result_copy(step, expert).wait()


def run_experts(rows, targets, grads, w_in, w_out, dp_count, line):
    experts, _, _, per, width = grads.shape
    units = w_in.shape[2]
    low, dma = jnp.bfloat16, pltpu.SemaphoreType.DMA
    whole, far = pl.BlockSpec(memory_space=pltpu.VMEM), pl.BlockSpec(memory_space=pl.ANY)
    groups = dp_count * experts
    return pl.pallas_call(
        functools.partial(expert_kernel, dp_count),
        in_specs=[whole, whole, far, far, far],
        out_specs=[whole, far, whole, whole],
        out_shape=[
            jax.ShapeDtypeStruct(rows.shape, jnp.float32),
            jax.ShapeDtypeStruct(grads.shape, low),
            jax.ShapeDtypeStruct((experts, width, units), jnp.float32),
            jax.ShapeDtypeStruct((experts, units, width), jnp.float32),
        ],
        scratch_shapes=[
            pltpu.VMEM((line,) + rows.shape, low),
            pltpu.VMEM((line, groups, per, width), low),
            pltpu.VMEM(grads.shape, low),
            pltpu.VMEM((experts, 2, dp_count, per, width), low),
            pltpu.VMEM((experts, dp_count, per, units), low),
            pltpu.VMEM((experts, dp_count, per, units), low),
            pltpu.VMEM(grads.shape, low),
            pltpu.VMEM((line, groups, per, width), low),
            pltpu.VMEM((line,) + rows.shape, low),
            pltpu.VMEM(w_in.shape, low),
            pltpu.VMEM(w_out.shape, low),
            pltpu.VMEM((2, width // 2, width), jnp.float32),
            dma((line + 1,)),
            dma((line,)),
            dma((line, dp_count)),
            dma((line, dp_count)),
            dma((line, dp_count)),
            dma((line, dp_count)),
            dma((line,)),
            dma((line,)),
            dma((line,)),
            dma((line + 1,)),
            dma((line + 1,)),
            dma((line, experts)),
            dma((2,)),
        ],
        compiler_params=pltpu.CompilerParams(
            collective_id=0, has_side_effects=True, vmem_limit_bytes=61 << 20
        ),
        cost_estimate=pl.CostEstimate(
            flops=12 * experts * line * dp_count * per * width * units,
            bytes_accessed=8 * grads.size,
            transcendentals=grads.size,
        ),
        name="experts",
    )(rows, targets, grads, w_in, w_out)


def norm_stats(values):
    center = jnp.mean(values, axis=-1, keepdims=True)
    centered = values - center
    inv_scale = lax.rsqrt(jnp.mean(centered * centered, axis=-1, keepdims=True) + EPSILON)
    return centered * inv_scale, inv_scale


def attend_pair(proj_ref, mixed_ref, log_ref, pair, head_dim):
    length = proj_ref.shape[0]
    wide = proj_ref.shape[1] // 3
    here = pl.ds(pair * PAIR, PAIR)
    lane = lax.broadcasted_iota(jnp.int32, (BLOCK, PAIR), 1)
    for first in range(0, length, BLOCK):
        rows, seen = pl.ds(first, BLOCK), pl.ds(0, first + BLOCK)
        wide_query = proj_ref[rows, here].astype(jnp.float32) * SCORE_SCALE
        key = proj_ref[seen, pl.ds(wide + pair * PAIR, PAIR)]
        value = proj_ref[seen, pl.ds(2 * wide + pair * PAIR, PAIR)]
        mixed = jnp.zeros((BLOCK, PAIR), jnp.float32)
        logs = jnp.zeros((BLOCK, PAIR), jnp.float32)
        for head in range(PAIR // head_dim):
            mine = lane // head_dim == head
            scores = masked_scores(lanes_of(wide_query, mine), key, first)
            top = jnp.max(scores, axis=-1, keepdims=True)
            powers = jnp.exp(scores - top)
            total = jnp.sum(powers, axis=-1, keepdims=True)
            probs = (powers * (1.0 / total)).astype(jnp.bfloat16)
            mixed = jnp.where(mine, dot_plain(probs, value), mixed)
            logs = jnp.where(mine, top + jnp.log(total), logs)
        mixed_ref[rows, here] = mixed.astype(jnp.bfloat16)
        log_ref[rows, here] = logs


class Share:
    def __init__(self, held, sems, dp_count):
        self.held, self.steps = held, dp_count // 2
        self.sems, self.dp_count = sems, dp_count
        self.me = lax.axis_index("dp")
        self.other = self.me + 1 - 2 * lax.rem(self.me, 2)

    def block(self, of, i):
        return lax.rem(of + self.dp_count - 2 * i, self.dp_count)

    def across(self, i):
        to = lax.rem(self.me + 2 * i, self.dp_count)
        mine = self.held.at[self.me]
        return send(mine, mine, self.sems.at[0, i], self.sems.at[1, i], dp=to)

    def within(self, i):
        piece = self.held.at[self.block(self.me, i)]
        return send(piece, piece, self.sems.at[2, i], self.sems.at[3, i], dp=self.other)

    def start(self):
        for i in range(1, self.steps):
            self.across(i).start()
        self.within(0).start()

    def relay(self):
        for i in range(1, self.steps):
            at = self.block(self.me, i)
            piece = self.held.at[at]
            send(piece, piece, self.sems.at[0, i], self.sems.at[1, i], dp=at).wait_recv()
            self.within(i).start()

    def finish(self):
        for i in range(self.steps):
            piece = self.held.at[self.block(self.other, i)]
            send(piece, piece, self.sems.at[2, i], self.sems.at[3, i], dp=self.other).wait_recv()

    def drain(self):
        for i in range(self.steps):
            if i:
                self.across(i).wait_send()
            self.within(i).wait_send()


def front_kernel(
    dp_count,
    head_dim,
    tokens_ref,
    mate_tokens_ref,
    cot_ref,
    own_target_ref,
    qkv_a_ref,
    qkv_b_ref,
    out_a_ref,
    out_b_ref,
    gains_ref,
    grads_ref,
    target_ref,
    wq_ref,
    wo_ref,
    first_ref,
    proj_ref,
    log_ref,
    mixed_ref,
    middle_ref,
    second_ref,
    held,
    slots,
    hop,
    out_parts,
    mixed_all,
    line_send,
    line_recv,
    send_sem,
    recv_sem,
    local_sem,
    target_send,
    target_recv,
    near_send,
    near_recv,
    mix_send,
    mix_recv,
    q_sems,
    o_sems,
):
    line = held.shape[0]
    experts, _, _, per, _ = grads_ref.shape
    rows = tokens_ref.shape[0]
    me, place = lax.axis_index("dp"), lax.axis_index("tensor")
    order = block_order(place)
    mate, across, last = order[1], lax.rem(place + 2, line), line - 1 - place
    part = lax.rem(place, 2)
    wide = proj_ref.shape[1] // 3
    greet(dp_count, line)

    near = [
        send(qkv_b_ref, hop, near_send.at[0], near_recv.at[0], tensor=across),
        send(out_a_ref, out_parts.at[1], near_send.at[1], near_recv.at[1], tensor=mate),
        send(out_b_ref, out_parts.at[0], near_send.at[2], near_recv.at[2], tensor=across),
        send(out_b_ref, out_parts.at[2], near_send.at[3], near_recv.at[3], tensor=last),
    ]
    for copy in near:
        copy.start()
    along = Line(cot_ref, held, line_send, line_recv)
    along.start()
    target_ref[place] = own_target_ref[...]

    def target_copy(i, at, to):
        return send(
            target_ref.at[at], target_ref.at[at], target_send.at[i], target_recv.at[i], tensor=to
        )

    for i in range(1, line):
        target_copy(i, place, lax.rem(place + i, line)).start()

    near[0].wait_recv()
    for kind in range(3):
        base = kind * wide
        wq_ref[me, :, base : base + PAIR] = qkv_a_ref[:, base : base + PAIR]
        wq_ref[me, :, base + PAIR : base + wide] = (
            qkv_a_ref[:, base + PAIR : base + wide].astype(jnp.float32)
            + hop[kind].astype(jnp.float32)
        ).astype(jnp.bfloat16)
    share_q = Share(wq_ref, q_sems, dp_count)
    share_q.start()
    for copy in near[1:]:
        copy.wait_recv()
    for group, (a, b) in enumerate(((out_a_ref[...], 0), (out_parts[1], 2))):
        base = group * wide
        a = a.astype(jnp.float32)
        b = out_parts[b].astype(jnp.float32)
        wo_ref[me, :, base : base + PAIR] = a[:, :PAIR].astype(jnp.bfloat16)
        wo_ref[me, :, base + PAIR : base + 2 * PAIR] = (a[:, PAIR:] + b[:, :PAIR]).astype(
            jnp.bfloat16
        )
        wo_ref[me, :, base + 2 * PAIR : base + wide] = b[:, PAIR:].astype(jnp.bfloat16)
    share_o = Share(wo_ref, o_sems, dp_count)
    share_o.start()

    def first_rows(i, carry):
        here = pl.ds(i * 128, 128)
        for which, source in ((part, tokens_ref), (1 - part, mate_tokens_ref)):
            unit, _ = norm_stats(source[here, :].astype(jnp.float32))
            unit = unit * gains_ref[0:1, :] + gains_ref[1:2, :]
            first_ref[which, here, :] = unit.astype(jnp.bfloat16)
        return carry

    lax.fori_loop(0, rows // 128, first_rows, 0)
    share_q.relay()
    share_o.relay()

    plane = Plane(
        lambda step, to: slots.at[step, pl.ds(to * experts, experts)],
        lambda step, at: grads_ref.at[:, step, at],
        send_sem,
        recv_sem,
        local_sem,
        dp_count,
    )

    def dispatch(step):
        source = cot_ref if step == 0 else held.at[order[step]]
        dispatch_block(source, target_ref, order[step], slots, step, per)
        plane.start(step)

    for i in range(1, line):
        at = lax.rem(place + line - i, line)
        target_copy(i, at, at).wait_recv()
    along.take(1)
    dispatch(0)
    dispatch(1)
    share_q.finish()

    def project(which):
        def one(i, carry):
            here = pl.ds(i * (rows // 2), rows // 2)
            weights = wq_ref[...].reshape(-1, 3 * wide)
            proj_ref[pl.ds(which * rows + i * (rows // 2), rows // 2), :] = dot_plain(
                first_ref[which, here, :], weights
            ).astype(jnp.bfloat16)
            return carry

        lax.fori_loop(0, 2, one, 0)

    project(0)
    project(1)

    def mix_copy(pair):
        here = pl.ds(pair * PAIR, PAIR)
        return send(
            mixed_all.at[pl.ds((1 - part) * rows, rows), here],
            mixed_ref.at[1, :, here],
            mix_send.at[pair],
            mix_recv.at[pair],
            tensor=mate,
        )

    for pair in range(wide // PAIR):
        attend_pair(proj_ref, mixed_all, log_ref, pair, head_dim)
        mix_copy(pair).start()
        if pair == 0:
            along.take(2)
            dispatch(2)
    along.take(3)
    dispatch(3)
    mixed_ref[0] = mixed_all[pl.ds(part * rows, rows), :]
    share_o.finish()
    for pair in range(wide // PAIR):
        mix_copy(pair).wait_recv()

    def finish_rows(i, carry):
        here = pl.ds(i * 128, 128)
        total = tokens_ref[here, :].astype(jnp.float32)
        total += dot_rows(mixed_ref[0, here, :], wo_ref[:, :, :wide].reshape(-1, wide)) + dot_rows(
            mixed_ref[1, here, :], wo_ref[:, :, wide:].reshape(-1, wide)
        )
        middle_ref[here, :] = total
        unit, _ = norm_stats(total)
        second_ref[here, :] = (unit * gains_ref[2:3, :] + gains_ref[3:4, :]).astype(jnp.bfloat16)
        return carry

    lax.fori_loop(0, rows // 128, finish_rows, 0)
    along.finish()
    share_q.drain()
    share_o.drain()
    for copy in near:
        copy.wait_send()
    for i in range(1, line):
        target_copy(i, place, lax.rem(place + i, line)).wait_send()
    for pair in range(wide // PAIR):
        mix_copy(pair).wait_send()
    for step in range(line):
        plane.wait_recv(step)
        plane.wait_send(step)


def run_front(tokens, mate_tokens, cotangent, target, weights, gains, sizes):
    dp_count, line, experts, per, head_dim = sizes
    rows, width = tokens.shape
    qkv_a, qkv_b, out_a, out_b = weights
    share, columns = qkv_a.shape
    wide = columns // 3
    low, dma = jnp.bfloat16, pltpu.SemaphoreType.DMA
    whole, far = pl.BlockSpec(memory_space=pltpu.VMEM), pl.BlockSpec(memory_space=pl.ANY)
    shape = jax.ShapeDtypeStruct
    return pl.pallas_call(
        functools.partial(front_kernel, dp_count, head_dim),
        in_specs=[whole] * 9,
        out_specs=[far] + [whole] * 9,
        out_shape=[
            shape((experts, line, dp_count, per, width), low),
            shape((line,) + target.shape, jnp.int32),
            shape((dp_count, share, columns), low),
            shape((dp_count, share, 2 * wide), low),
            shape((2, rows, width), low),
            shape((2 * rows, columns), low),
            shape((2 * rows, wide), jnp.float32),
            shape((2, rows, wide), low),
            shape((rows, width), jnp.float32),
            shape((rows, width), low),
        ],
        scratch_shapes=[
            pltpu.VMEM((line, rows, width), low),
            pltpu.VMEM((line, dp_count * experts, per, width), low),
            pltpu.VMEM(qkv_b.shape, low),
            pltpu.VMEM((3,) + out_b.shape, low),
            pltpu.VMEM((2 * rows, wide), low),
            dma((line + 1,)),
            dma((line,)),
            dma((line, dp_count)),
            dma((line, dp_count)),
            dma((line,)),
            dma((line,)),
            dma((line,)),
            dma((4,)),
            dma((4,)),
            dma((wide // PAIR,)),
            dma((wide // PAIR,)),
            dma((4, dp_count // 2)),
            dma((4, dp_count // 2)),
        ],
        compiler_params=pltpu.CompilerParams(
            collective_id=1, has_side_effects=True, vmem_limit_bytes=56 << 20
        ),
        name="front",
    )(tokens, mate_tokens, cotangent, target, *weights, gains)


def attend_back_pair(proj_ref, log_ref, grad_ref, out_ref, dk_sum, dv_sum, pair, head_dim):
    length, wide = proj_ref.shape[0], proj_ref.shape[1] // 3
    here = pl.ds(pair * PAIR, PAIR)
    key_at, value_at = pl.ds(wide + pair * PAIR, PAIR), pl.ds(2 * wide + pair * PAIR, PAIR)
    lane = lax.broadcasted_iota(jnp.int32, (BLOCK, PAIR), 1)
    for first in reversed(range(0, length, BLOCK)):
        rows, seen = pl.ds(first, BLOCK), pl.ds(0, first + BLOCK)
        lanes_seen = lax.broadcasted_iota(jnp.int32, (first + BLOCK, PAIR), 1)
        wide_query = proj_ref[rows, here].astype(jnp.float32) * SCORE_SCALE
        key, value, grad = proj_ref[seen, key_at], proj_ref[seen, value_at], grad_ref[rows, here]
        query, wide_grad = wide_query.astype(jnp.bfloat16), grad.astype(jnp.float32)
        dq = jnp.zeros((BLOCK, PAIR), jnp.float32)
        dk = jnp.zeros((first + BLOCK, PAIR), jnp.float32)
        dv = jnp.zeros((first + BLOCK, PAIR), jnp.float32)
        for head in range(PAIR // head_dim):
            mine = lane // head_dim == head
            there = lanes_seen // head_dim == head
            scores = masked_scores(lanes_of(wide_query, mine), key, first)
            log_total = log_ref[rows, pl.ds(pair * PAIR + head * head_dim, 1)]
            probs = jnp.exp(scores - log_total)
            prob_grad = dot_rows(lanes_of(wide_grad, mine), value)
            inner = jnp.sum(probs * prob_grad, axis=-1, keepdims=True)
            score_grad = (probs * (prob_grad - inner)).astype(jnp.bfloat16)
            dq = jnp.where(mine, dot_plain(score_grad, key), dq)
            dk = jnp.where(there, dot_columns(score_grad, query), dk)
            dv = jnp.where(there, dot_columns(probs.astype(jnp.bfloat16), grad), dv)
        out_ref[rows, here] = (dq * SCORE_SCALE).astype(jnp.bfloat16)
        if first + BLOCK == length:
            dk_sum[...] = dk
            dv_sum[...] = dv
        else:
            dk_sum[seen, :] += dk
            dv_sum[seen, :] += dv
    out_ref[:, key_at] = dk_sum[...].astype(jnp.bfloat16)
    out_ref[:, value_at] = dv_sum[...].astype(jnp.bfloat16)


class Pieces:
    def __init__(self, source, held, sems, dp_count):
        self.source, self.held, self.sems, self.dp_count = source, held, sems, dp_count
        self.me = lax.axis_index("dp")

    def copy(self, i, to):
        return send(
            self.source.at[to],
            self.held.at[self.me],
            self.sems.at[0, i],
            self.sems.at[1, i],
            dp=to,
        )

    def start(self):
        def one(i, carry):
            self.copy(i, lax.rem(self.me + i, self.dp_count)).start()
            return carry

        lax.fori_loop(1, self.dp_count, one, 0)

    def total(self, sum_ref):
        sum_ref[...] = self.source[self.me].astype(jnp.float32)

        def one(i, carry):
            at = lax.rem(self.me + self.dp_count - i, self.dp_count)
            send(
                self.source.at[self.me],
                self.held.at[at],
                self.sems.at[0, i],
                self.sems.at[1, i],
                dp=at,
            ).wait_recv()
            sum_ref[...] += self.held[at].astype(jnp.float32)
            return carry

        lax.fori_loop(1, self.dp_count, one, 0)

    def drain(self):
        def one(i, carry):
            self.copy(i, lax.rem(self.me + i, self.dp_count)).wait_send()
            return carry

        lax.fori_loop(1, self.dp_count, one, 0)


def norm_back_rows(grad, values, gain):
    unit, inv_scale = norm_stats(values)
    scaled = grad * gain
    mean_plain = jnp.mean(scaled, axis=-1, keepdims=True)
    mean_unit = jnp.mean(scaled * unit, axis=-1, keepdims=True)
    change = inv_scale * (scaled - mean_plain - unit * mean_unit)
    return (
        change,
        jnp.sum(grad * unit, axis=0, keepdims=True),
        jnp.sum(grad, axis=0, keepdims=True),
    )


def back_kernel(
    dp_count,
    head_dim,
    back_ref,
    cot_ref,
    tokens_ref,
    middle_ref,
    gains_ref,
    target_ref,
    wq_ref,
    wo_ref,
    first_ref,
    proj_ref,
    log_ref,
    mixed_ref,
    result_ref,
    out_ref,
    grad_tokens_ref,
    sums_ref,
    d_qkv_ref,
    d_out_ref,
    returned,
    stage,
    far,
    middle_grad,
    middle_low,
    mixed_grad,
    mixed_sent,
    qkv_grad,
    dk_sum,
    dv_sum,
    out_pieces,
    out_held,
    out_sum,
    out_sent,
    out_near,
    qkv_pieces,
    qkv_held,
    qkv_sum,
    qkv_sent,
    qkv_near,
    first_sent,
    first_near,
    line_sums,
    plane_sums,
    send_sem,
    recv_sem,
    local_sem,
    far_send,
    far_recv,
    near_send,
    near_recv,
    out_sems,
    qkv_sems,
    line_send,
    line_recv,
    plane_send,
    plane_recv,
):
    rows, width = tokens_ref.shape
    experts, line, _, per, _ = result_ref.shape
    wide = proj_ref.shape[1] // 3
    share = wq_ref.shape[1]
    me, place = lax.axis_index("dp"), lax.axis_index("tensor")
    order = block_order(place)
    mate, across, last = order[1], lax.rem(place + 2, line), line - 1 - place
    part = lax.rem(place, 2)
    greet(dp_count, line)
    plane = Plane(
        lambda step, to: result_ref.at[:, order[step], to],
        lambda step, at: returned.at[step, pl.ds(at * experts, experts)],
        send_sem,
        recv_sem,
        local_sem,
        dp_count,
    )
    plane.start(2)
    results = Return(plane, returned, target_ref, stage, far, far_send, far_recv, per)
    sums_ref[...] = jnp.zeros_like(sums_ref)

    def second_rows(i, carry):
        here = pl.ds(i * 128, 128)
        change, gain_sum, bias_sum = norm_back_rows(
            back_ref[here, :], middle_ref[here, :], gains_ref[2:3, :]
        )
        change = cot_ref[here, :].astype(jnp.float32) + change
        middle_grad[here, :] = change
        middle_low[here, :] = change.astype(jnp.bfloat16)
        sums_ref[2:3, :] += gain_sum
        sums_ref[3:4, :] += bias_sum
        return carry

    lax.fori_loop(0, rows // 128, second_rows, 0)
    mixed_sent[...] = dot_plain(
        middle_low[...], wo_ref[:, :, wide:].reshape(width, wide)
    ).astype(jnp.bfloat16)
    mixed_copy = send(
        mixed_sent,
        mixed_grad.at[pl.ds(part * rows, rows)],
        near_send.at[0],
        near_recv.at[0],
        tensor=mate,
    )
    mixed_copy.start()
    mixed_grad[pl.ds(part * rows, rows), :] = dot_plain(
        middle_low[...], wo_ref[:, :, :wide].reshape(width, wide)
    ).astype(jnp.bfloat16)
    for group in range(2):
        product_ = dot_columns(middle_low[...], mixed_ref[group]).astype(jnp.bfloat16)
        out_pieces[:, :, group * wide : (group + 1) * wide] = product_.reshape(
            dp_count, share, wide
        )
    outs = Pieces(out_pieces, out_held, out_sems, dp_count)
    outs.start()
    plane.start(3)
    send(
        mixed_sent,
        mixed_grad.at[pl.ds((1 - part) * rows, rows)],
        near_send.at[0],
        near_recv.at[0],
        tensor=mate,
    ).wait_recv()
    for pair in range(wide // PAIR):
        attend_back_pair(
            proj_ref, log_ref, mixed_grad, qkv_grad, dk_sum, dv_sum, pair, head_dim
        )
        if pair == 0:
            results.begin(2)
        if pair == 1:
            results.end(2)
    first_sent[...] = dot_rows(
        qkv_grad[pl.ds((1 - part) * rows, rows), :], wq_ref[...].reshape(width, 3 * wide)
    ).astype(jnp.bfloat16)
    first_copy = send(first_sent, first_near, near_send.at[1], near_recv.at[1], tensor=mate)
    first_copy.start()
    middle_rows = width // 2
    for half in range(2):
        total = dot_columns(
            first_ref[0, :, half * middle_rows : (half + 1) * middle_rows], qkv_grad[:rows, :]
        )
        total += dot_columns(
            first_ref[1, :, half * middle_rows : (half + 1) * middle_rows], qkv_grad[rows:, :]
        )
        qkv_pieces[pl.ds(half * dp_count // 2, dp_count // 2)] = total.astype(
            jnp.bfloat16
        ).reshape(dp_count // 2, share, 3 * wide)
    qkvs = Pieces(qkv_pieces, qkv_held, qkv_sems, dp_count)
    qkvs.start()
    results.begin(3, 1)
    outs.total(out_sum)
    for i, base in enumerate((wide, PAIR, wide + PAIR)):
        out_sent[i] = out_sum[:, base : base + 2 * PAIR].astype(jnp.bfloat16)
    out_copies = [
        send(out_sent.at[i], out_near.at[i], near_send.at[3 + i], near_recv.at[3 + i], tensor=to)
        for i, to in enumerate((mate, across, last))
    ]
    for copy in out_copies:
        copy.start()

    def first_rows(i, carry):
        here = pl.ds(i * 128, 128)
        grad = dot_rows(
            qkv_grad[pl.ds(part * rows + i * 128, 128), :], wq_ref[...].reshape(width, 3 * wide)
        )
        grad += first_near[here, :].astype(jnp.float32)
        change, gain_sum, bias_sum = norm_back_rows(
            grad, tokens_ref[here, :].astype(jnp.float32), gains_ref[0:1, :]
        )
        grad_tokens_ref[here, :] = (middle_grad[here, :] + change).astype(jnp.bfloat16)
        sums_ref[0:1, :] += gain_sum
        sums_ref[1:2, :] += bias_sum
        return carry

    first_copy.wait_recv()
    lax.fori_loop(0, rows // 128, first_rows, 0)
    line_sums[place] = sums_ref[...]

    def line_copy(i, at, to):
        return send(line_sums.at[at], line_sums.at[at], line_send.at[i], line_recv.at[i], tensor=to)

    for i in range(1, line):
        line_copy(i, place, lax.rem(place + i, line)).start()
    results.end(3)
    results.begin(1, 0)
    for i in range(1, line):
        at = lax.rem(place + line - i, line)
        line_copy(i, at, at).wait_recv()
    plane_sums[me] = (line_sums[0] + line_sums[1]) + (line_sums[2] + line_sums[3])

    def plane_copy(i, at, to):
        return send(
            plane_sums.at[at], plane_sums.at[at], plane_send.at[i], plane_recv.at[i], dp=to
        )

    def plane_start(i, carry):
        plane_copy(i, me, lax.rem(me + i, dp_count)).start()
        return carry

    lax.fori_loop(1, dp_count, plane_start, 0)
    qkvs.total(qkv_sum)
    for kind in range(3):
        base = kind * wide + PAIR
        qkv_sent[kind] = qkv_sum[:, base : base + 2 * PAIR].astype(jnp.bfloat16)
    qkv_copy = send(qkv_sent, qkv_near, near_send.at[2], near_recv.at[2], tensor=across)
    qkv_copy.start()
    plane.wait_recv(0)
    middle_grad[...] = middle_ref[...] + results.collect(0)

    def plane_wait(i, carry):
        at = lax.rem(me + dp_count - i, dp_count)
        plane_copy(i, at, at).wait_recv()
        return carry

    lax.fori_loop(1, dp_count, plane_wait, 0)
    sums_ref[...] = plane_sums[0]

    def plane_add(i, carry):
        sums_ref[...] += plane_sums[i]
        return carry

    lax.fori_loop(1, dp_count, plane_add, 0)
    for copy in out_copies:
        copy.wait_recv()
    arrived = [out_near[i].astype(jnp.float32) for i in range(3)]
    d_out_ref[:, :PAIR] = (
        out_sum[:, :PAIR] + arrived[0][:, :PAIR] + arrived[1][:, PAIR:] + arrived[2][:, PAIR:]
    )
    turned = pltpu.roll(arrived[1][:, :PAIR] + arrived[2][:, :PAIR], head_dim, 1)
    d_out_ref[:, PAIR:] = out_sum[:, PAIR : 2 * PAIR] + arrived[0][:, PAIR:] + turned
    qkv_copy.wait_recv()
    for kind in range(3):
        base, at = kind * wide, kind * 2 * PAIR
        come = qkv_near[kind].astype(jnp.float32)
        d_qkv_ref[:, at : at + PAIR] = qkv_sum[:, base : base + PAIR] + come[:, PAIR:]
        d_qkv_ref[:, at + PAIR : at + 2 * PAIR] = qkv_sum[
            :, base + PAIR : base + 2 * PAIR
        ] + pltpu.roll(come[:, :PAIR], head_dim, 1)
    results.wait()
    out_ref[...] = (
        middle_grad[...] + far[0].astype(jnp.float32) + far[1].astype(jnp.float32)
    ).astype(jnp.bfloat16)
    results.drain()
    outs.drain()
    qkvs.drain()
    mixed_copy.wait_send()
    first_copy.wait_send()
    qkv_copy.wait_send()
    for copy in out_copies:
        copy.wait_send()
    for i in range(1, line):
        line_copy(i, place, lax.rem(place + i, line)).wait_send()

    def plane_drain(i, carry):
        plane_copy(i, me, lax.rem(me + i, dp_count)).wait_send()
        return carry

    lax.fori_loop(1, dp_count, plane_drain, 0)


def run_back(dp_count, head_dim, *args):
    tokens, wq, proj, result = args[2], args[6], args[9], args[12]
    rows, width = tokens.shape
    experts, line, _, per, _ = result.shape
    share = wq.shape[1]
    wide = proj.shape[1] // 3
    low, wider, dma = jnp.bfloat16, jnp.float32, pltpu.SemaphoreType.DMA
    whole, far = pl.BlockSpec(memory_space=pltpu.VMEM), pl.BlockSpec(memory_space=pl.ANY)
    shape, vmem = jax.ShapeDtypeStruct, pltpu.VMEM
    return pl.pallas_call(
        functools.partial(back_kernel, dp_count, head_dim),
        in_specs=[whole] * 12 + [far],
        out_specs=[whole] * 5,
        out_shape=[
            shape((rows, width), low),
            shape((rows, width), low),
            shape((8, width), wider),
            shape((share, 6 * PAIR), wider),
            shape((share, 2 * PAIR), wider),
        ],
        scratch_shapes=[
            vmem((line, dp_count * experts, per, width), low),
            vmem((line, rows, width), low),
            vmem((line, rows, width), low),
            vmem((rows, width), wider),
            vmem((rows, width), low),
            vmem((2 * rows, wide), low),
            vmem((rows, wide), low),
            vmem((2 * rows, 3 * wide), low),
            vmem((2 * rows, PAIR), wider),
            vmem((2 * rows, PAIR), wider),
            vmem((dp_count, share, 2 * wide), low),
            vmem((dp_count, share, 2 * wide), low),
            vmem((share, 2 * wide), wider),
            vmem((3, share, 2 * PAIR), low),
            vmem((3, share, 2 * PAIR), low),
            vmem((dp_count, share, 3 * wide), low),
            vmem((dp_count, share, 3 * wide), low),
            vmem((share, 3 * wide), wider),
            vmem((3, share, 2 * PAIR), low),
            vmem((3, share, 2 * PAIR), low),
            vmem((rows, width), low),
            vmem((rows, width), low),
            vmem((line, 8, width), wider),
            vmem((dp_count, 8, width), wider),
            dma((line, dp_count)),
            dma((line, dp_count)),
            dma((line,)),
            dma((line + 1,)),
            dma((line + 1,)),
            dma((6,)),
            dma((6,)),
            dma((2, dp_count)),
            dma((2, dp_count)),
            dma((line,)),
            dma((line,)),
            dma((dp_count,)),
            dma((dp_count,)),
        ],
        compiler_params=pltpu.CompilerParams(
            collective_id=2, has_side_effects=True, vmem_limit_bytes=58 << 20
        ),
        name="back",
    )(*args)


def on_device(
    tokens,
    token_ids,
    hash_table,
    ln1_gain,
    ln1_bias,
    w_qkv,
    w_out,
    ln2_gain,
    ln2_bias,
    expert_in,
    expert_out,
    cotangent,
):
    low = jnp.bfloat16
    row_count, model_width = tokens.shape
    local_experts = expert_in.shape[0]
    dp_count = lax.axis_size("dp")
    line = lax.axis_size("tensor")
    head_dim = w_qkv.shape[2] // 3
    heads_shard = w_qkv.shape[1]

    mate_tokens = lax.ppermute(tokens, "tensor", [(t, t ^ 1) for t in range(line)])

    experts_total = dp_count * local_experts
    capacity = 2 * row_count // experts_total
    slot_count = experts_total * capacity
    expert_of = jnp.take(hash_table, token_ids)
    one_hot = (expert_of[:, None] == jnp.arange(experts_total, dtype=jnp.int32)[None, :]).astype(
        jnp.int32
    )
    before = (
        lax.broadcasted_iota(jnp.int32, (row_count, row_count), 0)
        > lax.broadcasted_iota(jnp.int32, (row_count, row_count), 1)
    ).astype(low)
    earlier = jnp.dot(before, one_hot.astype(low), preferred_element_type=jnp.float32)
    slot_rank = jnp.sum(earlier.astype(jnp.int32) * one_hot, axis=1)
    target = jnp.where(slot_rank < capacity, expert_of * capacity + slot_rank, slot_count)
    own_target = jnp.broadcast_to(target[None, :], (8, row_count))

    share = w_qkv.shape[0]
    wide = 2 * heads_shard * head_dim
    by_kind = w_qkv.astype(low).reshape(share, heads_shard, 3, head_dim).transpose(0, 2, 1, 3)
    qkv_a = jnp.pad(by_kind.reshape(share, 3, -1), ((0, 0), (0, 0), (0, wide // 2)))
    qkv_b = jnp.concatenate([by_kind[:, :, -1:], by_kind[:, :, :-1]], axis=2).reshape(share, 3, -1)
    qkv_b = jnp.pad(qkv_b, ((0, 0), (0, 0), (head_dim, 0))).transpose(1, 0, 2)
    out_rows = w_out.astype(low).T
    out_a = jnp.pad(out_rows, ((0, 0), (0, head_dim)))
    out_b = jnp.concatenate([out_rows[:, -head_dim:], out_rows[:, :-head_dim]], axis=1)
    out_b = jnp.pad(out_b, ((0, 0), (head_dim, 0)))
    gains = jnp.pad(jnp.stack([ln1_gain, ln1_bias, ln2_gain, ln2_bias]), ((0, 4), (0, 0)))
    sizes = (dp_count, line, local_experts, capacity, head_dim)
    (
        grad_rows,
        targets,
        qkv_weight,
        out_weight,
        first_all,
        projected,
        log_total,
        mixed_pair,
        middle,
        second_low,
    ) = run_front(
        tokens,
        mate_tokens,
        cotangent,
        own_target,
        (qkv_a.reshape(share, -1), qkv_b, out_a, out_b),
        gains,
        sizes,
    )
    second_grad, result, grad_expert_in, grad_expert_out = run_experts(
        second_low,
        targets,
        grad_rows,
        expert_in,
        expert_out,
        dp_count,
        line,
    )
    out, grad_tokens, sums, grad_qkv, grad_out = run_back(
        dp_count,
        head_dim,
        second_grad,
        cotangent,
        tokens,
        middle,
        gains,
        targets,
        qkv_weight,
        out_weight,
        first_all,
        projected,
        log_total,
        mixed_pair,
        result,
    )
    half = wide // 2
    grad_qkv = grad_qkv.reshape(share, 3, -1)[:, :, :half]
    grad_qkv = grad_qkv.reshape(share, 3, heads_shard, head_dim).transpose(0, 2, 1, 3)
    return (
        out,
        grad_tokens,
        sums[0],
        sums[1],
        grad_qkv.reshape(w_qkv.shape),
        grad_out[:, :half].T,
        sums[2],
        sums[3],
        grad_expert_in,
        grad_expert_out,
    )


def solution(mesh):
    rows = P(("dp", "tensor"), None)
    weights = (P("dp", "tensor", None), P("tensor", "dp"))
    experts = (P("dp", None, "tensor"), P("dp", "tensor", None))
    return jax.shard_map(
        on_device,
        mesh=mesh,
        in_specs=(rows, P(("dp", "tensor")), P(), P(), P(), *weights, P(), P(), *experts, rows),
        out_specs=(rows, rows, P(), P(), *weights, P(), P(), *experts),
        check_vma=False,
    )
```

```python
import functools

import jax
import jax.numpy as jnp
from jax import lax
from jax.experimental import pallas as pl
from jax.experimental.pallas import tpu as pltpu
from jax.sharding import PartitionSpec as P

LEN = 1024


EPSILON = 1e-05
SCORE_SCALE = 0.125
MASKED = -1e30
MESH = pl.DeviceIdType.MESH


def lanes_of(values, mask):
    return jnp.where(mask, values, 0.0).astype(jnp.bfloat16)


def dot_rows(left, right):
    return lax.dot_general(left, right, (((1,), (1,)), ((), ())), preferred_element_type=jnp.float32)


def dot_columns(left, right):
    return lax.dot_general(left, right, (((0,), (0,)), ((), ())), preferred_element_type=jnp.float32)


def dot_plain(left, right):
    return jnp.dot(left, right, preferred_element_type=jnp.float32)


def masked_scores(query, key, first):
    scores = dot_rows(query, key)
    rows, columns = scores.shape
    row = lax.broadcasted_iota(jnp.int32, (rows, rows), 0)
    column = lax.broadcasted_iota(jnp.int32, (rows, rows), 1)
    edge = jnp.where(row >= column, scores[:, first:], MASKED)
    return edge if first == 0 else jnp.concatenate([scores[:, :first], edge], axis=1)


PAIR = 128
BLOCK = 256


def block_order(place):
    half = place // 2
    return (place, 1 + 4 * half - place, 2 - half, 3 - 3 * half)


def greet(dp_count, line):
    me, place = lax.axis_index("dp"), lax.axis_index("tensor")
    barrier = pltpu.get_barrier_semaphore()

    def plane(i, carry):
        pl.semaphore_signal(
            barrier, 1, device_id={"dp": lax.rem(me + i, dp_count)}, device_id_type=MESH
        )
        return carry

    lax.fori_loop(1, dp_count, plane, 0)
    for i in range(1, line):
        pl.semaphore_signal(
            barrier, 1, device_id={"tensor": lax.rem(place + i, line)}, device_id_type=MESH
        )
    pl.semaphore_wait(barrier, dp_count + line - 2)


class Line:
    def __init__(self, own, held, send_sem, recv_sem):
        self.own, self.held, self.send_sem, self.recv_sem = own, held, send_sem, recv_sem
        self.place = lax.axis_index("tensor")
        self.order = block_order(self.place)
        self.last = held.shape[0] - 1

    def copy(self, source, block, index, to):
        return pltpu.make_async_remote_copy(
            src_ref=source,
            dst_ref=self.held.at[block],
            send_sem=self.send_sem.at[index],
            recv_sem=self.recv_sem.at[block],
            device_id={"tensor": to},
            device_id_type=MESH,
        )

    def left(self):
        return self.copy(self.own, self.place, 0, self.place - 1)

    def right(self):
        return self.copy(self.own, self.place, self.last + 1, self.place + 1)

    def onward(self, step):
        block = self.order[step]
        up = self.copy(self.held.at[block], block, step, self.place + 1)
        down = self.copy(self.held.at[block], block, step, self.place - 1)
        return (
            (jnp.logical_and(block < self.place, self.place < self.last), up),
            (jnp.logical_and(block > self.place, self.place > 0), down),
        )

    def start(self):
        pl.when(self.place > 0)(lambda: self.left().start())
        pl.when(self.place < self.last)(lambda: self.right().start())

    def take(self, step):
        block = self.order[step]
        self.copy(self.held.at[block], block, step, block).wait_recv()
        for needed, copy in self.onward(step):
            pl.when(needed)(copy.start)

    def finish(self):
        pl.when(self.place > 0)(lambda: self.left().wait_send())
        pl.when(self.place < self.last)(lambda: self.right().wait_send())
        for step in range(1, self.last + 1):
            for needed, copy in self.onward(step):
                pl.when(needed)(copy.wait_send)


def slot_matrix(target_ref, block, first, count):
    target = target_ref[block, 0:1, :]
    slot = lax.broadcasted_iota(jnp.int32, (count, target.shape[1]), 0) + first
    return jnp.where(slot == target, 1.0, 0.0).astype(jnp.bfloat16)


class Plane:
    def __init__(self, piece, place_of, send_sem, recv_sem, local_sem, dp_count):
        self.piece, self.place_of = piece, place_of
        self.send_sem, self.recv_sem, self.local_sem = send_sem, recv_sem, local_sem
        self.me, self.dp_count = lax.axis_index("dp"), dp_count

    def copy(self, step, i):
        to = lax.rem(self.me + i, self.dp_count)
        return pltpu.make_async_remote_copy(
            src_ref=self.piece(step, to),
            dst_ref=self.place_of(step, self.me),
            send_sem=self.send_sem.at[step, i],
            recv_sem=self.recv_sem.at[step, i],
            device_id={"dp": to},
            device_id_type=MESH,
        )

    def own(self, step):
        return pltpu.make_async_copy(
            self.piece(step, self.me), self.place_of(step, self.me), self.local_sem.at[step]
        )

    def start(self, step):
        def one(i, carry):
            self.copy(step, i).start()
            return carry

        lax.fori_loop(1, self.dp_count, one, 0)
        self.own(step).start()

    def wait_recv(self, step):
        def one(i, carry):
            here = lax.rem(self.me + self.dp_count - i, self.dp_count)
            pltpu.make_async_remote_copy(
                src_ref=self.piece(step, self.me),
                dst_ref=self.place_of(step, here),
                send_sem=self.send_sem.at[step, i],
                recv_sem=self.recv_sem.at[step, i],
                device_id={"dp": here},
                device_id_type=MESH,
            ).wait_recv()
            return carry

        lax.fori_loop(1, self.dp_count, one, 0)
        self.own(step).wait()

    def wait_send(self, step):
        def one(i, carry):
            self.copy(step, i).wait_send()
            return carry

        lax.fori_loop(1, self.dp_count, one, 0)


def dispatch_block(rows, target_ref, block, slots, step, per):
    groups = slots.shape[1]
    chunk = 256 // per

    def one(i, carry):
        chosen = slot_matrix(target_ref, block, i * 256, 256)
        values = dot_plain(chosen, rows[...]).astype(jnp.bfloat16)
        slots[step, pl.ds(i * chunk, chunk)] = values.reshape((chunk, per) + values.shape[1:])
        return carry

    lax.fori_loop(0, groups // chunk, one, 0)


def collect_block(slots, target_ref, block, step, per):
    groups = slots.shape[1]
    chunk = 256 // per
    total = None
    for i in range(groups // chunk):
        chosen = slot_matrix(target_ref, block, i * 256, 256)
        values = slots[step, pl.ds(i * chunk, chunk)]
        term = dot_columns(chosen, values.reshape((256,) + values.shape[2:]))
        total = term if total is None else total + term
    return total


def send(source, there, send_sem, recv_sem, **to):
    return pltpu.make_async_remote_copy(
        src_ref=source,
        dst_ref=there,
        send_sem=send_sem,
        recv_sem=recv_sem,
        device_id=to,
        device_id_type=MESH,
    )


class Return:
    def __init__(self, plane, returned, target_ref, stage, far, far_send, far_recv, per):
        self.plane, self.returned, self.target_ref = plane, returned, target_ref
        self.stage, self.far, self.per = stage, far, per
        self.far_send, self.far_recv = far_send, far_recv
        self.place = lax.axis_index("tensor")
        self.order = block_order(self.place)
        self.mine = lax.rem(self.place, 2)
        self.half = stage.shape[1] // 2
        self.kept = pl.ds(self.mine * self.half, self.half)
        self.passed = pl.ds((1 - self.mine) * self.half, self.half)

    def mate_copy(self):
        return send(
            self.stage.at[1],
            self.far.at[0],
            self.far_send.at[0],
            self.far_recv.at[0],
            tensor=self.order[1],
        )

    def half_copy(self, step, part):
        return send(
            self.stage.at[step, part],
            self.far.at[step, part],
            self.far_send.at[step - 1],
            self.far_recv.at[step - 1],
            tensor=self.order[1],
        )

    def owner_copy(self, step, part, at):
        return send(
            self.stage.at[step, part],
            self.far.at[1, part],
            self.far_send.at[step + 1],
            self.far_recv.at[3 + at],
            tensor=self.order[step],
        )

    def collect(self, step):
        return collect_block(self.returned, self.target_ref, self.order[step], step, self.per)

    def begin(self, step, then=None):
        self.plane.wait_recv(step)
        if then is not None:
            self.plane.start(then)
        self.stage[step] = self.collect(step).astype(jnp.bfloat16)
        if step == 1:
            self.mate_copy().start()
        else:
            self.half_copy(step, self.passed).start()

    def end(self, step):
        self.half_copy(step, self.kept).wait_recv()
        self.stage[step, self.kept] = (
            self.stage[step, self.kept].astype(jnp.float32)
            + self.far[step, self.kept].astype(jnp.float32)
        ).astype(jnp.bfloat16)
        self.owner_copy(step, self.kept, self.mine).start()

    def wait(self):
        self.mate_copy().wait()
        self.owner_copy(2, pl.ds(0, self.half), 0).wait_recv()
        self.owner_copy(2, pl.ds(self.half, self.half), 1).wait_recv()

    def drain(self):
        for step in range(4):
            self.plane.wait_send(step)
        for step in (2, 3):
            self.half_copy(step, self.passed).wait_send()
            self.owner_copy(step, self.kept, self.mine).wait_send()


GELU_SCALE = 0.7978845608028654
GELU_CUBE = 0.044715


def expert_kernel(
    dp_count,
    rows_ref,
    target_ref,
    grads_ref,
    wide_in_ref,
    wide_out_ref,
    back_ref,
    result_ref,
    d_in_ref,
    d_out_ref,
    held,
    slots,
    arrived,
    grads,
    active,
    hidden_grad,
    sent_back,
    returned,
    far,
    w_in_ref,
    w_out_ref,
    loaded,
    line_send,
    line_recv,
    send_sem,
    recv_sem,
    back_send,
    back_recv,
    local_sem,
    back_local,
    grad_sem,
    far_send,
    far_recv,
    out_sem,
    load_sem,
):
    line = held.shape[0]
    experts, _, _, per, width = arrived.shape
    place, me = lax.axis_index("tensor"), lax.axis_index("dp")
    order = block_order(place)
    rows_of = dp_count * per
    greet(dp_count, line)
    along = Line(rows_ref, held, line_send, line_recv)
    along.start()
    out_plane = Plane(
        lambda step, to: slots.at[step, pl.ds(to * experts, experts)],
        lambda step, at: arrived.at[:, step, at],
        send_sem,
        recv_sem,
        local_sem,
        dp_count,
    )
    back_plane = Plane(
        lambda step, to: sent_back.at[:, step, to],
        lambda step, at: returned.at[step, pl.ds(at * experts, experts)],
        back_send,
        back_recv,
        back_local,
        dp_count,
    )

    def grad_copy(step):
        return pltpu.make_async_copy(
            grads_ref.at[:, step], grads.at[:, step % 2], grad_sem.at[step]
        )

    def dispatch(step):
        if step:
            along.take(step)
        source = rows_ref if step == 0 else held.at[order[step]]
        dispatch_block(source, target_ref, order[step], slots, step, per)
        out_plane.start(step)

    half = dp_count // 2

    def forward(step):
        grad_copy(step).wait()
        for expert in range(experts):

            def one(i, carry):
                part = pl.ds(i * half, half)
                x = arrived[expert, step, part].reshape(half * per, width)
                g = grads[expert, step % 2, part].reshape(half * per, width)
                hidden = dot_plain(x, w_in_ref[expert])
                inner = GELU_SCALE * (hidden + GELU_CUBE * hidden * hidden * hidden)
                bend = jnp.tanh(inner)
                gate = 0.5 * (1.0 + bend)
                active[expert, part] = (
                    (hidden * gate).astype(jnp.bfloat16).reshape(half, per, -1)
                )
                slope = gate + 0.5 * hidden * (1.0 - bend * bend) * (
                    GELU_SCALE * (1.0 + 3.0 * GELU_CUBE * hidden * hidden)
                )
                change = (dot_rows(g, w_out_ref[expert]) * slope).astype(jnp.bfloat16)
                hidden_grad[expert, part] = change.reshape(half, per, -1)
                row_grad = dot_rows(change, w_in_ref[expert]).astype(jnp.bfloat16)
                sent_back[expert, step, part] = row_grad.reshape(half, per, width)
                return carry

            lax.fori_loop(0, 2, one, 0)
        if step > 1:
            back_plane.start(step)
        if step == 3:
            back_plane.start(1)

    def result_copy(step, expert):
        return pltpu.make_async_copy(
            slots.at[step, pl.ds(expert * dp_count, dp_count)],
            result_ref.at[expert, order[step]],
            out_sem.at[step, expert],
        )

    def later(step):
        out_plane.wait_send(step)
        for expert in range(experts):
            a = active[expert].reshape(rows_of, -1)
            result = dot_plain(a, w_out_ref[expert]).astype(jnp.bfloat16)
            slots[step, pl.ds(expert * dp_count, dp_count)] = result.reshape(
                dp_count, per, width
            )
            result_copy(step, expert).start()
            g = grads[expert, step % 2].reshape(rows_of, width)
            x = arrived[expert, step].reshape(rows_of, width)
            change = hidden_grad[expert].reshape(rows_of, -1)
            if step == 0:
                d_out_ref[expert] = dot_columns(a, g)
                d_in_ref[expert] = dot_columns(x, change)
            else:
                d_out_ref[expert] += dot_columns(a, g)
                d_in_ref[expert] += dot_columns(x, change)

    home = Return(back_plane, returned, target_ref, held, far, far_send, far_recv, per)
    chunk = loaded.shape[1]
    loads = [
        (wide, narrow, expert, i * chunk)
        for wide, narrow in ((wide_in_ref, w_in_ref), (wide_out_ref, w_out_ref))
        for expert in range(experts)
        for i in range(narrow.shape[1] // chunk)
    ]

    def load(i):
        wide, _, expert, first = loads[i]
        return pltpu.make_async_copy(
            wide.at[expert, pl.ds(first, chunk)], loaded.at[i % 2], load_sem.at[i % 2]
        )

    load(0).start()
    grad_copy(0).start()
    grad_copy(1).start()
    dispatch(0)
    for i, (_, narrow, expert, first) in enumerate(loads):
        if i + 1 < len(loads):
            load(i + 1).start()
        load(i).wait()
        narrow[expert, pl.ds(first, chunk), :] = loaded[i % 2].astype(jnp.bfloat16)
    dispatch(1)
    for step in range(line):
        out_plane.wait_recv(step)
        forward(step)
        if step + 2 < line:
            dispatch(step + 2)
        later(step)
        if step + 2 < line:
            grad_copy(step + 2).start()
    along.finish()
    home.begin(2, 0)
    home.end(2)
    home.begin(3)
    home.end(3)
    home.begin(1)
    back_plane.wait_recv(0)
    back_ref[...] = home.collect(0)
    home.wait()
    back_ref[...] += far[0].astype(jnp.float32) + far[1].astype(jnp.float32)
    home.drain()
    for step in range(line):
        for expert in range(experts):
            result_copy(step, expert).wait()


def run_experts(rows, targets, grads, w_in, w_out, dp_count, line):
    experts, _, _, per, width = grads.shape
    units = w_in.shape[2]
    low, dma = jnp.bfloat16, pltpu.SemaphoreType.DMA
    whole, far = pl.BlockSpec(memory_space=pltpu.VMEM), pl.BlockSpec(memory_space=pl.ANY)
    groups = dp_count * experts
    return pl.pallas_call(
        functools.partial(expert_kernel, dp_count),
        in_specs=[whole, whole, far, far, far],
        out_specs=[whole, far, whole, whole],
        out_shape=[
            jax.ShapeDtypeStruct(rows.shape, jnp.float32),
            jax.ShapeDtypeStruct(grads.shape, low),
            jax.ShapeDtypeStruct((experts, width, units), jnp.float32),
            jax.ShapeDtypeStruct((experts, units, width), jnp.float32),
        ],
        scratch_shapes=[
            pltpu.VMEM((line,) + rows.shape, low),
            pltpu.VMEM((line, groups, per, width), low),
            pltpu.VMEM(grads.shape, low),
            pltpu.VMEM((experts, 2, dp_count, per, width), low),
            pltpu.VMEM((experts, dp_count, per, units), low),
            pltpu.VMEM((experts, dp_count, per, units), low),
            pltpu.VMEM(grads.shape, low),
            pltpu.VMEM((line, groups, per, width), low),
            pltpu.VMEM((line,) + rows.shape, low),
            pltpu.VMEM(w_in.shape, low),
            pltpu.VMEM(w_out.shape, low),
            pltpu.VMEM((2, width // 2, width), jnp.float32),
            dma((line + 1,)),
            dma((line,)),
            dma((line, dp_count)),
            dma((line, dp_count)),
            dma((line, dp_count)),
            dma((line, dp_count)),
            dma((line,)),
            dma((line,)),
            dma((line,)),
            dma((line + 1,)),
            dma((line + 1,)),
            dma((line, experts)),
            dma((2,)),
        ],
        compiler_params=pltpu.CompilerParams(
            collective_id=0, has_side_effects=True, vmem_limit_bytes=61 << 20
        ),
        cost_estimate=pl.CostEstimate(
            flops=12 * experts * line * dp_count * per * width * units,
            bytes_accessed=8 * grads.size,
            transcendentals=grads.size,
        ),
        name="experts",
    )(rows, targets, grads, w_in, w_out)


def norm_stats(values):
    center = jnp.mean(values, axis=-1, keepdims=True)
    centered = values - center
    inv_scale = lax.rsqrt(jnp.mean(centered * centered, axis=-1, keepdims=True) + EPSILON)
    return centered * inv_scale, inv_scale


def attend_pair(proj_ref, mixed_ref, log_ref, pair, head_dim):
    length = proj_ref.shape[0]
    wide = proj_ref.shape[1] // 3
    here = pl.ds(pair * PAIR, PAIR)
    lane = lax.broadcasted_iota(jnp.int32, (BLOCK, PAIR), 1)
    for first in range(0, length, BLOCK):
        rows, seen = pl.ds(first, BLOCK), pl.ds(0, first + BLOCK)
        wide_query = proj_ref[rows, here].astype(jnp.float32) * SCORE_SCALE
        key = proj_ref[seen, pl.ds(wide + pair * PAIR, PAIR)]
        value = proj_ref[seen, pl.ds(2 * wide + pair * PAIR, PAIR)]
        mixed = jnp.zeros((BLOCK, PAIR), jnp.float32)
        logs = jnp.zeros((BLOCK, PAIR), jnp.float32)
        for head in range(PAIR // head_dim):
            mine = lane // head_dim == head
            scores = masked_scores(lanes_of(wide_query, mine), key, first)
            top = jnp.max(scores, axis=-1, keepdims=True)
            powers = jnp.exp(scores - top)
            total = jnp.sum(powers, axis=-1, keepdims=True)
            probs = (powers * (1.0 / total)).astype(jnp.bfloat16)
            mixed = jnp.where(mine, dot_plain(probs, value), mixed)
            logs = jnp.where(mine, top + jnp.log(total), logs)
        mixed_ref[rows, here] = mixed.astype(jnp.bfloat16)
        log_ref[rows, here] = logs


class Share:
    def __init__(self, held, sems, dp_count):
        self.held, self.steps = held, dp_count // 2
        self.sems, self.dp_count = sems, dp_count
        self.me = lax.axis_index("dp")
        self.other = self.me + 1 - 2 * lax.rem(self.me, 2)

    def block(self, of, i):
        return lax.rem(of + self.dp_count - 2 * i, self.dp_count)

    def across(self, i):
        to = lax.rem(self.me + 2 * i, self.dp_count)
        mine = self.held.at[self.me]
        return send(mine, mine, self.sems.at[0, i], self.sems.at[1, i], dp=to)

    def within(self, i):
        piece = self.held.at[self.block(self.me, i)]
        return send(piece, piece, self.sems.at[2, i], self.sems.at[3, i], dp=self.other)

    def start(self):
        for i in range(1, self.steps):
            self.across(i).start()
        self.within(0).start()

    def relay(self):
        for i in range(1, self.steps):
            at = self.block(self.me, i)
            piece = self.held.at[at]
            send(piece, piece, self.sems.at[0, i], self.sems.at[1, i], dp=at).wait_recv()
            self.within(i).start()

    def finish(self):
        for i in range(self.steps):
            piece = self.held.at[self.block(self.other, i)]
            send(piece, piece, self.sems.at[2, i], self.sems.at[3, i], dp=self.other).wait_recv()

    def drain(self):
        for i in range(self.steps):
            if i:
                self.across(i).wait_send()
            self.within(i).wait_send()


def front_kernel(
    dp_count,
    head_dim,
    tokens_ref,
    cot_ref,
    own_target_ref,
    qkv_a_ref,
    qkv_b_ref,
    out_a_ref,
    out_b_ref,
    gain_one_ref,
    bias_one_ref,
    gain_two_ref,
    bias_two_ref,
    grads_ref,
    gains_ref,
    target_ref,
    wq_ref,
    wo_ref,
    first_ref,
    proj_ref,
    log_ref,
    mixed_ref,
    middle_ref,
    second_ref,
    held,
    slots,
    hop,
    out_parts,
    mixed_all,
    mate_tokens_ref,
    line_send,
    line_recv,
    send_sem,
    recv_sem,
    local_sem,
    target_send,
    target_recv,
    near_send,
    near_recv,
    mix_send,
    mix_recv,
    q_sems,
    o_sems,
):
    line = held.shape[0]
    experts, _, _, per, _ = grads_ref.shape
    rows = tokens_ref.shape[0]
    me, place = lax.axis_index("dp"), lax.axis_index("tensor")
    order = block_order(place)
    mate, across, last = order[1], lax.rem(place + 2, line), line - 1 - place
    part = lax.rem(place, 2)
    wide = proj_ref.shape[1] // 3
    greet(dp_count, line)

    near = [
        send(qkv_b_ref, hop, near_send.at[0], near_recv.at[0], tensor=across),
        send(out_a_ref, out_parts.at[1], near_send.at[1], near_recv.at[1], tensor=mate),
        send(out_b_ref, out_parts.at[0], near_send.at[2], near_recv.at[2], tensor=across),
        send(out_b_ref, out_parts.at[2], near_send.at[3], near_recv.at[3], tensor=last),
    ]
    for copy in near:
        copy.start()
    along = Line(cot_ref, held, line_send, line_recv)
    along.start()
    token_copy = send(
        tokens_ref, mate_tokens_ref, near_send.at[4], near_recv.at[4], tensor=mate
    )
    token_copy.start()
    target_ref[place] = jnp.broadcast_to(own_target_ref[...].reshape(1, rows), (8, rows))
    for i, values in enumerate((gain_one_ref, bias_one_ref, gain_two_ref, bias_two_ref)):
        gains_ref[i : i + 1, :] = values[...].reshape(1, -1)

    def target_copy(i, at, to):
        return send(
            target_ref.at[at], target_ref.at[at], target_send.at[i], target_recv.at[i], tensor=to
        )

    for i in range(1, line):
        target_copy(i, place, lax.rem(place + i, line)).start()

    plane = Plane(
        lambda step, to: slots.at[step, pl.ds(to * experts, experts)],
        lambda step, at: grads_ref.at[:, step, at],
        send_sem,
        recv_sem,
        local_sem,
        dp_count,
    )

    def dispatch(step):
        source = cot_ref if step == 0 else held.at[order[step]]
        dispatch_block(source, target_ref, order[step], slots, step, per)
        plane.start(step)

    dispatch(0)
    near[0].wait_recv()
    for kind in range(3):
        base = kind * wide
        wq_ref[me, :, base : base + PAIR] = qkv_a_ref[:, base : base + PAIR]
        wq_ref[me, :, base + PAIR : base + wide] = (
            qkv_a_ref[:, base + PAIR : base + wide].astype(jnp.float32)
            + hop[kind].astype(jnp.float32)
        ).astype(jnp.bfloat16)
    share_q = Share(wq_ref, q_sems, dp_count)
    share_q.start()
    for copy in near[1:]:
        copy.wait_recv()
    for group, (a, b) in enumerate(((out_a_ref[...], 0), (out_parts[1], 2))):
        base = group * wide
        a = a.astype(jnp.float32)
        b = out_parts[b].astype(jnp.float32)
        wo_ref[me, :, base : base + PAIR] = a[:, :PAIR].astype(jnp.bfloat16)
        wo_ref[me, :, base + PAIR : base + 2 * PAIR] = (a[:, PAIR:] + b[:, :PAIR]).astype(
            jnp.bfloat16
        )
        wo_ref[me, :, base + 2 * PAIR : base + wide] = b[:, PAIR:].astype(jnp.bfloat16)
    share_o = Share(wo_ref, o_sems, dp_count)
    share_o.start()

    def first_rows(which, source):
        def one(i, carry):
            here = pl.ds(i * 128, 128)
            unit, _ = norm_stats(source[here, :].astype(jnp.float32))
            unit = unit * gains_ref[0:1, :] + gains_ref[1:2, :]
            first_ref[which, here, :] = unit.astype(jnp.bfloat16)
            return carry

        lax.fori_loop(0, rows // 128, one, 0)

    first_rows(part, tokens_ref)
    share_q.relay()
    along.take(1)
    for i in range(1, line):
        at = lax.rem(place + line - i, line)
        target_copy(i, at, at).wait_recv()
    dispatch(1)
    share_o.relay()
    share_q.finish()

    def project(which):
        def one(i, carry):
            here = pl.ds(i * (rows // 2), rows // 2)
            weights = wq_ref[...].reshape(-1, 3 * wide)
            proj_ref[pl.ds(which * rows + i * (rows // 2), rows // 2), :] = dot_plain(
                first_ref[which, here, :], weights
            ).astype(jnp.bfloat16)
            return carry

        lax.fori_loop(0, 2, one, 0)

    project(part)
    token_copy.wait_recv()
    first_rows(1 - part, mate_tokens_ref)
    project(1 - part)
    along.take(2)
    dispatch(2)

    def mix_copy(pair):
        here = pl.ds(pair * PAIR, PAIR)
        return send(
            mixed_all.at[pl.ds((1 - part) * rows, rows), here],
            mixed_ref.at[1, :, here],
            mix_send.at[pair],
            mix_recv.at[pair],
            tensor=mate,
        )

    for pair in range(wide // PAIR):
        attend_pair(proj_ref, mixed_all, log_ref, pair, head_dim)
        mix_copy(pair).start()
        if pair == 1:
            along.take(3)
            dispatch(3)
    mixed_ref[0] = mixed_all[pl.ds(part * rows, rows), :]
    share_o.finish()
    for pair in range(wide // PAIR):
        mix_copy(pair).wait_recv()

    def finish_rows(i, carry):
        here = pl.ds(i * 128, 128)
        total = tokens_ref[here, :].astype(jnp.float32)
        total += dot_rows(mixed_ref[0, here, :], wo_ref[:, :, :wide].reshape(-1, wide)) + dot_rows(
            mixed_ref[1, here, :], wo_ref[:, :, wide:].reshape(-1, wide)
        )
        middle_ref[here, :] = total
        unit, _ = norm_stats(total)
        second_ref[here, :] = (unit * gains_ref[2:3, :] + gains_ref[3:4, :]).astype(jnp.bfloat16)
        return carry

    lax.fori_loop(0, rows // 128, finish_rows, 0)
    along.finish()
    token_copy.wait_send()
    share_q.drain()
    share_o.drain()
    for copy in near:
        copy.wait_send()
    for i in range(1, line):
        target_copy(i, place, lax.rem(place + i, line)).wait_send()
    for pair in range(wide // PAIR):
        mix_copy(pair).wait_send()
    for step in range(line):
        plane.wait_recv(step)
        plane.wait_send(step)


def run_front(tokens, cotangent, target, weights, gains, sizes):
    dp_count, line, experts, per, head_dim = sizes
    rows, width = tokens.shape
    qkv_a, qkv_b, out_a, out_b = weights
    share, columns = qkv_a.shape
    wide = columns // 3
    low, dma = jnp.bfloat16, pltpu.SemaphoreType.DMA
    whole, far = pl.BlockSpec(memory_space=pltpu.VMEM), pl.BlockSpec(memory_space=pl.ANY)
    shape = jax.ShapeDtypeStruct
    return pl.pallas_call(
        functools.partial(front_kernel, dp_count, head_dim),
        in_specs=[whole] * 11,
        out_specs=[far] + [whole] * 10,
        out_shape=[
            shape((experts, line, dp_count, per, width), low),
            shape((8, width), jnp.float32),
            shape((line, 8, rows), jnp.int32),
            shape((dp_count, share, columns), low),
            shape((dp_count, share, 2 * wide), low),
            shape((2, rows, width), low),
            shape((2 * rows, columns), low),
            shape((2 * rows, wide), jnp.float32),
            shape((2, rows, wide), low),
            shape((rows, width), jnp.float32),
            shape((rows, width), low),
        ],
        scratch_shapes=[
            pltpu.VMEM((line, rows, width), low),
            pltpu.VMEM((line, dp_count * experts, per, width), low),
            pltpu.VMEM(qkv_b.shape, low),
            pltpu.VMEM((3,) + out_b.shape, low),
            pltpu.VMEM((2 * rows, wide), low),
            pltpu.VMEM((rows, width), low),
            dma((line + 1,)),
            dma((line,)),
            dma((line, dp_count)),
            dma((line, dp_count)),
            dma((line,)),
            dma((line,)),
            dma((line,)),
            dma((5,)),
            dma((5,)),
            dma((wide // PAIR,)),
            dma((wide // PAIR,)),
            dma((4, dp_count // 2)),
            dma((4, dp_count // 2)),
        ],
        compiler_params=pltpu.CompilerParams(
            collective_id=1, has_side_effects=True, vmem_limit_bytes=56 << 20
        ),
        name="front",
    )(tokens, cotangent, target, *weights, *gains)


def attend_back_pair(proj_ref, log_ref, grad_ref, out_ref, dk_sum, dv_sum, pair, head_dim):
    length, wide = proj_ref.shape[0], proj_ref.shape[1] // 3
    here = pl.ds(pair * PAIR, PAIR)
    key_at, value_at = pl.ds(wide + pair * PAIR, PAIR), pl.ds(2 * wide + pair * PAIR, PAIR)
    lane = lax.broadcasted_iota(jnp.int32, (BLOCK, PAIR), 1)
    for first in reversed(range(0, length, BLOCK)):
        rows, seen = pl.ds(first, BLOCK), pl.ds(0, first + BLOCK)
        lanes_seen = lax.broadcasted_iota(jnp.int32, (first + BLOCK, PAIR), 1)
        wide_query = proj_ref[rows, here].astype(jnp.float32) * SCORE_SCALE
        key, value, grad = proj_ref[seen, key_at], proj_ref[seen, value_at], grad_ref[rows, here]
        query, wide_grad = wide_query.astype(jnp.bfloat16), grad.astype(jnp.float32)
        dq = jnp.zeros((BLOCK, PAIR), jnp.float32)
        dk = jnp.zeros((first + BLOCK, PAIR), jnp.float32)
        dv = jnp.zeros((first + BLOCK, PAIR), jnp.float32)
        for head in range(PAIR // head_dim):
            mine = lane // head_dim == head
            there = lanes_seen // head_dim == head
            scores = masked_scores(lanes_of(wide_query, mine), key, first)
            log_total = log_ref[rows, pl.ds(pair * PAIR + head * head_dim, 1)]
            probs = jnp.exp(scores - log_total)
            prob_grad = dot_rows(lanes_of(wide_grad, mine), value)
            inner = jnp.sum(probs * prob_grad, axis=-1, keepdims=True)
            score_grad = (probs * (prob_grad - inner)).astype(jnp.bfloat16)
            dq = jnp.where(mine, dot_plain(score_grad, key), dq)
            dk = jnp.where(there, dot_columns(score_grad, query), dk)
            dv = jnp.where(there, dot_columns(probs.astype(jnp.bfloat16), grad), dv)
        out_ref[rows, here] = (dq * SCORE_SCALE).astype(jnp.bfloat16)
        if first + BLOCK == length:
            dk_sum[...] = dk
            dv_sum[...] = dv
        else:
            dk_sum[seen, :] += dk
            dv_sum[seen, :] += dv
    out_ref[:, key_at] = dk_sum[...].astype(jnp.bfloat16)
    out_ref[:, value_at] = dv_sum[...].astype(jnp.bfloat16)


class Pieces:
    def __init__(self, source, held, sems, dp_count):
        self.source, self.held, self.sems, self.dp_count = source, held, sems, dp_count
        self.me = lax.axis_index("dp")

    def copy(self, i, to):
        return send(
            self.source.at[to],
            self.held.at[self.me],
            self.sems.at[0, i],
            self.sems.at[1, i],
            dp=to,
        )

    def start(self):
        def one(i, carry):
            self.copy(i, lax.rem(self.me + i, self.dp_count)).start()
            return carry

        lax.fori_loop(1, self.dp_count, one, 0)

    def total(self, sum_ref):
        sum_ref[...] = self.source[self.me].astype(jnp.float32)

        def one(i, carry):
            at = lax.rem(self.me + self.dp_count - i, self.dp_count)
            send(
                self.source.at[self.me],
                self.held.at[at],
                self.sems.at[0, i],
                self.sems.at[1, i],
                dp=at,
            ).wait_recv()
            sum_ref[...] += self.held[at].astype(jnp.float32)
            return carry

        lax.fori_loop(1, self.dp_count, one, 0)

    def drain(self):
        def one(i, carry):
            self.copy(i, lax.rem(self.me + i, self.dp_count)).wait_send()
            return carry

        lax.fori_loop(1, self.dp_count, one, 0)


def norm_back_rows(grad, values, gain):
    unit, inv_scale = norm_stats(values)
    scaled = grad * gain
    mean_plain = jnp.mean(scaled, axis=-1, keepdims=True)
    mean_unit = jnp.mean(scaled * unit, axis=-1, keepdims=True)
    change = inv_scale * (scaled - mean_plain - unit * mean_unit)
    return (
        change,
        jnp.sum(grad * unit, axis=0, keepdims=True),
        jnp.sum(grad, axis=0, keepdims=True),
    )


def back_kernel(
    dp_count,
    head_dim,
    back_ref,
    cot_ref,
    tokens_ref,
    middle_ref,
    gains_ref,
    target_ref,
    wq_ref,
    wo_ref,
    first_ref,
    proj_ref,
    log_ref,
    mixed_ref,
    result_ref,
    out_ref,
    grad_tokens_ref,
    sums_ref,
    d_qkv_ref,
    d_out_ref,
    returned,
    stage,
    far,
    middle_grad,
    middle_low,
    mixed_grad,
    mixed_sent,
    qkv_grad,
    dk_sum,
    dv_sum,
    out_pieces,
    out_held,
    out_sum,
    out_sent,
    out_near,
    qkv_pieces,
    qkv_held,
    qkv_sum,
    qkv_sent,
    qkv_near,
    first_sent,
    first_near,
    line_sums,
    plane_sums,
    send_sem,
    recv_sem,
    local_sem,
    far_send,
    far_recv,
    near_send,
    near_recv,
    out_sems,
    qkv_sems,
    line_send,
    line_recv,
    plane_send,
    plane_recv,
):
    rows, width = tokens_ref.shape
    experts, line, _, per, _ = result_ref.shape
    wide = proj_ref.shape[1] // 3
    share = wq_ref.shape[1]
    me, place = lax.axis_index("dp"), lax.axis_index("tensor")
    order = block_order(place)
    mate, across, last = order[1], lax.rem(place + 2, line), line - 1 - place
    part = lax.rem(place, 2)
    greet(dp_count, line)
    plane = Plane(
        lambda step, to: result_ref.at[:, order[step], to],
        lambda step, at: returned.at[step, pl.ds(at * experts, experts)],
        send_sem,
        recv_sem,
        local_sem,
        dp_count,
    )
    plane.start(2)
    results = Return(plane, returned, target_ref, stage, far, far_send, far_recv, per)
    sums_ref[...] = jnp.zeros_like(sums_ref)

    def second_rows(i, carry):
        here = pl.ds(i * 128, 128)
        change, gain_sum, bias_sum = norm_back_rows(
            back_ref[here, :], middle_ref[here, :], gains_ref[2:3, :]
        )
        change = cot_ref[here, :].astype(jnp.float32) + change
        middle_grad[here, :] = change
        middle_low[here, :] = change.astype(jnp.bfloat16)
        sums_ref[2:3, :] += gain_sum
        sums_ref[3:4, :] += bias_sum
        return carry

    lax.fori_loop(0, rows // 128, second_rows, 0)
    mixed_sent[...] = dot_plain(
        middle_low[...], wo_ref[:, :, wide:].reshape(width, wide)
    ).astype(jnp.bfloat16)
    mixed_copy = send(
        mixed_sent,
        mixed_grad.at[pl.ds(part * rows, rows)],
        near_send.at[0],
        near_recv.at[0],
        tensor=mate,
    )
    mixed_copy.start()
    mixed_grad[pl.ds(part * rows, rows), :] = dot_plain(
        middle_low[...], wo_ref[:, :, :wide].reshape(width, wide)
    ).astype(jnp.bfloat16)
    for group in range(2):
        product_ = dot_columns(middle_low[...], mixed_ref[group]).astype(jnp.bfloat16)
        out_pieces[:, :, group * wide : (group + 1) * wide] = product_.reshape(
            dp_count, share, wide
        )
    outs = Pieces(out_pieces, out_held, out_sems, dp_count)
    outs.start()
    plane.start(3)
    send(
        mixed_sent,
        mixed_grad.at[pl.ds((1 - part) * rows, rows)],
        near_send.at[0],
        near_recv.at[0],
        tensor=mate,
    ).wait_recv()
    for pair in range(wide // PAIR):
        attend_back_pair(
            proj_ref, log_ref, mixed_grad, qkv_grad, dk_sum, dv_sum, pair, head_dim
        )
        if pair == 0:
            results.begin(2)
        if pair == 1:
            results.end(2)
            plane.start(1)
    first_sent[...] = dot_rows(
        qkv_grad[pl.ds((1 - part) * rows, rows), :], wq_ref[...].reshape(width, 3 * wide)
    ).astype(jnp.bfloat16)
    first_copy = send(first_sent, first_near, near_send.at[1], near_recv.at[1], tensor=mate)
    first_copy.start()
    middle_rows = width // 2
    for half in range(2):
        total = dot_columns(
            first_ref[0, :, half * middle_rows : (half + 1) * middle_rows], qkv_grad[:rows, :]
        )
        total += dot_columns(
            first_ref[1, :, half * middle_rows : (half + 1) * middle_rows], qkv_grad[rows:, :]
        )
        qkv_pieces[pl.ds(half * dp_count // 2, dp_count // 2)] = total.astype(
            jnp.bfloat16
        ).reshape(dp_count // 2, share, 3 * wide)
    qkvs = Pieces(qkv_pieces, qkv_held, qkv_sems, dp_count)
    qkvs.start()
    results.begin(3, 0)
    outs.total(out_sum)
    for i, base in enumerate((wide, PAIR, wide + PAIR)):
        out_sent[i] = out_sum[:, base : base + 2 * PAIR].astype(jnp.bfloat16)
    out_copies = [
        send(out_sent.at[i], out_near.at[i], near_send.at[3 + i], near_recv.at[3 + i], tensor=to)
        for i, to in enumerate((mate, across, last))
    ]
    for copy in out_copies:
        copy.start()

    def first_rows(i, carry):
        here = pl.ds(i * 128, 128)
        grad = dot_rows(
            qkv_grad[pl.ds(part * rows + i * 128, 128), :], wq_ref[...].reshape(width, 3 * wide)
        )
        grad += first_near[here, :].astype(jnp.float32)
        change, gain_sum, bias_sum = norm_back_rows(
            grad, tokens_ref[here, :].astype(jnp.float32), gains_ref[0:1, :]
        )
        grad_tokens_ref[here, :] = (middle_grad[here, :] + change).astype(jnp.bfloat16)
        sums_ref[0:1, :] += gain_sum
        sums_ref[1:2, :] += bias_sum
        return carry

    first_copy.wait_recv()
    lax.fori_loop(0, rows // 128, first_rows, 0)
    line_sums[place] = sums_ref[...]

    def line_copy(i, at, to):
        return send(line_sums.at[at], line_sums.at[at], line_send.at[i], line_recv.at[i], tensor=to)

    for i in range(1, line):
        line_copy(i, place, lax.rem(place + i, line)).start()
    results.end(3)
    results.begin(1)
    for i in range(1, line):
        at = lax.rem(place + line - i, line)
        line_copy(i, at, at).wait_recv()
    plane_sums[me] = (line_sums[0] + line_sums[1]) + (line_sums[2] + line_sums[3])

    def plane_copy(i, at, to):
        return send(
            plane_sums.at[at], plane_sums.at[at], plane_send.at[i], plane_recv.at[i], dp=to
        )

    def plane_start(i, carry):
        plane_copy(i, me, lax.rem(me + i, dp_count)).start()
        return carry

    lax.fori_loop(1, dp_count, plane_start, 0)
    qkvs.total(qkv_sum)
    for kind in range(3):
        base = kind * wide + PAIR
        qkv_sent[kind] = qkv_sum[:, base : base + 2 * PAIR].astype(jnp.bfloat16)
    qkv_copy = send(qkv_sent, qkv_near, near_send.at[2], near_recv.at[2], tensor=across)
    qkv_copy.start()
    plane.wait_recv(0)
    middle_grad[...] = middle_ref[...] + results.collect(0)

    def plane_wait(i, carry):
        at = lax.rem(me + dp_count - i, dp_count)
        plane_copy(i, at, at).wait_recv()
        return carry

    lax.fori_loop(1, dp_count, plane_wait, 0)
    sums_ref[...] = plane_sums[0]

    def plane_add(i, carry):
        sums_ref[...] += plane_sums[i]
        return carry

    lax.fori_loop(1, dp_count, plane_add, 0)
    for copy in out_copies:
        copy.wait_recv()
    arrived = [out_near[i].astype(jnp.float32) for i in range(3)]
    d_out_ref[:, :PAIR] = (
        out_sum[:, :PAIR] + arrived[0][:, :PAIR] + arrived[1][:, PAIR:] + arrived[2][:, PAIR:]
    )
    turned = pltpu.roll(arrived[1][:, :PAIR] + arrived[2][:, :PAIR], head_dim, 1)
    d_out_ref[:, PAIR:] = out_sum[:, PAIR : 2 * PAIR] + arrived[0][:, PAIR:] + turned
    qkv_copy.wait_recv()
    for kind in range(3):
        base, at = kind * wide, kind * 2 * PAIR
        come = qkv_near[kind].astype(jnp.float32)
        d_qkv_ref[:, at : at + PAIR] = qkv_sum[:, base : base + PAIR] + come[:, PAIR:]
        d_qkv_ref[:, at + PAIR : at + 2 * PAIR] = qkv_sum[
            :, base + PAIR : base + 2 * PAIR
        ] + pltpu.roll(come[:, :PAIR], head_dim, 1)
    results.wait()
    out_ref[...] = (
        middle_grad[...] + far[0].astype(jnp.float32) + far[1].astype(jnp.float32)
    ).astype(jnp.bfloat16)
    results.drain()
    outs.drain()
    qkvs.drain()
    mixed_copy.wait_send()
    first_copy.wait_send()
    qkv_copy.wait_send()
    for copy in out_copies:
        copy.wait_send()
    for i in range(1, line):
        line_copy(i, place, lax.rem(place + i, line)).wait_send()

    def plane_drain(i, carry):
        plane_copy(i, me, lax.rem(me + i, dp_count)).wait_send()
        return carry

    lax.fori_loop(1, dp_count, plane_drain, 0)


def run_back(dp_count, head_dim, *args):
    tokens, wq, proj, result = args[2], args[6], args[9], args[12]
    rows, width = tokens.shape
    experts, line, _, per, _ = result.shape
    share = wq.shape[1]
    wide = proj.shape[1] // 3
    low, wider, dma = jnp.bfloat16, jnp.float32, pltpu.SemaphoreType.DMA
    whole, far = pl.BlockSpec(memory_space=pltpu.VMEM), pl.BlockSpec(memory_space=pl.ANY)
    shape, vmem = jax.ShapeDtypeStruct, pltpu.VMEM
    return pl.pallas_call(
        functools.partial(back_kernel, dp_count, head_dim),
        in_specs=[whole] * 12 + [far],
        out_specs=[whole] * 5,
        out_shape=[
            shape((rows, width), low),
            shape((rows, width), low),
            shape((8, width), wider),
            shape((share, 6 * PAIR), wider),
            shape((share, 2 * PAIR), wider),
        ],
        scratch_shapes=[
            vmem((line, dp_count * experts, per, width), low),
            vmem((line, rows, width), low),
            vmem((line, rows, width), low),
            vmem((rows, width), wider),
            vmem((rows, width), low),
            vmem((2 * rows, wide), low),
            vmem((rows, wide), low),
            vmem((2 * rows, 3 * wide), low),
            vmem((2 * rows, PAIR), wider),
            vmem((2 * rows, PAIR), wider),
            vmem((dp_count, share, 2 * wide), low),
            vmem((dp_count, share, 2 * wide), low),
            vmem((share, 2 * wide), wider),
            vmem((3, share, 2 * PAIR), low),
            vmem((3, share, 2 * PAIR), low),
            vmem((dp_count, share, 3 * wide), low),
            vmem((dp_count, share, 3 * wide), low),
            vmem((share, 3 * wide), wider),
            vmem((3, share, 2 * PAIR), low),
            vmem((3, share, 2 * PAIR), low),
            vmem((rows, width), low),
            vmem((rows, width), low),
            vmem((line, 8, width), wider),
            vmem((dp_count, 8, width), wider),
            dma((line, dp_count)),
            dma((line, dp_count)),
            dma((line,)),
            dma((line + 1,)),
            dma((line + 1,)),
            dma((6,)),
            dma((6,)),
            dma((2, dp_count)),
            dma((2, dp_count)),
            dma((line,)),
            dma((line,)),
            dma((dp_count,)),
            dma((dp_count,)),
        ],
        compiler_params=pltpu.CompilerParams(
            collective_id=2, has_side_effects=True, vmem_limit_bytes=58 << 20
        ),
        name="back",
    )(*args)


def on_device(
    tokens,
    token_ids,
    hash_table,
    ln1_gain,
    ln1_bias,
    w_qkv,
    w_out,
    ln2_gain,
    ln2_bias,
    expert_in,
    expert_out,
    cotangent,
):
    low = jnp.bfloat16
    row_count, model_width = tokens.shape
    local_experts = expert_in.shape[0]
    dp_count = lax.axis_size("dp")
    line = lax.axis_size("tensor")
    head_dim = w_qkv.shape[2] // 3
    heads_shard = w_qkv.shape[1]

    experts_total = dp_count * local_experts
    capacity = 2 * row_count // experts_total
    slot_count = experts_total * capacity
    expert_of = jnp.take(hash_table, token_ids)
    one_hot = (expert_of[:, None] == jnp.arange(experts_total, dtype=jnp.int32)[None, :]).astype(
        jnp.int32
    )
    before = (
        lax.broadcasted_iota(jnp.int32, (row_count, row_count), 0)
        > lax.broadcasted_iota(jnp.int32, (row_count, row_count), 1)
    ).astype(low)
    earlier = jnp.dot(before, one_hot.astype(low), preferred_element_type=jnp.float32)
    slot_rank = jnp.sum(earlier.astype(jnp.int32) * one_hot, axis=1)
    target = jnp.where(slot_rank < capacity, expert_of * capacity + slot_rank, slot_count)

    share = w_qkv.shape[0]
    wide = 2 * heads_shard * head_dim
    by_kind = w_qkv.astype(low).reshape(share, heads_shard, 3, head_dim).transpose(0, 2, 1, 3)
    qkv_a = jnp.pad(by_kind.reshape(share, 3, -1), ((0, 0), (0, 0), (0, wide // 2)))
    qkv_b = jnp.concatenate([by_kind[:, :, -1:], by_kind[:, :, :-1]], axis=2).reshape(share, 3, -1)
    qkv_b = jnp.pad(qkv_b, ((0, 0), (0, 0), (head_dim, 0))).transpose(1, 0, 2)
    out_rows = w_out.astype(low).T
    out_a = jnp.pad(out_rows, ((0, 0), (0, head_dim)))
    out_b = jnp.concatenate([out_rows[:, -head_dim:], out_rows[:, :-head_dim]], axis=1)
    out_b = jnp.pad(out_b, ((0, 0), (head_dim, 0)))
    sizes = (dp_count, line, local_experts, capacity, head_dim)
    (
        grad_rows,
        gains,
        targets,
        qkv_weight,
        out_weight,
        first_all,
        projected,
        log_total,
        mixed_pair,
        middle,
        second_low,
    ) = run_front(
        tokens,
        cotangent,
        target,
        (qkv_a.reshape(share, -1), qkv_b, out_a, out_b),
        (ln1_gain, ln1_bias, ln2_gain, ln2_bias),
        sizes,
    )
    second_grad, result, grad_expert_in, grad_expert_out = run_experts(
        second_low,
        targets,
        grad_rows,
        expert_in,
        expert_out,
        dp_count,
        line,
    )
    out, grad_tokens, sums, grad_qkv, grad_out = run_back(
        dp_count,
        head_dim,
        second_grad,
        cotangent,
        tokens,
        middle,
        gains,
        targets,
        qkv_weight,
        out_weight,
        first_all,
        projected,
        log_total,
        mixed_pair,
        result,
    )
    half = wide // 2
    grad_qkv = grad_qkv.reshape(share, 3, -1)[:, :, :half]
    grad_qkv = grad_qkv.reshape(share, 3, heads_shard, head_dim).transpose(0, 2, 1, 3)
    return (
        out,
        grad_tokens,
        sums[0],
        sums[1],
        grad_qkv.reshape(w_qkv.shape),
        grad_out[:, :half].T,
        sums[2],
        sums[3],
        grad_expert_in,
        grad_expert_out,
    )


def solution(mesh):
    rows = P(("dp", "tensor"), None)
    weights = (P("dp", "tensor", None), P("tensor", "dp"))
    experts = (P("dp", None, "tensor"), P("dp", "tensor", None))
    return jax.shard_map(
        on_device,
        mesh=mesh,
        in_specs=(rows, P(("dp", "tensor")), P(), P(), P(), *weights, P(), P(), *experts, rows),
        out_specs=(rows, rows, P(), P(), *weights, P(), P(), *experts),
        check_vma=False,
    )
```

```python
import functools

import jax
import jax.numpy as jnp
from jax import lax
from jax.experimental import pallas as pl
from jax.experimental.pallas import tpu as pltpu
from jax.sharding import PartitionSpec as P

LEN = 1024


EPSILON = 1e-05
SCORE_SCALE = 0.125
MASKED = -1e30
MESH = pl.DeviceIdType.MESH


def lanes_of(values, mask):
    return jnp.where(mask, values, 0.0).astype(jnp.bfloat16)


def dot_rows(left, right):
    return lax.dot_general(left, right, (((1,), (1,)), ((), ())), preferred_element_type=jnp.float32)


def dot_columns(left, right):
    return lax.dot_general(left, right, (((0,), (0,)), ((), ())), preferred_element_type=jnp.float32)


def dot_plain(left, right):
    return jnp.dot(left, right, preferred_element_type=jnp.float32)


def masked_scores(query, key, first):
    scores = dot_rows(query, key)
    rows, columns = scores.shape
    row = lax.broadcasted_iota(jnp.int32, (rows, rows), 0)
    column = lax.broadcasted_iota(jnp.int32, (rows, rows), 1)
    edge = jnp.where(row >= column, scores[:, first:], MASKED)
    return edge if first == 0 else jnp.concatenate([scores[:, :first], edge], axis=1)


PAIR = 128
BLOCK = 256


def block_order(place):
    half = place // 2
    return (place, 1 + 4 * half - place, 2 - half, 3 - 3 * half)


def greet(dp_count, line):
    me, place = lax.axis_index("dp"), lax.axis_index("tensor")
    barrier = pltpu.get_barrier_semaphore()

    def plane(i, carry):
        pl.semaphore_signal(
            barrier, 1, device_id={"dp": lax.rem(me + i, dp_count)}, device_id_type=MESH
        )
        return carry

    lax.fori_loop(1, dp_count, plane, 0)
    for i in range(1, line):
        pl.semaphore_signal(
            barrier, 1, device_id={"tensor": lax.rem(place + i, line)}, device_id_type=MESH
        )
    pl.semaphore_wait(barrier, dp_count + line - 2)


class Line:
    def __init__(self, own, held, send_sem, recv_sem):
        self.own, self.held, self.send_sem, self.recv_sem = own, held, send_sem, recv_sem
        self.place = lax.axis_index("tensor")
        self.order = block_order(self.place)
        self.last = held.shape[0] - 1

    def copy(self, source, block, index, to):
        return pltpu.make_async_remote_copy(
            src_ref=source,
            dst_ref=self.held.at[block],
            send_sem=self.send_sem.at[index],
            recv_sem=self.recv_sem.at[block],
            device_id={"tensor": to},
            device_id_type=MESH,
        )

    def left(self):
        return self.copy(self.own, self.place, 0, self.place - 1)

    def right(self):
        return self.copy(self.own, self.place, self.last + 1, self.place + 1)

    def onward(self, step):
        block = self.order[step]
        up = self.copy(self.held.at[block], block, step, self.place + 1)
        down = self.copy(self.held.at[block], block, step, self.place - 1)
        return (
            (jnp.logical_and(block < self.place, self.place < self.last), up),
            (jnp.logical_and(block > self.place, self.place > 0), down),
        )

    def start(self):
        pl.when(self.place > 0)(lambda: self.left().start())
        pl.when(self.place < self.last)(lambda: self.right().start())

    def take(self, step):
        block = self.order[step]
        self.copy(self.held.at[block], block, step, block).wait_recv()
        for needed, copy in self.onward(step):
            pl.when(needed)(copy.start)

    def finish(self):
        pl.when(self.place > 0)(lambda: self.left().wait_send())
        pl.when(self.place < self.last)(lambda: self.right().wait_send())
        for step in range(1, self.last + 1):
            for needed, copy in self.onward(step):
                pl.when(needed)(copy.wait_send)


def slot_matrix(target_ref, block, first, count):
    target = target_ref[block, 0:1, :]
    slot = lax.broadcasted_iota(jnp.int32, (count, target.shape[1]), 0) + first
    return jnp.where(slot == target, 1.0, 0.0).astype(jnp.bfloat16)


class Plane:
    def __init__(self, piece, place_of, send_sem, recv_sem, local_sem, dp_count):
        self.piece, self.place_of = piece, place_of
        self.send_sem, self.recv_sem, self.local_sem = send_sem, recv_sem, local_sem
        self.me, self.dp_count = lax.axis_index("dp"), dp_count

    def copy(self, step, i):
        to = lax.rem(self.me + i, self.dp_count)
        return pltpu.make_async_remote_copy(
            src_ref=self.piece(step, to),
            dst_ref=self.place_of(step, self.me),
            send_sem=self.send_sem.at[step, i],
            recv_sem=self.recv_sem.at[step, i],
            device_id={"dp": to},
            device_id_type=MESH,
        )

    def own(self, step):
        return pltpu.make_async_copy(
            self.piece(step, self.me), self.place_of(step, self.me), self.local_sem.at[step]
        )

    def start(self, step):
        def one(i, carry):
            self.copy(step, i).start()
            return carry

        lax.fori_loop(1, self.dp_count, one, 0)
        self.own(step).start()

    def wait_recv(self, step):
        def one(i, carry):
            here = lax.rem(self.me + self.dp_count - i, self.dp_count)
            pltpu.make_async_remote_copy(
                src_ref=self.piece(step, self.me),
                dst_ref=self.place_of(step, here),
                send_sem=self.send_sem.at[step, i],
                recv_sem=self.recv_sem.at[step, i],
                device_id={"dp": here},
                device_id_type=MESH,
            ).wait_recv()
            return carry

        lax.fori_loop(1, self.dp_count, one, 0)
        self.own(step).wait()

    def wait_send(self, step):
        def one(i, carry):
            self.copy(step, i).wait_send()
            return carry

        lax.fori_loop(1, self.dp_count, one, 0)


def dispatch_block(rows, target_ref, block, slots, step, per):
    groups = slots.shape[1]
    chunk = 256 // per

    def one(i, carry):
        chosen = slot_matrix(target_ref, block, i * 256, 256)
        values = dot_plain(chosen, rows[...]).astype(jnp.bfloat16)
        slots[step, pl.ds(i * chunk, chunk)] = values.reshape((chunk, per) + values.shape[1:])
        return carry

    lax.fori_loop(0, groups // chunk, one, 0)


def collect_block(slots, target_ref, block, step, per):
    groups = slots.shape[1]
    chunk = 256 // per
    total = None
    for i in range(groups // chunk):
        chosen = slot_matrix(target_ref, block, i * 256, 256)
        values = slots[step, pl.ds(i * chunk, chunk)]
        term = dot_columns(chosen, values.reshape((256,) + values.shape[2:]))
        total = term if total is None else total + term
    return total


def send(source, there, send_sem, recv_sem, **to):
    return pltpu.make_async_remote_copy(
        src_ref=source,
        dst_ref=there,
        send_sem=send_sem,
        recv_sem=recv_sem,
        device_id=to,
        device_id_type=MESH,
    )


class Return:
    def __init__(self, plane, returned, target_ref, stage, far, far_send, far_recv, per):
        self.plane, self.returned, self.target_ref = plane, returned, target_ref
        self.stage, self.far, self.per = stage, far, per
        self.far_send, self.far_recv = far_send, far_recv
        self.place = lax.axis_index("tensor")
        self.order = block_order(self.place)
        self.mine = lax.rem(self.place, 2)
        self.half = stage.shape[1] // 2
        self.kept = pl.ds(self.mine * self.half, self.half)
        self.passed = pl.ds((1 - self.mine) * self.half, self.half)

    def mate_copy(self):
        return send(
            self.stage.at[1],
            self.far.at[0],
            self.far_send.at[0],
            self.far_recv.at[0],
            tensor=self.order[1],
        )

    def half_copy(self, step, part):
        return send(
            self.stage.at[step, part],
            self.far.at[step, part],
            self.far_send.at[step - 1],
            self.far_recv.at[step - 1],
            tensor=self.order[1],
        )

    def owner_copy(self, step, part, at):
        return send(
            self.stage.at[step, part],
            self.far.at[1, part],
            self.far_send.at[step + 1],
            self.far_recv.at[3 + at],
            tensor=self.order[step],
        )

    def collect(self, step):
        return collect_block(self.returned, self.target_ref, self.order[step], step, self.per)

    def begin(self, step, then=None):
        self.plane.wait_recv(step)
        if then is not None:
            self.plane.start(then)
        self.stage[step] = self.collect(step).astype(jnp.bfloat16)
        if step == 1:
            self.mate_copy().start()
        else:
            self.half_copy(step, self.passed).start()

    def end(self, step):
        self.half_copy(step, self.kept).wait_recv()
        self.stage[step, self.kept] = (
            self.stage[step, self.kept].astype(jnp.float32)
            + self.far[step, self.kept].astype(jnp.float32)
        ).astype(jnp.bfloat16)
        self.owner_copy(step, self.kept, self.mine).start()

    def wait(self):
        self.mate_copy().wait()
        self.owner_copy(2, pl.ds(0, self.half), 0).wait_recv()
        self.owner_copy(2, pl.ds(self.half, self.half), 1).wait_recv()

    def drain(self):
        for step in range(4):
            self.plane.wait_send(step)
        for step in (2, 3):
            self.half_copy(step, self.passed).wait_send()
            self.owner_copy(step, self.kept, self.mine).wait_send()


GELU_SCALE = 0.7978845608028654
GELU_CUBE = 0.044715


def expert_kernel(
    dp_count,
    rows_ref,
    target_ref,
    grads_ref,
    wide_in_ref,
    wide_out_ref,
    back_ref,
    result_ref,
    d_in_out_ref,
    d_out_out_ref,
    held,
    slots,
    arrived,
    grads,
    active,
    hidden_grad,
    sent_back,
    returned,
    far,
    w_in_ref,
    w_out_ref,
    loaded,
    d_in_ref,
    d_out_ref,
    line_send,
    line_recv,
    send_sem,
    recv_sem,
    back_send,
    back_recv,
    local_sem,
    back_local,
    grad_sem,
    far_send,
    far_recv,
    out_sem,
    load_sem,
    d_sem,
):
    line = held.shape[0]
    experts, _, _, per, width = arrived.shape
    place, me = lax.axis_index("tensor"), lax.axis_index("dp")
    order = block_order(place)
    rows_of = dp_count * per
    greet(dp_count, line)
    along = Line(rows_ref, held, line_send, line_recv)
    along.start()
    out_plane = Plane(
        lambda step, to: slots.at[step, pl.ds(to * experts, experts)],
        lambda step, at: arrived.at[:, step, at],
        send_sem,
        recv_sem,
        local_sem,
        dp_count,
    )
    back_plane = Plane(
        lambda step, to: sent_back.at[:, step, to],
        lambda step, at: returned.at[step, pl.ds(at * experts, experts)],
        back_send,
        back_recv,
        back_local,
        dp_count,
    )

    def grad_copy(step):
        return pltpu.make_async_copy(
            grads_ref.at[:, step], grads.at[:, step % 2], grad_sem.at[step]
        )

    def dispatch(step):
        if step:
            along.take(step)
        source = rows_ref if step == 0 else held.at[order[step]]
        dispatch_block(source, target_ref, order[step], slots, step, per)
        out_plane.start(step)

    half = dp_count // 2

    def forward(step):
        grad_copy(step).wait()
        for expert in range(experts):

            def one(i, carry):
                part = pl.ds(i * half, half)
                x = arrived[expert, step, part].reshape(half * per, width)
                g = grads[expert, step % 2, part].reshape(half * per, width)
                hidden = dot_plain(x, w_in_ref[expert])
                inner = GELU_SCALE * (hidden + GELU_CUBE * hidden * hidden * hidden)
                bend = jnp.tanh(inner)
                gate = 0.5 * (1.0 + bend)
                active[expert, part] = (
                    (hidden * gate).astype(jnp.bfloat16).reshape(half, per, -1)
                )
                slope = gate + 0.5 * hidden * (1.0 - bend * bend) * (
                    GELU_SCALE * (1.0 + 3.0 * GELU_CUBE * hidden * hidden)
                )
                change = (dot_rows(g, w_out_ref[expert]) * slope).astype(jnp.bfloat16)
                hidden_grad[expert, part] = change.reshape(half, per, -1)
                row_grad = dot_rows(change, w_in_ref[expert]).astype(jnp.bfloat16)
                sent_back[expert, step, part] = row_grad.reshape(half, per, width)
                return carry

            lax.fori_loop(0, 2, one, 0)
        if step > 1:
            back_plane.start(step)
        if step == 3:
            back_plane.start(1)
            back_plane.start(0)

    def result_copy(step, expert):
        return pltpu.make_async_copy(
            slots.at[step, pl.ds(expert * dp_count, dp_count)],
            result_ref.at[expert, order[step]],
            out_sem.at[step, expert],
        )

    def later(step):
        out_plane.wait_send(step)
        for expert in range(experts):
            a = active[expert].reshape(rows_of, -1)
            result = dot_plain(a, w_out_ref[expert]).astype(jnp.bfloat16)
            slots[step, pl.ds(expert * dp_count, dp_count)] = result.reshape(
                dp_count, per, width
            )
            result_copy(step, expert).start()
            g = grads[expert, step % 2].reshape(rows_of, width)
            x = arrived[expert, step].reshape(rows_of, width)
            change = hidden_grad[expert].reshape(rows_of, -1)
            if step == 0:
                d_out_ref[expert] = dot_columns(a, g)
                d_in_ref[expert] = dot_columns(x, change)
            else:
                d_out_ref[expert] += dot_columns(a, g)
                d_in_ref[expert] += dot_columns(x, change)

    home = Return(back_plane, returned, target_ref, held, far, far_send, far_recv, per)
    chunk = loaded.shape[1]
    loads = [
        (wide, narrow, expert, i * chunk)
        for wide, narrow in ((wide_in_ref, w_in_ref), (wide_out_ref, w_out_ref))
        for expert in range(experts)
        for i in range(narrow.shape[1] // chunk)
    ]

    def load(i):
        wide, _, expert, first = loads[i]
        return pltpu.make_async_copy(
            wide.at[expert, pl.ds(first, chunk)], loaded.at[i % 2], load_sem.at[i % 2]
        )

    load(0).start()
    grad_copy(0).start()
    grad_copy(1).start()
    dispatch(0)
    for i, (_, narrow, expert, first) in enumerate(loads):
        if i + 1 < len(loads):
            load(i + 1).start()
        load(i).wait()
        narrow[expert, pl.ds(first, chunk), :] = loaded[i % 2].astype(jnp.bfloat16)
    dispatch(1)
    for step in range(line):
        out_plane.wait_recv(step)
        forward(step)
        if step + 2 < line:
            dispatch(step + 2)
        later(step)
        if step + 2 < line:
            grad_copy(step + 2).start()
    d_copies = [
        pltpu.make_async_copy(d_in_ref, d_in_out_ref, d_sem.at[0]),
        pltpu.make_async_copy(d_out_ref, d_out_out_ref, d_sem.at[1]),
    ]
    for copy in d_copies:
        copy.start()
    along.finish()
    home.begin(2)
    home.end(2)
    home.begin(3)
    home.end(3)
    home.begin(1)
    back_plane.wait_recv(0)
    back_ref[...] = home.collect(0)
    home.wait()
    back_ref[...] += far[0].astype(jnp.float32) + far[1].astype(jnp.float32)
    home.drain()
    for copy in d_copies:
        copy.wait()
    for step in range(line):
        for expert in range(experts):
            result_copy(step, expert).wait()


def run_experts(rows, targets, grads, w_in, w_out, dp_count, line):
    experts, _, _, per, width = grads.shape
    units = w_in.shape[2]
    low, dma = jnp.bfloat16, pltpu.SemaphoreType.DMA
    whole, far = pl.BlockSpec(memory_space=pltpu.VMEM), pl.BlockSpec(memory_space=pl.ANY)
    groups = dp_count * experts
    return pl.pallas_call(
        functools.partial(expert_kernel, dp_count),
        in_specs=[whole, whole, far, far, far],
        out_specs=[whole, far, far, far],
        out_shape=[
            jax.ShapeDtypeStruct(rows.shape, jnp.float32),
            jax.ShapeDtypeStruct(grads.shape, low),
            jax.ShapeDtypeStruct((experts, width, units), jnp.float32),
            jax.ShapeDtypeStruct((experts, units, width), jnp.float32),
        ],
        scratch_shapes=[
            pltpu.VMEM((line,) + rows.shape, low),
            pltpu.VMEM((line, groups, per, width), low),
            pltpu.VMEM(grads.shape, low),
            pltpu.VMEM((experts, 2, dp_count, per, width), low),
            pltpu.VMEM((experts, dp_count, per, units), low),
            pltpu.VMEM((experts, dp_count, per, units), low),
            pltpu.VMEM(grads.shape, low),
            pltpu.VMEM((line, groups, per, width), low),
            pltpu.VMEM((line,) + rows.shape, low),
            pltpu.VMEM(w_in.shape, low),
            pltpu.VMEM(w_out.shape, low),
            pltpu.VMEM((2, width // 2, width), jnp.float32),
            pltpu.VMEM((experts, width, units), jnp.float32),
            pltpu.VMEM((experts, units, width), jnp.float32),
            dma((line + 1,)),
            dma((line,)),
            dma((line, dp_count)),
            dma((line, dp_count)),
            dma((line, dp_count)),
            dma((line, dp_count)),
            dma((line,)),
            dma((line,)),
            dma((line,)),
            dma((line + 1,)),
            dma((line + 1,)),
            dma((line, experts)),
            dma((2,)),
            dma((2,)),
        ],
        compiler_params=pltpu.CompilerParams(
            collective_id=0, has_side_effects=True, vmem_limit_bytes=61 << 20
        ),
        cost_estimate=pl.CostEstimate(
            flops=12 * experts * line * dp_count * per * width * units,
            bytes_accessed=8 * grads.size,
            transcendentals=grads.size,
        ),
        name="experts",
    )(rows, targets, grads, w_in, w_out)


def norm_stats(values):
    center = jnp.mean(values, axis=-1, keepdims=True)
    centered = values - center
    inv_scale = lax.rsqrt(jnp.mean(centered * centered, axis=-1, keepdims=True) + EPSILON)
    return centered * inv_scale, inv_scale


def attend_pair(proj_ref, mixed_ref, log_ref, pair, head_dim):
    length = proj_ref.shape[0]
    wide = proj_ref.shape[1] // 3
    here = pl.ds(pair * PAIR, PAIR)
    lane = lax.broadcasted_iota(jnp.int32, (BLOCK, PAIR), 1)
    for first in range(0, length, BLOCK):
        rows, seen = pl.ds(first, BLOCK), pl.ds(0, first + BLOCK)
        wide_query = proj_ref[rows, here].astype(jnp.float32) * SCORE_SCALE
        key = proj_ref[seen, pl.ds(wide + pair * PAIR, PAIR)]
        value = proj_ref[seen, pl.ds(2 * wide + pair * PAIR, PAIR)]
        mixed = jnp.zeros((BLOCK, PAIR), jnp.float32)
        logs = jnp.zeros((BLOCK, PAIR), jnp.float32)
        for head in range(PAIR // head_dim):
            mine = lane // head_dim == head
            scores = masked_scores(lanes_of(wide_query, mine), key, first)
            top = jnp.max(scores, axis=-1, keepdims=True)
            powers = jnp.exp(scores - top)
            total = jnp.sum(powers, axis=-1, keepdims=True)
            probs = (powers * (1.0 / total)).astype(jnp.bfloat16)
            mixed = jnp.where(mine, dot_plain(probs, value), mixed)
            logs = jnp.where(mine, top + jnp.log(total), logs)
        mixed_ref[rows, here] = mixed.astype(jnp.bfloat16)
        log_ref[rows, here] = logs


class Share:
    def __init__(self, held, sems, dp_count):
        self.held, self.steps = held, dp_count // 2
        self.sems, self.dp_count = sems, dp_count
        self.me = lax.axis_index("dp")
        self.other = self.me + 1 - 2 * lax.rem(self.me, 2)

    def block(self, of, i):
        return lax.rem(of + self.dp_count - 2 * i, self.dp_count)

    def across(self, i):
        to = lax.rem(self.me + 2 * i, self.dp_count)
        mine = self.held.at[self.me]
        return send(mine, mine, self.sems.at[0, i], self.sems.at[1, i], dp=to)

    def within(self, i):
        piece = self.held.at[self.block(self.me, i)]
        return send(piece, piece, self.sems.at[2, i], self.sems.at[3, i], dp=self.other)

    def start(self):
        for i in range(1, self.steps):
            self.across(i).start()
        self.within(0).start()

    def relay(self):
        for i in range(1, self.steps):
            at = self.block(self.me, i)
            piece = self.held.at[at]
            send(piece, piece, self.sems.at[0, i], self.sems.at[1, i], dp=at).wait_recv()
            self.within(i).start()

    def finish(self):
        for i in range(self.steps):
            piece = self.held.at[self.block(self.other, i)]
            send(piece, piece, self.sems.at[2, i], self.sems.at[3, i], dp=self.other).wait_recv()

    def drain(self):
        for i in range(self.steps):
            if i:
                self.across(i).wait_send()
            self.within(i).wait_send()


def front_kernel(
    dp_count,
    head_dim,
    tokens_ref,
    cot_ref,
    own_target_ref,
    qkv_a_ref,
    qkv_b_ref,
    out_a_ref,
    out_b_ref,
    gain_one_ref,
    bias_one_ref,
    gain_two_ref,
    bias_two_ref,
    grads_ref,
    gains_ref,
    target_ref,
    wq_ref,
    wo_ref,
    first_ref,
    proj_ref,
    log_ref,
    mixed_ref,
    middle_ref,
    second_ref,
    held,
    slots,
    hop,
    out_parts,
    mixed_all,
    mate_tokens_ref,
    line_send,
    line_recv,
    send_sem,
    recv_sem,
    local_sem,
    target_send,
    target_recv,
    near_send,
    near_recv,
    mix_send,
    mix_recv,
    q_sems,
    o_sems,
):
    line = held.shape[0]
    experts, _, _, per, _ = grads_ref.shape
    rows = tokens_ref.shape[0]
    me, place = lax.axis_index("dp"), lax.axis_index("tensor")
    order = block_order(place)
    mate, across, last = order[1], lax.rem(place + 2, line), line - 1 - place
    part = lax.rem(place, 2)
    wide = proj_ref.shape[1] // 3
    greet(dp_count, line)

    near = [
        send(qkv_b_ref, hop, near_send.at[0], near_recv.at[0], tensor=across),
        send(out_a_ref, out_parts.at[1], near_send.at[1], near_recv.at[1], tensor=mate),
        send(out_b_ref, out_parts.at[0], near_send.at[2], near_recv.at[2], tensor=across),
        send(out_b_ref, out_parts.at[2], near_send.at[3], near_recv.at[3], tensor=last),
    ]
    for copy in near:
        copy.start()
    along = Line(cot_ref, held, line_send, line_recv)
    along.start()
    token_copy = send(
        tokens_ref, mate_tokens_ref, near_send.at[4], near_recv.at[4], tensor=mate
    )
    token_copy.start()
    target_ref[place] = jnp.broadcast_to(own_target_ref[...].reshape(1, rows), (8, rows))
    for i, values in enumerate((gain_one_ref, bias_one_ref, gain_two_ref, bias_two_ref)):
        gains_ref[i : i + 1, :] = values[...].reshape(1, -1)

    def target_copy(i, at, to):
        return send(
            target_ref.at[at], target_ref.at[at], target_send.at[i], target_recv.at[i], tensor=to
        )

    for i in range(1, line):
        target_copy(i, place, lax.rem(place + i, line)).start()

    plane = Plane(
        lambda step, to: slots.at[step, pl.ds(to * experts, experts)],
        lambda step, at: grads_ref.at[:, step, at],
        send_sem,
        recv_sem,
        local_sem,
        dp_count,
    )

    def dispatch(step):
        source = cot_ref if step == 0 else held.at[order[step]]
        dispatch_block(source, target_ref, order[step], slots, step, per)
        plane.start(step)

    dispatch(0)
    near[0].wait_recv()
    for kind in range(3):
        base = kind * wide
        wq_ref[me, :, base : base + PAIR] = qkv_a_ref[:, base : base + PAIR]
        wq_ref[me, :, base + PAIR : base + wide] = (
            qkv_a_ref[:, base + PAIR : base + wide].astype(jnp.float32)
            + hop[kind].astype(jnp.float32)
        ).astype(jnp.bfloat16)
    share_q = Share(wq_ref, q_sems, dp_count)
    share_q.start()
    for copy in near[1:]:
        copy.wait_recv()
    for group, (a, b) in enumerate(((out_a_ref[...], 0), (out_parts[1], 2))):
        base = group * wide
        a = a.astype(jnp.float32)
        b = out_parts[b].astype(jnp.float32)
        wo_ref[me, :, base : base + PAIR] = a[:, :PAIR].astype(jnp.bfloat16)
        wo_ref[me, :, base + PAIR : base + 2 * PAIR] = (a[:, PAIR:] + b[:, :PAIR]).astype(
            jnp.bfloat16
        )
        wo_ref[me, :, base + 2 * PAIR : base + wide] = b[:, PAIR:].astype(jnp.bfloat16)
    share_o = Share(wo_ref, o_sems, dp_count)
    share_o.start()

    def first_rows(which, source):
        def one(i, carry):
            here = pl.ds(i * 128, 128)
            unit, _ = norm_stats(source[here, :].astype(jnp.float32))
            unit = unit * gains_ref[0:1, :] + gains_ref[1:2, :]
            first_ref[which, here, :] = unit.astype(jnp.bfloat16)
            return carry

        lax.fori_loop(0, rows // 128, one, 0)

    first_rows(part, tokens_ref)
    share_q.relay()
    along.take(1)
    for i in range(1, line):
        at = lax.rem(place + line - i, line)
        target_copy(i, at, at).wait_recv()
    dispatch(1)
    share_o.relay()
    share_q.finish()

    def project(which):
        def one(i, carry):
            here = pl.ds(i * (rows // 2), rows // 2)
            weights = wq_ref[...].reshape(-1, 3 * wide)
            proj_ref[pl.ds(which * rows + i * (rows // 2), rows // 2), :] = dot_plain(
                first_ref[which, here, :], weights
            ).astype(jnp.bfloat16)
            return carry

        lax.fori_loop(0, 2, one, 0)

    token_copy.wait_recv()
    project(part)
    first_rows(1 - part, mate_tokens_ref)
    along.take(2)
    dispatch(2)
    project(1 - part)

    def mix_copy(pair):
        here = pl.ds(pair * PAIR, PAIR)
        return send(
            mixed_all.at[pl.ds((1 - part) * rows, rows), here],
            mixed_ref.at[1, :, here],
            mix_send.at[pair],
            mix_recv.at[pair],
            tensor=mate,
        )

    for pair in range(wide // PAIR):
        attend_pair(proj_ref, mixed_all, log_ref, pair, head_dim)
        mix_copy(pair).start()
        if pair == 1:
            along.take(3)
            dispatch(3)
    mixed_ref[0] = mixed_all[pl.ds(part * rows, rows), :]
    share_o.finish()
    for pair in range(wide // PAIR):
        mix_copy(pair).wait_recv()

    def finish_rows(i, carry):
        here = pl.ds(i * 128, 128)
        total = tokens_ref[here, :].astype(jnp.float32)
        total += dot_rows(mixed_ref[0, here, :], wo_ref[:, :, :wide].reshape(-1, wide)) + dot_rows(
            mixed_ref[1, here, :], wo_ref[:, :, wide:].reshape(-1, wide)
        )
        middle_ref[here, :] = total
        unit, _ = norm_stats(total)
        second_ref[here, :] = (unit * gains_ref[2:3, :] + gains_ref[3:4, :]).astype(jnp.bfloat16)
        return carry

    lax.fori_loop(0, rows // 128, finish_rows, 0)
    along.finish()
    token_copy.wait_send()
    share_q.drain()
    share_o.drain()
    for copy in near:
        copy.wait_send()
    for i in range(1, line):
        target_copy(i, place, lax.rem(place + i, line)).wait_send()
    for pair in range(wide // PAIR):
        mix_copy(pair).wait_send()
    for step in range(line):
        plane.wait_recv(step)
        plane.wait_send(step)


def run_front(tokens, cotangent, target, weights, gains, sizes):
    dp_count, line, experts, per, head_dim = sizes
    rows, width = tokens.shape
    qkv_a, qkv_b, out_a, out_b = weights
    share, columns = qkv_a.shape
    wide = columns // 3
    low, dma = jnp.bfloat16, pltpu.SemaphoreType.DMA
    whole, far = pl.BlockSpec(memory_space=pltpu.VMEM), pl.BlockSpec(memory_space=pl.ANY)
    shape = jax.ShapeDtypeStruct
    return pl.pallas_call(
        functools.partial(front_kernel, dp_count, head_dim),
        in_specs=[whole] * 11,
        out_specs=[far] + [whole] * 10,
        out_shape=[
            shape((experts, line, dp_count, per, width), low),
            shape((8, width), jnp.float32),
            shape((line, 8, rows), jnp.int32),
            shape((dp_count, share, columns), low),
            shape((dp_count, share, 2 * wide), low),
            shape((2, rows, width), low),
            shape((2 * rows, columns), low),
            shape((2 * rows, wide), jnp.float32),
            shape((2, rows, wide), low),
            shape((rows, width), jnp.float32),
            shape((rows, width), low),
        ],
        scratch_shapes=[
            pltpu.VMEM((line, rows, width), low),
            pltpu.VMEM((line, dp_count * experts, per, width), low),
            pltpu.VMEM(qkv_b.shape, low),
            pltpu.VMEM((3,) + out_b.shape, low),
            pltpu.VMEM((2 * rows, wide), low),
            pltpu.VMEM((rows, width), low),
            dma((line + 1,)),
            dma((line,)),
            dma((line, dp_count)),
            dma((line, dp_count)),
            dma((line,)),
            dma((line,)),
            dma((line,)),
            dma((5,)),
            dma((5,)),
            dma((wide // PAIR,)),
            dma((wide // PAIR,)),
            dma((4, dp_count // 2)),
            dma((4, dp_count // 2)),
        ],
        compiler_params=pltpu.CompilerParams(
            collective_id=1, has_side_effects=True, vmem_limit_bytes=56 << 20
        ),
        name="front",
    )(tokens, cotangent, target, *weights, *gains)


def attend_back_pair(proj_ref, log_ref, grad_ref, out_ref, dk_sum, dv_sum, pair, head_dim):
    length, wide = proj_ref.shape[0], proj_ref.shape[1] // 3
    here = pl.ds(pair * PAIR, PAIR)
    key_at, value_at = pl.ds(wide + pair * PAIR, PAIR), pl.ds(2 * wide + pair * PAIR, PAIR)
    lane = lax.broadcasted_iota(jnp.int32, (BLOCK, PAIR), 1)
    for first in reversed(range(0, length, BLOCK)):
        rows, seen = pl.ds(first, BLOCK), pl.ds(0, first + BLOCK)
        lanes_seen = lax.broadcasted_iota(jnp.int32, (first + BLOCK, PAIR), 1)
        wide_query = proj_ref[rows, here].astype(jnp.float32) * SCORE_SCALE
        key, value, grad = proj_ref[seen, key_at], proj_ref[seen, value_at], grad_ref[rows, here]
        query, wide_grad = wide_query.astype(jnp.bfloat16), grad.astype(jnp.float32)
        dq = jnp.zeros((BLOCK, PAIR), jnp.float32)
        dk = jnp.zeros((first + BLOCK, PAIR), jnp.float32)
        dv = jnp.zeros((first + BLOCK, PAIR), jnp.float32)
        for head in range(PAIR // head_dim):
            mine = lane // head_dim == head
            there = lanes_seen // head_dim == head
            scores = masked_scores(lanes_of(wide_query, mine), key, first)
            log_total = log_ref[rows, pl.ds(pair * PAIR + head * head_dim, 1)]
            probs = jnp.exp(scores - log_total)
            prob_grad = dot_rows(lanes_of(wide_grad, mine), value)
            inner = jnp.sum(probs * prob_grad, axis=-1, keepdims=True)
            score_grad = (probs * (prob_grad - inner)).astype(jnp.bfloat16)
            dq = jnp.where(mine, dot_plain(score_grad, key), dq)
            dk = jnp.where(there, dot_columns(score_grad, query), dk)
            dv = jnp.where(there, dot_columns(probs.astype(jnp.bfloat16), grad), dv)
        out_ref[rows, here] = (dq * SCORE_SCALE).astype(jnp.bfloat16)
        if first + BLOCK == length:
            dk_sum[...] = dk
            dv_sum[...] = dv
        else:
            dk_sum[seen, :] += dk
            dv_sum[seen, :] += dv
    out_ref[:, key_at] = dk_sum[...].astype(jnp.bfloat16)
    out_ref[:, value_at] = dv_sum[...].astype(jnp.bfloat16)


class Pieces:
    def __init__(self, source, held, sems, dp_count):
        self.source, self.held, self.sems, self.dp_count = source, held, sems, dp_count
        self.me = lax.axis_index("dp")

    def copy(self, i, to):
        return send(
            self.source.at[to],
            self.held.at[self.me],
            self.sems.at[0, i],
            self.sems.at[1, i],
            dp=to,
        )

    def start(self):
        def one(i, carry):
            self.copy(i, lax.rem(self.me + i, self.dp_count)).start()
            return carry

        lax.fori_loop(1, self.dp_count, one, 0)

    def total(self, sum_ref):
        sum_ref[...] = self.source[self.me].astype(jnp.float32)

        def one(i, carry):
            at = lax.rem(self.me + self.dp_count - i, self.dp_count)
            send(
                self.source.at[self.me],
                self.held.at[at],
                self.sems.at[0, i],
                self.sems.at[1, i],
                dp=at,
            ).wait_recv()
            sum_ref[...] += self.held[at].astype(jnp.float32)
            return carry

        lax.fori_loop(1, self.dp_count, one, 0)

    def drain(self):
        def one(i, carry):
            self.copy(i, lax.rem(self.me + i, self.dp_count)).wait_send()
            return carry

        lax.fori_loop(1, self.dp_count, one, 0)


def norm_back_rows(grad, values, gain):
    unit, inv_scale = norm_stats(values)
    scaled = grad * gain
    mean_plain = jnp.mean(scaled, axis=-1, keepdims=True)
    mean_unit = jnp.mean(scaled * unit, axis=-1, keepdims=True)
    change = inv_scale * (scaled - mean_plain - unit * mean_unit)
    return (
        change,
        jnp.sum(grad * unit, axis=0, keepdims=True),
        jnp.sum(grad, axis=0, keepdims=True),
    )


def back_kernel(
    dp_count,
    head_dim,
    back_ref,
    cot_ref,
    tokens_ref,
    middle_ref,
    gains_ref,
    target_ref,
    wq_ref,
    wo_ref,
    first_ref,
    proj_ref,
    log_ref,
    mixed_ref,
    result_ref,
    out_ref,
    grad_tokens_ref,
    sums_ref,
    d_qkv_ref,
    d_out_ref,
    returned,
    stage,
    far,
    middle_grad,
    middle_low,
    mixed_grad,
    mixed_sent,
    qkv_grad,
    dk_sum,
    dv_sum,
    out_pieces,
    out_held,
    out_sum,
    out_sent,
    out_near,
    qkv_pieces,
    qkv_held,
    qkv_sum,
    qkv_sent,
    qkv_near,
    first_sent,
    first_near,
    line_sums,
    plane_sums,
    send_sem,
    recv_sem,
    local_sem,
    far_send,
    far_recv,
    near_send,
    near_recv,
    out_sems,
    qkv_sems,
    line_send,
    line_recv,
    plane_send,
    plane_recv,
):
    rows, width = tokens_ref.shape
    experts, line, _, per, _ = result_ref.shape
    wide = proj_ref.shape[1] // 3
    share = wq_ref.shape[1]
    me, place = lax.axis_index("dp"), lax.axis_index("tensor")
    order = block_order(place)
    mate, across, last = order[1], lax.rem(place + 2, line), line - 1 - place
    part = lax.rem(place, 2)
    greet(dp_count, line)
    plane = Plane(
        lambda step, to: result_ref.at[:, order[step], to],
        lambda step, at: returned.at[step, pl.ds(at * experts, experts)],
        send_sem,
        recv_sem,
        local_sem,
        dp_count,
    )
    plane.start(2)
    results = Return(plane, returned, target_ref, stage, far, far_send, far_recv, per)
    sums_ref[...] = jnp.zeros_like(sums_ref)

    def second_rows(i, carry):
        here = pl.ds(i * 128, 128)
        change, gain_sum, bias_sum = norm_back_rows(
            back_ref[here, :], middle_ref[here, :], gains_ref[2:3, :]
        )
        change = cot_ref[here, :].astype(jnp.float32) + change
        middle_grad[here, :] = change
        middle_low[here, :] = change.astype(jnp.bfloat16)
        sums_ref[2:3, :] += gain_sum
        sums_ref[3:4, :] += bias_sum
        return carry

    lax.fori_loop(0, rows // 128, second_rows, 0)
    mixed_sent[...] = dot_plain(
        middle_low[...], wo_ref[:, :, wide:].reshape(width, wide)
    ).astype(jnp.bfloat16)
    mixed_copy = send(
        mixed_sent,
        mixed_grad.at[pl.ds(part * rows, rows)],
        near_send.at[0],
        near_recv.at[0],
        tensor=mate,
    )
    mixed_copy.start()
    mixed_grad[pl.ds(part * rows, rows), :] = dot_plain(
        middle_low[...], wo_ref[:, :, :wide].reshape(width, wide)
    ).astype(jnp.bfloat16)
    for group in range(2):
        product_ = dot_columns(middle_low[...], mixed_ref[group]).astype(jnp.bfloat16)
        out_pieces[:, :, group * wide : (group + 1) * wide] = product_.reshape(
            dp_count, share, wide
        )
    outs = Pieces(out_pieces, out_held, out_sems, dp_count)
    outs.start()
    plane.start(3)
    send(
        mixed_sent,
        mixed_grad.at[pl.ds((1 - part) * rows, rows)],
        near_send.at[0],
        near_recv.at[0],
        tensor=mate,
    ).wait_recv()
    for pair in range(wide // PAIR):
        attend_back_pair(
            proj_ref, log_ref, mixed_grad, qkv_grad, dk_sum, dv_sum, pair, head_dim
        )
        if pair == 0:
            results.begin(2)
        if pair == 1:
            results.end(2)
            plane.start(1)
    first_sent[...] = dot_rows(
        qkv_grad[pl.ds((1 - part) * rows, rows), :], wq_ref[...].reshape(width, 3 * wide)
    ).astype(jnp.bfloat16)
    first_copy = send(first_sent, first_near, near_send.at[1], near_recv.at[1], tensor=mate)
    first_copy.start()
    middle_rows = width // 2
    for half in range(2):
        total = dot_columns(
            first_ref[0, :, half * middle_rows : (half + 1) * middle_rows], qkv_grad[:rows, :]
        )
        total += dot_columns(
            first_ref[1, :, half * middle_rows : (half + 1) * middle_rows], qkv_grad[rows:, :]
        )
        qkv_pieces[pl.ds(half * dp_count // 2, dp_count // 2)] = total.astype(
            jnp.bfloat16
        ).reshape(dp_count // 2, share, 3 * wide)
    qkvs = Pieces(qkv_pieces, qkv_held, qkv_sems, dp_count)
    qkvs.start()
    results.begin(3, 0)
    outs.total(out_sum)
    for i, base in enumerate((wide, PAIR, wide + PAIR)):
        out_sent[i] = out_sum[:, base : base + 2 * PAIR].astype(jnp.bfloat16)
    out_copies = [
        send(out_sent.at[i], out_near.at[i], near_send.at[3 + i], near_recv.at[3 + i], tensor=to)
        for i, to in enumerate((mate, across, last))
    ]
    for copy in out_copies:
        copy.start()

    def first_rows(i, carry):
        here = pl.ds(i * 128, 128)
        grad = dot_rows(
            qkv_grad[pl.ds(part * rows + i * 128, 128), :], wq_ref[...].reshape(width, 3 * wide)
        )
        grad += first_near[here, :].astype(jnp.float32)
        change, gain_sum, bias_sum = norm_back_rows(
            grad, tokens_ref[here, :].astype(jnp.float32), gains_ref[0:1, :]
        )
        grad_tokens_ref[here, :] = (middle_grad[here, :] + change).astype(jnp.bfloat16)
        sums_ref[0:1, :] += gain_sum
        sums_ref[1:2, :] += bias_sum
        return carry

    first_copy.wait_recv()
    lax.fori_loop(0, rows // 128, first_rows, 0)
    line_sums[place] = sums_ref[...]

    def line_copy(i, at, to):
        return send(line_sums.at[at], line_sums.at[at], line_send.at[i], line_recv.at[i], tensor=to)

    for i in range(1, line):
        line_copy(i, place, lax.rem(place + i, line)).start()
    results.end(3)
    results.begin(1)
    for i in range(1, line):
        at = lax.rem(place + line - i, line)
        line_copy(i, at, at).wait_recv()
    plane_sums[me] = (line_sums[0] + line_sums[1]) + (line_sums[2] + line_sums[3])

    def plane_copy(i, at, to):
        return send(
            plane_sums.at[at], plane_sums.at[at], plane_send.at[i], plane_recv.at[i], dp=to
        )

    def plane_start(i, carry):
        plane_copy(i, me, lax.rem(me + i, dp_count)).start()
        return carry

    lax.fori_loop(1, dp_count, plane_start, 0)
    qkvs.total(qkv_sum)
    for kind in range(3):
        base = kind * wide + PAIR
        qkv_sent[kind] = qkv_sum[:, base : base + 2 * PAIR].astype(jnp.bfloat16)
    qkv_copy = send(qkv_sent, qkv_near, near_send.at[2], near_recv.at[2], tensor=across)
    qkv_copy.start()
    plane.wait_recv(0)
    middle_grad[...] = middle_ref[...] + results.collect(0)

    def plane_wait(i, carry):
        at = lax.rem(me + dp_count - i, dp_count)
        plane_copy(i, at, at).wait_recv()
        return carry

    lax.fori_loop(1, dp_count, plane_wait, 0)
    sums_ref[...] = plane_sums[0]

    def plane_add(i, carry):
        sums_ref[...] += plane_sums[i]
        return carry

    lax.fori_loop(1, dp_count, plane_add, 0)
    for copy in out_copies:
        copy.wait_recv()
    arrived = [out_near[i].astype(jnp.float32) for i in range(3)]
    d_out_ref[:, :PAIR] = (
        out_sum[:, :PAIR] + arrived[0][:, :PAIR] + arrived[1][:, PAIR:] + arrived[2][:, PAIR:]
    )
    turned = pltpu.roll(arrived[1][:, :PAIR] + arrived[2][:, :PAIR], head_dim, 1)
    d_out_ref[:, PAIR:] = out_sum[:, PAIR : 2 * PAIR] + arrived[0][:, PAIR:] + turned
    qkv_copy.wait_recv()
    for kind in range(3):
        base, at = kind * wide, kind * 2 * PAIR
        come = qkv_near[kind].astype(jnp.float32)
        d_qkv_ref[:, at : at + PAIR] = qkv_sum[:, base : base + PAIR] + come[:, PAIR:]
        d_qkv_ref[:, at + PAIR : at + 2 * PAIR] = qkv_sum[
            :, base + PAIR : base + 2 * PAIR
        ] + pltpu.roll(come[:, :PAIR], head_dim, 1)
    results.wait()
    out_ref[...] = (
        middle_grad[...] + far[0].astype(jnp.float32) + far[1].astype(jnp.float32)
    ).astype(jnp.bfloat16)
    results.drain()
    outs.drain()
    qkvs.drain()
    mixed_copy.wait_send()
    first_copy.wait_send()
    qkv_copy.wait_send()
    for copy in out_copies:
        copy.wait_send()
    for i in range(1, line):
        line_copy(i, place, lax.rem(place + i, line)).wait_send()

    def plane_drain(i, carry):
        plane_copy(i, me, lax.rem(me + i, dp_count)).wait_send()
        return carry

    lax.fori_loop(1, dp_count, plane_drain, 0)


def run_back(dp_count, head_dim, *args):
    tokens, wq, proj, result = args[2], args[6], args[9], args[12]
    rows, width = tokens.shape
    experts, line, _, per, _ = result.shape
    share = wq.shape[1]
    wide = proj.shape[1] // 3
    low, wider, dma = jnp.bfloat16, jnp.float32, pltpu.SemaphoreType.DMA
    whole, far = pl.BlockSpec(memory_space=pltpu.VMEM), pl.BlockSpec(memory_space=pl.ANY)
    shape, vmem = jax.ShapeDtypeStruct, pltpu.VMEM
    return pl.pallas_call(
        functools.partial(back_kernel, dp_count, head_dim),
        in_specs=[whole] * 12 + [far],
        out_specs=[whole] * 5,
        out_shape=[
            shape((rows, width), low),
            shape((rows, width), low),
            shape((8, width), wider),
            shape((share, 6 * PAIR), wider),
            shape((share, 2 * PAIR), wider),
        ],
        scratch_shapes=[
            vmem((line, dp_count * experts, per, width), low),
            vmem((line, rows, width), low),
            vmem((line, rows, width), low),
            vmem((rows, width), wider),
            vmem((rows, width), low),
            vmem((2 * rows, wide), low),
            vmem((rows, wide), low),
            vmem((2 * rows, 3 * wide), low),
            vmem((2 * rows, PAIR), wider),
            vmem((2 * rows, PAIR), wider),
            vmem((dp_count, share, 2 * wide), low),
            vmem((dp_count, share, 2 * wide), low),
            vmem((share, 2 * wide), wider),
            vmem((3, share, 2 * PAIR), low),
            vmem((3, share, 2 * PAIR), low),
            vmem((dp_count, share, 3 * wide), low),
            vmem((dp_count, share, 3 * wide), low),
            vmem((share, 3 * wide), wider),
            vmem((3, share, 2 * PAIR), low),
            vmem((3, share, 2 * PAIR), low),
            vmem((rows, width), low),
            vmem((rows, width), low),
            vmem((line, 8, width), wider),
            vmem((dp_count, 8, width), wider),
            dma((line, dp_count)),
            dma((line, dp_count)),
            dma((line,)),
            dma((line + 1,)),
            dma((line + 1,)),
            dma((6,)),
            dma((6,)),
            dma((2, dp_count)),
            dma((2, dp_count)),
            dma((line,)),
            dma((line,)),
            dma((dp_count,)),
            dma((dp_count,)),
        ],
        compiler_params=pltpu.CompilerParams(
            collective_id=2, has_side_effects=True, vmem_limit_bytes=58 << 20
        ),
        name="back",
    )(*args)


def on_device(
    tokens,
    token_ids,
    hash_table,
    ln1_gain,
    ln1_bias,
    w_qkv,
    w_out,
    ln2_gain,
    ln2_bias,
    expert_in,
    expert_out,
    cotangent,
):
    low = jnp.bfloat16
    row_count, model_width = tokens.shape
    local_experts = expert_in.shape[0]
    dp_count = lax.axis_size("dp")
    line = lax.axis_size("tensor")
    head_dim = w_qkv.shape[2] // 3
    heads_shard = w_qkv.shape[1]

    experts_total = dp_count * local_experts
    capacity = 2 * row_count // experts_total
    slot_count = experts_total * capacity
    expert_of = jnp.take(hash_table, token_ids)
    one_hot = (expert_of[:, None] == jnp.arange(experts_total, dtype=jnp.int32)[None, :]).astype(
        jnp.int32
    )
    before = (
        lax.broadcasted_iota(jnp.int32, (row_count, row_count), 0)
        > lax.broadcasted_iota(jnp.int32, (row_count, row_count), 1)
    ).astype(low)
    earlier = jnp.dot(before, one_hot.astype(low), preferred_element_type=jnp.float32)
    slot_rank = jnp.sum(earlier.astype(jnp.int32) * one_hot, axis=1)
    target = jnp.where(slot_rank < capacity, expert_of * capacity + slot_rank, slot_count)

    share = w_qkv.shape[0]
    wide = 2 * heads_shard * head_dim
    by_kind = w_qkv.astype(low).reshape(share, heads_shard, 3, head_dim).transpose(0, 2, 1, 3)
    qkv_a = jnp.pad(by_kind.reshape(share, 3, -1), ((0, 0), (0, 0), (0, wide // 2)))
    qkv_b = jnp.concatenate([by_kind[:, :, -1:], by_kind[:, :, :-1]], axis=2).reshape(share, 3, -1)
    qkv_b = jnp.pad(qkv_b, ((0, 0), (0, 0), (head_dim, 0))).transpose(1, 0, 2)
    out_rows = w_out.astype(low).T
    out_a = jnp.pad(out_rows, ((0, 0), (0, head_dim)))
    out_b = jnp.concatenate([out_rows[:, -head_dim:], out_rows[:, :-head_dim]], axis=1)
    out_b = jnp.pad(out_b, ((0, 0), (head_dim, 0)))
    sizes = (dp_count, line, local_experts, capacity, head_dim)
    (
        grad_rows,
        gains,
        targets,
        qkv_weight,
        out_weight,
        first_all,
        projected,
        log_total,
        mixed_pair,
        middle,
        second_low,
    ) = run_front(
        tokens,
        cotangent,
        target,
        (qkv_a.reshape(share, -1), qkv_b, out_a, out_b),
        (ln1_gain, ln1_bias, ln2_gain, ln2_bias),
        sizes,
    )
    second_grad, result, grad_expert_in, grad_expert_out = run_experts(
        second_low,
        targets,
        grad_rows,
        expert_in,
        expert_out,
        dp_count,
        line,
    )
    out, grad_tokens, sums, grad_qkv, grad_out = run_back(
        dp_count,
        head_dim,
        second_grad,
        cotangent,
        tokens,
        middle,
        gains,
        targets,
        qkv_weight,
        out_weight,
        first_all,
        projected,
        log_total,
        mixed_pair,
        result,
    )
    half = wide // 2
    grad_qkv = grad_qkv.reshape(share, 3, -1)[:, :, :half]
    grad_qkv = grad_qkv.reshape(share, 3, heads_shard, head_dim).transpose(0, 2, 1, 3)
    return (
        out,
        grad_tokens,
        sums[0],
        sums[1],
        grad_qkv.reshape(w_qkv.shape),
        grad_out[:, :half].T,
        sums[2],
        sums[3],
        grad_expert_in,
        grad_expert_out,
    )


def solution(mesh):
    rows = P(("dp", "tensor"), None)
    weights = (P("dp", "tensor", None), P("tensor", "dp"))
    experts = (P("dp", None, "tensor"), P("dp", "tensor", None))
    return jax.shard_map(
        on_device,
        mesh=mesh,
        in_specs=(rows, P(("dp", "tensor")), P(), P(), P(), *weights, P(), P(), *experts, rows),
        out_specs=(rows, rows, P(), P(), *weights, P(), P(), *experts),
        check_vma=False,
    )
```
